32 devices in a mesh: shard: 8 (over z, x), ctx: 2 (over core), tp: 2 (over y).
Axes of the slice: x: 2, y: 2, z: 4, core: 2. Of those that a mesh axis runs over, the one named last changes fastest.
Arguments:
- tokens: bfloat16 [16, 1024, 1088], P(('shard', 'tp'), 'ctx'), may hold values from -6 to 6
- segment_ids: int32 [16, 1024], P(('shard', 'tp')), may hold values from 0 to 3, never falling along the last dimension, each value on 1 to 512 neighbouring positions
- norm_gains: bfloat16 [2, 1088], P(None, 'shard'), may hold values from 0.25 to 1.75
- norm_shifts: bfloat16 [2, 1088], P(None, 'shard'), may hold values from -3 to 3
- biases: bfloat16 [4, 1088], P(None, 'shard'), may hold values from -3 to 3
- w_qkv: bfloat16 [1088, 3264], P('shard'), may hold values from -4 to 4
- w_o: bfloat16 [1088, 1088], P('shard'), may hold values from -0.75 to 0.75
- w_in: bfloat16 [1088, 4352], P('shard', 'tp'), may hold values from -0.1875 to 0.1875
- b_in: bfloat16 [4352], P('tp'), may hold values from -3 to 3
- w_out: bfloat16 [4352, 1088], P('tp', 'shard'), may hold values from -0.09375 to 0.09375
- cotangent: bfloat16 [16, 1024, 1088], P(('shard', 'tp'), 'ctx'), may hold values from -6 to 6
Outputs:
- mixed: bfloat16 [16, 1024, 1088], P(('shard', 'tp'), 'ctx')
- tokens_grad: float32 [16, 1024, 1088], P(('shard', 'tp'), 'ctx')
- norm_gains_grad: float32 [2, 1088], P(None, ('shard', 'ctx'))
- norm_shifts_grad: float32 [2, 1088], P(None, ('shard', 'ctx'))
- biases_grad: float32 [4, 1088], P(None, ('shard', 'ctx'))
- w_qkv_grad: float32 [1088, 3264], P(('shard', 'ctx'))
- w_o_grad: float32 [1088, 1088], P(('shard', 'ctx'))
- w_in_grad: float32 [1088, 4352], P(('shard', 'ctx'), 'tp')
- b_in_grad: float32 [2, 2176], P('tp', ('shard', 'ctx'))
- w_out_grad: float32 [4352, 1088], P('tp', ('shard', 'ctx'))
The draws below stay inside these ranges and needn't reach their ends.
Inputs may be any that keep to these rules, and one draw needn't show every extreme that they name: `segment_ids`: in each sequence the ids never fall; each document holds 1 to 512 positions, and one holds exactly 512.
All inputs are finite; a program needn't handle non-finite values.
Results may differ from the reference program's by a relative error of at most 0.009.
The reference program's roundings to bfloat16 on the way count: a program that leaves them out, or rounds other values in their place, can miss the bound.
Values may be sent and summed in bfloat16 or wider, within the bound.
A program may use at most 192 MiB of HBM per device.

```python
import math
import jax
import jax.numpy as jnp
import numpy as np
from jax import lax

D = 1088
HEADS = 17
HEAD_DIM = 64
FF = 4352
LEN = 1024
SEQS = 16
N_TP = 2


def draw_w_qkv(key, part):
    base_draw = jnp.clip(jax.random.normal(key, (D, 3 * D), jnp.float32), -4.0, 4.0) * D ** (-0.5)
    return base_draw.astype(jnp.bfloat16)


def steps_of(own_key, extent, pieces, low, top_value):
    def one(dim, blocks):
        heights = jax.random.uniform(jax.random.fold_in(jax.random.fold_in(own_key, 6), dim), (blocks,), jnp.float32, low / len(pieces), top_value / len(pieces))
        return jnp.repeat(jnp.exp(heights), extent[dim] // blocks).reshape((-1,) + (1,) * (len(extent) - dim - 1))

    gain = one(*pieces[0])
    for cut in pieces[1:]:
        gain = gain * one(*cut)
    return gain


def length_profile(amount, total, most, skew):
    weights = [(1 << 20) // math.isqrt(standing ** skew) + 1 for standing in range(2, amount + 1)]
    rest, holding = total - most - (amount - 1), [1] * (amount - 1)
    while rest > 0:
        free = [i for i in range(amount - 1) if holding[i] < most]
        pool, budget = sum([weights[i] for i in free]), rest
        for i in free:
            more = min(most - holding[i], max(1, budget * weights[i] // pool), rest)
            holding[i] = holding[i] + more
            rest = rest - more
    return np.array([most] + holding)


def ragged(stream_key, amount, total, limit, slope):
    if amount == 2:
        one = jax.random.randint(stream_key, (), max(1, total - limit), min(limit, total - 1) + 1)
        return jnp.stack([one, total - one])
    tallies = jnp.asarray(length_profile(amount, total, limit, slope), jnp.int32)
    twos = (amount - 1) // 2
    donor, receiver = tallies[1:1 + 2 * twos:2], tallies[2:2 + 2 * twos:2]
    slack = jnp.minimum(donor - 1, limit - receiver)
    shifted = jax.random.randint(jax.random.fold_in(stream_key, 1), (twos,), 0, 1 << 20) % (slack + 1)
    tallies = tallies.at[1:1 + 2 * twos:2].set(donor - shifted).at[2:2 + 2 * twos:2].set(receiver + shifted)
    return tallies[jax.random.permutation(jax.random.fold_in(stream_key, 2), amount)]


def scatter_about(own_key, extent, deviation, limit, split=(), held_as=jnp.bfloat16):
    loudness = steps_of(own_key, extent, split, -0.22, 0.18) if split else 1.0
    values = jax.random.normal(own_key, extent, jnp.float32) * deviation * loudness
    return jnp.minimum(jnp.maximum(values, -limit), limit).astype(held_as)


def setup_inputs(seed: int = 0) -> dict:
    streams_of = jax.random.split(jax.random.key(seed), 12)
    return {
        "tokens": scatter_about(streams_of[0], (SEQS, LEN, D), 1.0, 6.0, ((0, 16), (1, 2))),
        "segment_ids": jax.vmap(lambda own: jnp.searchsorted(jnp.cumsum(ragged(own, 4, LEN, LEN // 2, 2)), jnp.arange(LEN), side="right"))(jax.random.split(streams_of[1], SEQS)).reshape((SEQS, LEN)).astype(jnp.int32),
        "norm_gains": jnp.clip(1.0 + 0.15 * jax.random.normal(streams_of[2], (2, D), jnp.float32), 0.25, 1.75).astype(jnp.bfloat16),
        "norm_shifts": scatter_about(streams_of[3], (2, D), 0.5, 3.0, ((1, 8),)),
        "biases": scatter_about(streams_of[4], (4, D), 0.4, 3.0, ((1, 8),)),
        "w_qkv": draw_w_qkv(jax.random.fold_in(streams_of[11], 71), 0),
        "w_o": scatter_about(streams_of[6], (D, D), (D // 16) ** -0.5, 0.75, ((0, 8),)),
        "w_in": scatter_about(streams_of[7], (D, FF), D ** -0.5, 0.1875, ((0, 8), (1, 2))),
        "b_in": scatter_about(streams_of[8], (FF,), 0.5, 3.0, ((0, 2),)),
        "w_out": scatter_about(streams_of[9], (FF, D), FF ** -0.5, 0.09375, ((0, 2), (1, 8))),
        "cotangent": scatter_about(streams_of[10], (SEQS, LEN, D), 1.0, 6.0, ((0, 16), (1, 2))),
    }


@jax.custom_vjp
def low(v):
    return lax.optimization_barrier(v.astype(jnp.bfloat16)).astype(jnp.float32)

@jax.custom_vjp
def low_back(v):
    return v

def low_keep(v):
    return (low(v), None)

def low_pass(kept, grad):
    return (grad,)

def back_keep(v):
    return (v, None)

def back_low(kept, grad):
    return (low(grad),)
low.defvjp(low_keep, low_pass)
low_back.defvjp(back_keep, back_low)

def matmul(left_side, right_side):
    return jnp.dot(left_side, right_side, precision=lax.Precision.HIGHEST, preferred_element_type=jnp.float32)

def layer_norm(values, gain_row, shift_row):
    center = lax.optimization_barrier(jnp.mean(values, axis=-1, keepdims=True))
    spread = values - center
    variance = lax.optimization_barrier(jnp.mean(spread * spread, axis=-1, keepdims=True))
    return spread * lax.rsqrt(variance + 1e-05) * gain_row + shift_row

def gelu_tanh(values):
    return 0.5 * values * (1.0 + jnp.tanh(math.sqrt(2.0 / math.pi) * (values + 0.044715 * values * values * values)))

def forward(hidden, segments, gains, shifts, bias_rows, qkv_weight, proj_weight, up_weight, up_bias, down_weight):
    length = hidden.shape[0]
    score_scale = HEAD_DIM ** (-0.5)
    normed = low(layer_norm(hidden, gains[0], shifts[0]))
    projected = matmul(normed, qkv_weight)
    queries = low_back(low(projected[:, :D] + bias_rows[0]))
    keys_all = low_back(low(projected[:, D:2 * D]))
    values_all = low_back(low(projected[:, 2 * D:] + bias_rows[1]))
    position = jnp.arange(length)
    allowed = (position[None, :] <= position[:, None]) & (segments[None, :] == segments[:, None])
    query_heads = queries.reshape(length, HEADS, HEAD_DIM)
    key_heads = keys_all.reshape(length, HEADS, HEAD_DIM)
    value_heads = values_all.reshape(length, HEADS, HEAD_DIM)
    scores = low_back(jnp.einsum('qhd,khd->hqk', query_heads, key_heads, precision=lax.Precision.HIGHEST) * score_scale)
    masked = jnp.where(allowed[None, :, :], scores, -1e+30)
    highest = lax.optimization_barrier(jnp.max(masked, axis=-1, keepdims=True))
    weights = jnp.exp(masked - highest)
    probabilities = low(weights / lax.optimization_barrier(jnp.sum(weights, axis=-1, keepdims=True)))
    attended = jnp.einsum('hqk,khd->qhd', probabilities, value_heads, precision=lax.Precision.HIGHEST).reshape(length, D)
    attended = low_back(low(attended))
    branch = low_back(matmul(attended, proj_weight) + bias_rows[2])
    middle = hidden + branch
    normed_two = low(layer_norm(middle, gains[1], shifts[1]))
    inner_values = low_back(matmul(normed_two, up_weight) + up_bias)
    active = low(gelu_tanh(inner_values))
    mixed_rows = low_back(matmul(active, down_weight) + bias_rows[3])
    return middle + mixed_rows

def reference(tokens, segment_ids, norm_gains, norm_shifts, biases, w_qkv, w_o, w_in, b_in, w_out, cotangent):
    params = (norm_gains.astype(jnp.float32), norm_shifts.astype(jnp.float32), biases.astype(jnp.float32), w_qkv.astype(jnp.float32), w_o.astype(jnp.float32), w_in.astype(jnp.float32), b_in.astype(jnp.float32), w_out.astype(jnp.float32))
    initial = tuple((jnp.zeros_like(tensor) for tensor in params))

    def one_sequence(totals, slices):
        hidden, segments, grad_rows = slices

        def apply(hidden_in, gains, shifts, bias_rows, qkv_weight, proj_weight, up_weight, up_bias, down_weight):
            return forward(hidden_in, segments, gains, shifts, bias_rows, qkv_weight, proj_weight, up_weight, up_bias, down_weight)
        result, pull_back = jax.vjp(apply, hidden.astype(jnp.float32), params[0], params[1], params[2], params[3], params[4], params[5], params[6], params[7])
        updates = pull_back(grad_rows.astype(jnp.float32))
        totals = tuple((running + update for running, update in zip(totals, updates[1:])))
        return (totals, (result.astype(jnp.bfloat16), updates[0]))
    totals, outputs = lax.scan(one_sequence, initial, (tokens, segment_ids, cotangent))
    mixed_all, tokens_grad = outputs
    return (mixed_all, tokens_grad, totals[0], totals[1], totals[2], totals[3], totals[4], totals[5], totals[6].reshape(N_TP, FF // N_TP), totals[7])
```

```python
import math

import jax
import jax.numpy as jnp
from jax import lax
from jax.experimental import pallas as pl
from jax.experimental.pallas import tpu as pltpu
from jax.sharding import PartitionSpec as P

D = 1088
HEADS = 17
HEAD_DIM = 64


def layer_norm(values, gain_row, shift_row):
    center = jnp.mean(values, axis=-1, keepdims=True)
    spread = values - center
    variance = jnp.mean(spread * spread, axis=-1, keepdims=True)
    return spread * lax.rsqrt(variance + 1e-05) * gain_row + shift_row


def gelu_tanh(values):
    return (
        0.5
        * values
        * (
            1.0
            + jnp.tanh(math.sqrt(2.0 / math.pi) * (values + 0.044715 * values * values * values))
        )
    )


def contract_rows(left_side, right_side):
    return lax.dot_general(
        left_side, right_side, (((0,), (0,)), ((), ())), preferred_element_type=jnp.float32
    )


def contract_cols(left_side, right_side):
    return lax.dot_general(
        left_side, right_side, (((1,), (1,)), ((), ())), preferred_element_type=jnp.float32
    )


def split_heads(matrix):
    return matrix.reshape(matrix.shape[0], HEADS, HEAD_DIM).transpose(1, 0, 2)


def merge_heads(stacked):
    return stacked.transpose(1, 0, 2).reshape(stacked.shape[1], D)


BF = jnp.bfloat16
F32 = jnp.float32
MESH = pl.DeviceIdType.MESH
EPS = 1e-05
BR = 144
UNIT = 128


def mm(left, right):
    return jnp.dot(left, right, preferred_element_type=F32)


def remote(src, dst, send, recv, device):
    return pltpu.make_async_remote_copy(
        src_ref=src, dst_ref=dst, send_sem=send, recv_sem=recv,
        device_id=device, device_id_type=MESH,
    )


class Place:
    def __init__(self):
        self.s = lax.axis_index("shard")
        self.c = lax.axis_index("ctx")
        self.t = lax.axis_index("tp")
        self.z = self.s // 2
        self.x = self.s - 2 * self.z
        self.xb = 1 - self.x
        self.tb = 1 - self.t
        z = self.z
        self.peers = [
            z + 1 - 2 * lax.rem(z, 2),
            jnp.where(z < 2, 2, 1),
            jnp.where(z < 2, 3, 0),
        ]
        self.core = (self.s, 1 - self.c, self.t)
        self.xdev = (2 * z + self.xb, self.c, self.t)
        self.ydev = (self.s, self.c, self.tb)

    def zdev(self, zp):
        return (2 * zp + self.x, self.c, self.t)

    def greet(self):
        barrier = pltpu.get_barrier_semaphore()
        devices = [self.core, self.xdev, self.ydev] + [self.zdev(p) for p in self.peers]
        for device in devices:
            pl.semaphore_signal(barrier, inc=1, device_id=device, device_id_type=MESH)
        pl.semaphore_wait(barrier, len(devices))


def rows_of(s):
    return pl.ds(pl.multiple_of(s * BR, 16), BR)


class Gather:
    def __init__(self, here, number, own, loc, route, send, recv):
        self.h, self.p, self.own, self.loc, self.route = here, number, own, loc, route
        self.send, self.recv = send, recv

    def push(self, src, s, t, device, i):
        remote(src, self.loc(s, t), self.send.at[self.p, i],
               self.recv.at[self.p, s * 2 + t], device).start()

    def take(self, s, t):
        ref = self.loc(s, t)
        remote(ref, ref, self.send.at[self.p, 0], self.recv.at[self.p, s * 2 + t],
               self.h.core).wait_recv()

    def stage0(self):
        h = self.h
        two, three = self.devs()
        for i, zp in enumerate(h.peers):
            self.push(self.own, h.s, h.t, h.zdev(zp), i)
        self.push(self.own, h.s, h.t, two, 3)
        if self.route in ("zxy", "zyx"):
            self.push(self.own, h.s, h.t, three, 7)

    def devs(self):
        h = self.h
        return (h.ydev, h.xdev) if self.route == "zyx" else (h.xdev, h.ydev)

    def stage1(self):
        h = self.h
        two, three = self.devs()
        for k, zp in enumerate(h.peers):
            s = 2 * zp + h.x
            self.take(s, h.t)
            self.push(self.loc(s, h.t), s, h.t, two, 4 + k)
            if self.route != "zx":
                self.push(self.loc(s, h.t), s, h.t, three, 8 + k)

    def stage2(self):
        h = self.h
        two, three = self.devs()
        for k, zp in enumerate([h.z] + h.peers):
            if self.route == "zyx":
                s, t = 2 * zp + h.x, h.tb
            else:
                s, t = 2 * zp + h.xb, h.t
            self.take(s, t)
            if self.route != "zx":
                self.push(self.loc(s, t), s, t, three, 11 + k)

    def stage3(self):
        h = self.h
        if self.route == "zx":
            return
        for k, zp in enumerate([h.z] + h.peers):
            if self.route == "zyx":
                self.take(2 * zp + h.xb, h.t)
                self.take(2 * zp + h.xb, h.tb)
            else:
                if not (self.route == "kv" and k == 0):
                    self.take(2 * zp + h.x, h.tb)
                self.take(2 * zp + h.xb, h.tb)

    def drain(self):
        sends = {"zx": range(7), "kv": [0, 1, 2, 3, 4, 5, 6, 8, 9, 10, 11, 12, 13, 14],
                 "zxy": range(15), "zyx": range(15)}[self.route]
        for i in sends:
            remote(self.own, self.own, self.send.at[self.p, i], self.recv.at[self.p, 0],
                   self.h.core).wait_send()


def normalise(x, mask, gain, shift, count):
    mean = jnp.sum(x, axis=1, keepdims=True) * (1.0 / count)
    spread = (x - mean) * mask
    var = jnp.sum(spread * spread, axis=1, keepdims=True) * (1.0 / count)
    return spread * lax.rsqrt(var + EPS) * gain + shift


def forward_kernel(
    x_ref, cot_ref, pa, po, pi, pu, small, bin_ref, segr, segc, lanes,
    wa_o, wo_o, wi_o, wu_o, n1t_o, n2t_o, cott_o, cot_o, qn_o, kn_o, vn_o, qt_o, kt_o, ot_o,
    lse_o, mid_o, inner_o, par_o, mb_o,
    wa, wog, wo, wi, wu, n1, cot, n2, sm, par, bins, qn, kn, vn, qt, kt, vt, mb, ot, att, mid,
    inner, stage, lse, wof,
    send, recv, dsend, drecv, ssend, srecv, lsem, osem, isem,
):
    h = Place()
    c, s, t = h.c, h.s, h.t
    rows = x_ref.shape[0]
    length = 2 * rows
    count = 1088
    own = pl.ds(pl.multiple_of(c * rows, rows), rows)
    sib = pl.ds(pl.multiple_of((1 - c) * rows, rows), rows)

    def piece(number, src, buf, route, src_col, col, width):
        if route == "kv":
            own_ref = src.at[:, pl.ds(pl.multiple_of(src_col(t), UNIT), width)]
        else:
            own_ref = src.at[:, pl.ds(src_col, width)]

        def loc(sp, tp):
            where = col(tp)
            if not isinstance(where, int):
                where = pl.multiple_of(where, UNIT)
            return buf.at[rows_of(sp), pl.ds(where, width)]

        return Gather(h, number, own_ref, loc, route, send, recv)

    q_main = piece(0, pa, wa, "zx", 0, lambda tp: 0, 512)
    kv_main = piece(1, pa, wa, "kv", lambda tp: 512 + 512 * tp, lambda tp: 512 + 512 * tp, 512)
    o_main = piece(2, po, wog.at[c], "zx", 0, lambda tp: 0, 512)
    i_one = piece(3, pi, wi, "zxy", 0, lambda tp: 1024 * tp, 640)
    i_two = piece(4, pi, wi, "zyx", 640, lambda tp: 1024 * tp + 640, 384)
    u_one = piece(5, pu, wu, "zxy", 0, lambda tp: 1024 * tp, 640)
    u_two = piece(6, pu, wu, "zyx", 640, lambda tp: 1024 * tp + 640, 384)
    q_more = piece(7, pa, wa, "zx", 1536, lambda tp: 1536, 128)
    kv_more = piece(8, pa, wa, "kv", lambda tp: 1664 + 128 * tp, lambda tp: 1664 + 128 * tp, 128)
    o_more = piece(9, po, wog.at[c], "zx", 512, lambda tp: 512, 128)
    i_more = piece(10, pi, wi, "zyx", 1024, lambda tp: 2048 + 128 * tp, 128)
    u_more = piece(11, pu, wu, "zyx", 1024, lambda tp: 2048 + 128 * tp, 128)

    def each(stage, mains, mores):
        for p in mains:
            getattr(p, stage)()

        @pl.when(c == 0)
        def _():
            for p in mores:
                getattr(p, stage)()

    A, AX = [q_main, kv_main], [q_more, kv_more]
    O, OX = [o_main], [o_more]
    I, IX = [i_one, i_two], [i_more]
    U, UX = [u_one, u_two], [u_more]

    def small_copy(sp, device, i):
        return remote(sm.at[sp], sm.at[sp], ssend.at[i], srecv.at[sp], device)

    @pl.when(c == 1)
    def _():
        wi[:, 2048:2304] = jnp.zeros((1152, 256), BF)
        wu[:, 2048:2304] = jnp.zeros((1152, 256), BF)
        wa[:, 1536:1920] = jnp.zeros((1152, 384), BF)

    local = []

    def fill(src, dst):
        copy = pltpu.make_async_copy(src, dst, lsem.at[len(local)])
        copy.start()
        local.append(copy)

    fill(small, sm.at[s])
    fill(bin_ref, bins.at[t])
    fill(cot_ref, cot.at[own])
    fill(pa, wa.at[rows_of(s)])
    fill(po, wog.at[c, rows_of(s)])
    fill(pi.at[:, 0:1024], wi.at[rows_of(s), pl.ds(pl.multiple_of(t * 1024, UNIT), 1024)])
    fill(pu.at[:, 0:1024], wu.at[rows_of(s), pl.ds(pl.multiple_of(t * 1024, UNIT), 1024)])
    fill(pi.at[:, 1024:1152], wi.at[rows_of(s), pl.ds(pl.multiple_of(2048 + t * 128, UNIT), 128)])
    fill(pu.at[:, 1024:1152], wu.at[rows_of(s), pl.ds(pl.multiple_of(2048 + t * 128, UNIT), 128)])

    h.greet()
    local[0].wait()
    local[1].wait()
    for i, zp in enumerate(h.peers):
        small_copy(s, h.zdev(zp), i).start()
    small_copy(s, h.xdev, 3).start()
    bin_copy = remote(bins.at[t], bins.at[t], ssend.at[7], srecv.at[8], h.ydev)
    bin_copy.start()
    each("stage0", A, AX)
    each("stage0", O, OX)
    each("stage0", I, IX)
    each("stage0", U, UX)
    local[2].wait()
    cot_copy = remote(cot.at[own], cot.at[own], dsend.at[0], drecv.at[0], h.core)
    cot_copy.start()
    for k, zp in enumerate(h.peers):
        sp = 2 * zp + h.x
        small_copy(sp, h.xdev, 4 + k).wait_recv()
        small_copy(sp, h.xdev, 4 + k).start()
    for zp in [h.z] + h.peers:
        small_copy(2 * zp + h.xb, h.xdev, 0).wait_recv()

    padded = jnp.zeros((8, 1152), F32)
    natural = jnp.zeros((8, 1152), F32)
    for sp in range(8):
        wide = jnp.concatenate([sm[sp], jnp.zeros((8, 896), F32)], axis=1)
        padded = padded + (pltpu.roll(wide, 144 * sp, 1) if sp else wide)
        natural = natural + (pltpu.roll(wide, 136 * sp, 1) if sp else wide)
    par[0:8] = padded
    shifted = pltpu.roll(natural, 576, 1)
    par[8:16] = jnp.where(c == 0, natural, shifted)
    mask = lanes[0:1, :]

    @pl.loop(0, rows // 128)
    def _(i):
        at = pl.ds(pl.multiple_of(i * 128, 128), 128)
        to = pl.ds(pl.multiple_of(c * rows + i * 128, 128), 128)
        n1[to, :] = normalise(
            x_ref[at, :].astype(F32), mask, par[0:1, :], par[2:3, :], count
        ).astype(BF)

    n1_copy = remote(n1.at[own], n1.at[own], dsend.at[1], drecv.at[1], h.core)
    n1_copy.start()

    top = 0
    for b in range(4):
        first = max(0, b - 2)
        width = (b + 1 - first) * 256
        kpos = lax.broadcasted_iota(jnp.int32, (width, 256), 0) + first * 256
        qpos = lax.broadcasted_iota(jnp.int32, (width, 256), 1) + b * 256
        seen = (kpos <= qpos) & (
            segc[first * 256:first * 256 + width, 0:1] == segr[0:1, b * 256:b * 256 + 256]
        )
        mb[top:top + width, :] = jnp.where(seen, 0.0, -1e30)
        top += width

    each("stage1", A, AX)
    each("stage1", O, OX)
    each("stage2", A, AX)

    outs = []

    def flush(src, dst):
        copy = pltpu.make_async_copy(src, dst, osem.at[len(outs)])
        copy.start()
        outs.append(copy)

    flush(par, par_o)
    flush(mb, mb_o)

    def transposed(src, dst, n):
        copies = []
        for i in range(length // 256):
            slot = i % 2
            if i >= 2:
                copies[i - 2].wait()
            stage[slot] = src[256 * i:256 * i + 256, :].T
            copy = pltpu.make_async_copy(
                stage.at[slot], dst.at[:, pl.ds(256 * i, 256)], isem.at[n + slot])
            copy.start()
            copies.append(copy)
        copies[-2].wait()
        copies[-1].wait()

    cot_copy.wait_recv()
    flush(cot, cot_o)
    transposed(cot, cott_o, 0)
    n1_copy.wait_recv()
    transposed(n1, n1t_o, 0)

    each("stage1", I, IX)
    each("stage3", A, AX)
    for copy in local[3:]:
        copy.wait()

    def project(i, col, width, name, first_head):
        at = pl.ds(pl.multiple_of(i * 512, 512), 512)
        got = mm(n1[at, :], wa[:, col:col + width])
        where = 64 * first_head
        if name != "k":
            row = 12 if name == "q" else 13
            got = got + par[row:row + 1, where:where + width]
        low = got.astype(BF)
        if name == "q":
            low = low * jnp.asarray(0.125, BF)
        natural_ref, turned = {"q": (qn, qt), "k": (kn, kt), "v": (vn, vt)}[name]
        turned[where:where + width, at] = low.T
        natural_ref[at, where:where + width] = low

    for name, col in (("q", 0), ("k", 512), ("v", 1024)):
        for j in range(2):
            @pl.loop(0, 2)
            def _(i):
                project(i, col + 256 * j, 256, name, 4 * j)

    @pl.when(c == 0)
    def _():
        for name, col in (("q", 1536), ("k", 1664), ("v", 1792)):
            @pl.loop(0, 2)
            def _(i):
                project(i, col, 128, name, 8)

    @pl.when(c == 1)
    def _():
        for turned in (qt, kt, vt):
            turned[512:640, :] = jnp.zeros((128, length), BF)
        for natural_ref in (qn, kn, vn):
            natural_ref[:, 512:640] = jnp.zeros((length, 128), BF)

    flush(wa, wa_o)
    for src, dst in ((qn, qn_o), (kn, kn_o), (vn, vn_o), (qt, qt_o), (kt, kt_o)):
        flush(src, dst)
    each("stage1", U, UX)
    each("stage2", O, OX)

    wo_copy = remote(wog.at[c], wog.at[c], dsend.at[2], drecv.at[2], h.core)
    wo_copy.start()
    each("stage2", I, IX)

    lse[...] = jnp.zeros_like(lse)
    ot[c, 512:640, :] = jnp.zeros((128, length), BF)

    def attend(head):
        feat = pl.ds(pl.multiple_of(head * 64, 64), 64)
        pair = pl.ds(pl.multiple_of(head // 2 * 128, 128), 128)
        mine = lax.broadcasted_iota(jnp.int32, (128, 256), 0) // 64 == lax.rem(head, 2)
        top = 0
        for b in range(4):
            first = max(0, b - 2)
            width = (b + 1 - first) * 256
            keys = slice(first * 256, first * 256 + width)
            cols = slice(b * 256, b * 256 + 256)
            scores = mm(kn[keys, pair], jnp.where(mine, qt[pair, cols], jnp.zeros((), BF)))
            scores = scores + mb[top:top + width, :]
            top += width
            highest = jnp.max(scores, axis=0, keepdims=True)
            weights = jnp.exp(scores - highest)
            total = jnp.sum(weights, axis=0, keepdims=True)
            probs = (weights * (1.0 / total)).astype(BF)
            ot[c, feat, cols] = mm(vt[feat, keys], probs).astype(BF)
            lse[pl.ds(head, 1), cols] = highest + jnp.log(total)

    @pl.loop(0, 9 - c)
    def _(head):
        attend(head)

    flush(lse, lse_o)
    for i in range(2):
        at = pl.ds(pl.multiple_of(c * rows + 256 * i, 256), 256)
        att[c, 256 * i:256 * i + 256, :] = ot[c, :, at].T
    for i in range(2):
        at = pl.ds(pl.multiple_of((1 - c) * rows + 256 * i, 256), 256)
        vt[256 * i:256 * i + 256, 0:640] = ot[c, :, at].T
    att_copy = remote(vt.at[0:rows, 0:640], att.at[c], dsend.at[3], drecv.at[3], h.core)
    att_copy.start()
    ot_copy = remote(ot.at[c], ot.at[c], dsend.at[4], drecv.at[4], h.core)
    ot_copy.start()
    each("stage2", U, UX)

    wo_copy.wait_recv()
    for half in range(2):
        other = 512 * half
        for sp in range(8):
            wof[136 * sp:136 * sp + 136, :] = wog[half, 144 * sp:144 * sp + 144, 0:512].astype(F32)[0:136]
        wo[0:576, other:other + 512] = wof[0:576, :].astype(BF)
        wo[640:1152, other:other + 512] = wof[576:1088, :].astype(BF)
    for sp in range(8):
        wof[136 * sp:136 * sp + 136, 0:128] = wog[0, 144 * sp:144 * sp + 144, 512:640].astype(F32)[0:136]
    wo[0:576, 1024:1152] = wof[0:576, 0:128].astype(BF)
    wo[640:1152, 1024:1152] = wof[576:1088, 0:128].astype(BF)
    wo[576:640, :] = jnp.zeros((64, 1152), BF)
    wo[1152:1280, :] = jnp.zeros((128, 1152), BF)
    flush(wo.at[pl.ds(pl.multiple_of(c * 640, 128), 640)], wo_o)
    att_copy.wait_recv()
    att_copy.wait_send()

    @pl.loop(0, 4)
    def _(i):
        at = pl.ds(pl.multiple_of(i * 128, 128), 128)
        to = pl.ds(pl.multiple_of(c * rows + i * 128, 128), 128)
        x = (
            x_ref[at, :].astype(F32)
            + (mm(att[0, at, :], wo[0:640, :]) + mm(att[1, at, :], wo[640:1280, :]))
            + par[6:7, :]
        )
        mid[at, :] = x
        n2[to, :] = normalise(x, mask, par[1:2, :], par[3:4, :], count).astype(BF)

    flush(mid, mid_o)
    n2_copy = remote(n2.at[own], n2.at[own], dsend.at[5], drecv.at[5], h.core)
    n2_copy.start()
    ot_copy.wait_recv()
    flush(ot, ot_o)
    each("stage3", I, IX)
    n2_copy.wait_recv()
    transposed(n2, n2t_o, 0)
    bin_copy.wait_recv()
    flush(wi, wi_o)

    def hidden(j):
        slot = lax.rem(j, 2)
        cols = pl.ds(pl.multiple_of(j * 256, 256), 256)

        def out():
            return pltpu.make_async_copy(inner.at[slot], inner_o.at[:, cols], isem.at[2 + slot])

        @pl.when(j >= 2)
        def _():
            out().wait()
        half = j // 4
        off = pl.multiple_of(256 * (j - 4 * half), 256)
        bias = jnp.where(
            j < 8,
            bins[pl.ds(jnp.minimum(half, 1), 1), 0:1, pl.ds(jnp.where(j < 8, off, 0), 256)][0],
            jnp.concatenate([bins[0, 0:1, 1024:1152], bins[1, 0:1, 1024:1152]], axis=1),
        )

        @pl.loop(0, 4)
        def _(i):
            at = pl.ds(pl.multiple_of(i * 256, 256), 256)
            inner[slot, at, :] = mm(n2[at, :], wi[:, cols]) + bias
        out().start()

    @pl.loop(0, 9 - c)
    def _(j):
        hidden(j)
    for slot in range(2):
        pltpu.make_async_copy(inner.at[slot], inner_o.at[:, 0:256], isem.at[2 + slot]).wait()

    each("stage3", U, UX)
    flush(wu, wu_o)
    for copy in outs:
        copy.wait()
    for i in range(7):
        small_copy(s, h.xdev, i).wait_send()
    for copy in (bin_copy, cot_copy, n1_copy, wo_copy, ot_copy, n2_copy):
        copy.wait_send()
    each("drain", A + O + I + U, AX + OX + IX + UX)


def spread_features(matrix, shards):
    rows, width = matrix.shape
    each = width // shards
    return jnp.pad(matrix.reshape(rows, shards, each), ((0, 0), (0, 0), (0, BR - each))).reshape(
        rows, shards * BR)


def run_forward(tokens, segment_ids, norm_gains, norm_shifts, biases, w_qkv, w_o, w_in, b_in,
                w_out, cotangent):
    c = lax.axis_index("ctx")
    deep = ((0, 8), (0, 0))
    x = spread_features(tokens[0], 8)
    cot = spread_features(cotangent[0], 8)
    qkv = jnp.pad(w_qkv.reshape(136, 3, 1088), ((0, 8), (0, 0), (0, 128)))
    qkv = lax.dynamic_slice_in_dim(qkv, c * 576, 640, axis=2)
    keep = (lax.broadcasted_iota(jnp.int32, (1, 1, 640), 2) < 576)
    qkv = jnp.where(keep, qkv, jnp.zeros((), BF))
    pa = jnp.concatenate([qkv[:, :, :512].reshape(144, 1536), qkv[:, :, 512:].reshape(144, 384)], axis=1)
    po = jnp.pad(spread_features(w_o, 8), deep)
    po = jnp.concatenate([lax.dynamic_slice_in_dim(po, c * 512, 512, axis=1), po[:, 1024:]], axis=1)
    pi = lax.dynamic_slice_in_dim(jnp.pad(w_in, ((0, 8), (0, 128))), c * 1152, 1152, axis=1)
    pu = lax.dynamic_slice_in_dim(jnp.pad(w_out.T, ((0, 8), (0, 128))), c * 1152, 1152, axis=1)
    small = jnp.pad(jnp.concatenate([norm_gains, norm_shifts, biases], axis=0).astype(F32),
                    ((0, 0), (0, 120)))
    bins = lax.dynamic_slice_in_dim(jnp.pad(b_in.astype(F32), (0, 128)), c * 1152, 1152)
    bins = jnp.broadcast_to(bins[None], (8, 1152))
    segr = jnp.broadcast_to(segment_ids, (8, 1024))
    segc = segment_ids.reshape(1024, 1)
    lanes = jnp.broadcast_to(
        (lax.rem(lax.iota(jnp.int32, 1152), BR) < 136).astype(F32)[None], (8, 1152))
    hbm = pl.BlockSpec(memory_space=pltpu.HBM)
    vmem = pl.BlockSpec(memory_space=pltpu.VMEM)
    sds = jax.ShapeDtypeStruct
    shapes = [
        sds((1152, 1920), BF), sds((640, 1152), BF), sds((1152, 2304), BF), sds((1152, 2304), BF),
        sds((1152, 1024), BF), sds((1152, 1024), BF), sds((1152, 1024), BF), sds((1024, 1152), BF),
        sds((1024, 640), BF), sds((1024, 640), BF), sds((1024, 640), BF),
        sds((640, 1024), BF), sds((640, 1024), BF), sds((2, 640, 1024), BF),
        sds((16, 1024), F32), sds((512, 1152), F32), sds((1024, 2304), F32), sds((16, 1152), F32), sds((2304, 256), F32),
    ]
    V = pltpu.VMEM
    dma = pltpu.SemaphoreType.DMA
    scratch = [
        V((1152, 1920), BF), V((2, 1152, 640), BF), V((1280, 1152), BF), V((1152, 2304), BF),
        V((1152, 2304), BF), V((1024, 1152), BF), V((1024, 1152), BF), V((1024, 1152), BF),
        V((8, 8, 256), F32), V((16, 1152), F32), V((2, 8, 1152), F32),
        V((1024, 640), BF), V((1024, 640), BF), V((1024, 640), BF),
        V((640, 1024), BF), V((640, 1024), BF), V((640, 1024), BF),
        V((2304, 256), F32), V((2, 640, 1024), BF), V((2, 512, 640), BF), V((512, 1152), F32),
        V((2, 1024, 256), F32), V((2, 1152, 256), BF), V((16, 1024), F32), V((1088, 512), F32),
        dma((12, 15)), dma((12, 16)), dma((6,)), dma((6,)), dma((8,)), dma((9,)), dma((9,)),
        dma((19,)), dma((4,)),
    ]
    kept = pl.pallas_call(
        forward_kernel, out_shape=shapes, in_specs=[vmem] * 11, out_specs=[hbm] * len(shapes),
        scratch_shapes=scratch,
        compiler_params=pltpu.CompilerParams(
            collective_id=0, has_side_effects=True, vmem_limit_bytes=63 << 20),
        cost_estimate=pl.CostEstimate(flops=12 * 10**9, bytes_accessed=60 * 10**6, transcendentals=10**7),
        name="forward",
    )(x, cot, pa, po, pi, pu, small, bins, segr, segc, lanes)
    return x, lanes, kept


def nt(left, right):
    return lax.dot_general(left, right, (((1,), (1,)), ((), ())), preferred_element_type=F32)


def backward_kernel(
    par, lse, lanes, wa_h, wo_h, wi_h, wu_h, n1t_h, n2t_h, cott_h, cot_h, qn_h, kn_h, vn_h, qt_h,
    kt_h, ot_h, mid_h, inner_h, mb_h, x_h,
    mixed_o, tokens_o, out_o, in_o, qkv_o, proj_o, sums_o, go_h, gi_h,
    WI, WU, ACT, IG, COT, COTT, N2T, inner, F1, F2, F3, F4, mix, yr, xr, zr, tile, acck, accv,
    xra, zra, ysa, yra, go, xro, zro, yso, yro, sg, sgx, sgz, sgy, bsum,
    load, innersem, tilesem, heldsem, ysend, yrecv, xsend, xrecv, zsend, zrecv,
    axs, axr, azs, azr, ays, ayr, oxs, oxr, ozs, ozr, oys, oyr, gsend, grecv, dsend, drecv,
    outsem, finsend, finrecv, finloc,
):
    h = Place()
    c, s, t, z, x = h.c, h.s, h.t, h.z, h.x
    rows = 512
    count = 1088.0
    own0 = pl.multiple_of(c * rows, rows)
    sib0 = pl.multiple_of((1 - c) * rows, rows)
    n_tiles = 9 - c

    def fetch(n, src, dst):
        copy = pltpu.make_async_copy(src, dst, load.at[n])
        copy.start()
        return copy

    def tile_of(i):
        return jnp.where(i < 4, 4 * h.tb + i, jnp.where(i < 8, 4 * t + i - 4, 8))

    def inner_copy(i):
        slot = lax.rem(i, 2)
        return pltpu.make_async_copy(
            inner_h.at[:, pl.ds(pl.multiple_of(256 * tile_of(i), 256), 256)],
            inner.at[pl.ds(pl.multiple_of(1024 * slot, 1024), 1024)], innersem.at[slot])

    inner_copy(0).start()
    first = [fetch(0, cot_h, COT), fetch(1, wu_h, WU), fetch(2, cott_h, COTT)]
    second = [fetch(3, n2t_h, N2T), fetch(4, wi_h, WI), fetch(5, mid_h, F4)]
    h.greet()

    @pl.when(c == 1)
    def _():
        ACT[:, 2048:2304] = jnp.zeros((1024, 256), BF)
        IG[:, 2048:2304] = jnp.zeros((1024, 256), BF)
    sg[...] = jnp.zeros_like(sg)

    held = tile.at[0]

    outs = (go_h, gi_h)

    def y_copy(m, k):
        if isinstance(k, int) and k == 4:
            src = outs[m].at[:, :, :, pl.ds(pl.multiple_of(2048 + 128 * h.tb, 128), 128)]
            dst = yr.at[m, :, :, :, 1024:1152]
        else:
            src = outs[m].at[:, :, :, pl.ds(pl.multiple_of(1024 * h.tb + 256 * k, 256), 256)]
            dst = yr.at[m, :, :, :, pl.ds(pl.multiple_of(256 * k, 256), 256)]
        return remote(src, dst, ysend.at[m, k], yrecv.at[m, k], h.ydev)

    def cols_of(k):
        return slice(256 * k, 256 * k + 256) if k < 4 else slice(1024, 1152)

    def x_copy(m, k):
        cols = cols_of(k)
        return remote(yr.at[m, :, h.xb, :, cols], xr.at[m, :, :, cols],
                      xsend.at[m, k], xrecv.at[m, k], h.xdev)

    def slot_at(zp):
        return lax.rem(z - zp + 3, 4)

    def z_copy(m, k, i, zp):
        cols = cols_of(k)
        return remote(xr.at[m, zp, :, cols], zr.at[m, slot_at(zp), :, cols],
                      zsend.at[m, k, i], zrecv.at[m, k, slot_at(zp)], h.zdev(zp))

    def held_copy(m, k):
        if k < 4:
            src = outs[m].at[:, :, :, pl.ds(pl.multiple_of(1024 * t + 256 * k, 256), 256)]
            return pltpu.make_async_copy(src, held, heldsem.at[0])
        src = outs[m].at[:, :, :, pl.ds(pl.multiple_of(2048 + 128 * t, 128), 128)]
        return pltpu.make_async_copy(src, held.at[:, :, :, 0:128], heldsem.at[0])

    def after_y(m, k):
        mine = held_copy(m, k)
        mine.start()
        y_copy(m, k).wait_recv()
        mine.wait()
        cols = cols_of(k)
        width = 256 if k < 4 else 128

        @pl.loop(0, 4)
        def _(zp):
            for xp in range(2):
                yr[m, zp, xp, :, cols] = (
                    yr[m, zp, xp, :, cols].astype(F32) + held[zp, xp, :, 0:width].astype(F32)
                ).astype(BF)
        x_copy(m, k).start()

    def after_x(m, k):
        x_copy(m, k).wait_recv()
        cols = cols_of(k)

        @pl.loop(0, 4)
        def _(zp):
            xr[m, zp, :, cols] = (
                xr[m, zp, :, cols].astype(F32) + yr[m, zp, x, :, cols].astype(F32)
            ).astype(BF)
        for i, zp in enumerate(h.peers):
            z_copy(m, k, i, zp).start()

    def after_z(m, k):
        cols = cols_of(k)
        for i in range(3):
            ref = zr.at[m, i, :, cols]
            remote(ref, ref, zsend.at[m, k, 0], zrecv.at[m, k, i], h.core).wait_recv()
        F4[144 * m:144 * m + 144, cols] = (
            (xr[m, z, :, cols].astype(F32) + zr[m, 0, :, cols].astype(F32))
            + (zr[m, 1, :, cols].astype(F32) + zr[m, 2, :, cols].astype(F32)))

    def chunk(step, k):
        for m in range(2):
            if k < 4:
                step(m, k)
            else:
                @pl.when(c == 0)
                def _():
                    step(m, k)

    root = math.sqrt(2.0 / math.pi)
    for copy in first:
        copy.wait()

    @pl.loop(0, n_tiles)
    def _(i):
        base = pl.multiple_of(1024 * lax.rem(i, 2), 1024)
        inner_copy(i).wait()

        @pl.when(i + 1 < n_tiles)
        def _():
            inner_copy(i + 1).start()
        cols = pl.ds(pl.multiple_of(256 * tile_of(i), 256), 256)
        bsum[...] = jnp.zeros_like(bsum)

        @pl.loop(0, 4)
        def _(q):
            at = pl.ds(pl.multiple_of(256 * q, 256), 256)
            v = inner[pl.ds(pl.multiple_of(base + 256 * q, 256), 256), :]
            square = v * v
            bent = jnp.tanh(root * (v + 0.044715 * square * v))
            ACT[at, cols] = (0.5 * v * (1.0 + bent)).astype(BF)
            slope = 0.5 * (1.0 + bent) + (0.5 * root) * v * (1.0 - bent * bent) * (
                1.0 + (3.0 * 0.044715) * square)
            low = (mm(COT[at, :], WU[:, cols]) * slope).astype(BF)
            IG[at, cols] = low
            bsum[0:1, :] = bsum[0:1, :] + jnp.sum(low.astype(F32), axis=0, keepdims=True)

        @pl.when(i == 0)
        def _():
            second[0].wait()

        copies = []
        for m in range(2):
            @pl.loop(0, 2)
            def _(half):
                at = pl.ds(pl.multiple_of(576 * half, 576), 576)
                if m == 0:
                    got = mm(COTT[at, :], ACT[:, cols])
                else:
                    got = mm(N2T[at, :], IG[:, cols])
                for q in range(4):
                    block = got[144 * q:144 * q + 144, :]
                    where = (2 * half + q // 2, q % 2)
                    if m == 0:
                        tile[m, where[0], where[1]] = block.astype(BF)
                    else:
                        tile[m, where[0], where[1], 0:128] = block[0:128].astype(BF)
                        line = lax.broadcasted_iota(jnp.int32, (16, 256), 0) == 8
                        tile[m, where[0], where[1], 128:144] = jnp.where(
                            line, bsum[0:1, :], block[128:144]).astype(BF)
            copy = pltpu.make_async_copy(tile.at[m], outs[m].at[:, :, :, cols], tilesem.at[m])
            copy.start()
            copies.append(copy)
        for copy in copies:
            copy.wait()

        @pl.when(i < 4)
        def _():
            y_copy(0, i).start()
            y_copy(1, i).start()

        @pl.when(i == 8)
        def _():
            y_copy(0, 4).start()
            y_copy(1, 4).start()

    chunk(after_y, 0)

    second[1].wait()
    second[2].wait()

    def n2_copy(i):
        at = pl.ds(pl.multiple_of(384 * i, 128), 384)
        return remote(F3.at[:, at], F2.at[:, at], dsend.at[i], drecv.at[i], h.core)

    @pl.loop(0, 3)
    def _(i):
        at = pl.ds(pl.multiple_of(384 * i, 128), 384)
        F3[:, at] = nt(IG[pl.ds(sib0, rows), :], WI[at, :]).astype(BF)
        n2_copy(i).start()

    @pl.loop(0, 3)
    def _(i):
        at = pl.ds(pl.multiple_of(384 * i, 128), 384)
        F1[:, at] = nt(IG[pl.ds(own0, rows), :], WI[at, :])
    n2_sends = [n2_copy(i) for i in range(3)]

    wo_load = fetch(6, wo_h, WI.at[0:640, 0:1152])
    q_loads = [fetch(7, qn_h, IG.at[:, 0:640]), fetch(8, kn_h, IG.at[:, 640:1280]),
               fetch(9, vn_h, IG.at[:, 1280:1920]),
               fetch(11, n1t_h, N2T)]


    def mix_copy(i):
        at = pl.ds(pl.multiple_of(384 * i, 128), 384)
        return remote(WI.at[640:1152, at], mix.at[:, at], dsend.at[3 + i], drecv.at[3 + i], h.core)

    @pl.loop(0, 3)
    def _(i):
        at = pl.ds(pl.multiple_of(384 * i, 128), 384)
        WI[640:1152, at] = nt(ACT[pl.ds(sib0, rows), :], WU[at, :]).astype(BF)
        mix_copy(i).start()
    mix_sends = [mix_copy(i) for i in range(3)]

    mask = lanes[0:1, :]
    for copy in n2_sends:
        copy.wait_recv()

    @pl.loop(0, 4)
    def _(q):
        at = pl.ds(pl.multiple_of(128 * q, 128), 128)
        to = pl.ds(pl.multiple_of(own0 + 128 * q, 128), 128)
        grad = F1[at, :] + F2[at, :].astype(F32)
        v = F4[at, :]
        mean = jnp.sum(v, axis=1, keepdims=True) * (1.0 / count)
        spread = (v - mean) * mask
        rstd = lax.rsqrt(jnp.sum(spread * spread, axis=1, keepdims=True) * (1.0 / count) + EPS)
        hat = spread * rstd
        scaled = grad * par[1:2, :]
        grad_out = COT[to, :].astype(F32)
        got = grad_out + rstd * (
            scaled - jnp.sum(scaled, axis=1, keepdims=True) * (1.0 / count)
            - hat * (jnp.sum(scaled * hat, axis=1, keepdims=True) * (1.0 / count))) * mask
        low = got.astype(BF)
        F1[at, :] = got
        COT[to, :] = low
        sg[3:4, 0:1152] = sg[3:4, 0:1152] + jnp.sum(grad * hat, axis=0, keepdims=True)
        sg[4:5, 0:1152] = sg[4:5, 0:1152] + jnp.sum(grad, axis=0, keepdims=True)
        sg[5:6, 0:1152] = sg[5:6, 0:1152] + jnp.sum(grad_out, axis=0, keepdims=True)
        sg[6:7, 0:1152] = sg[6:7, 0:1152] + jnp.sum(low.astype(F32), axis=0, keepdims=True)

    bg_copy = remote(COT.at[pl.ds(own0, rows)], COT.at[pl.ds(own0, rows)], dsend.at[6], drecv.at[6], h.core)
    bg_copy.start()

    for copy in n2_sends:
        copy.wait_send()
    for copy in mix_sends:
        copy.wait_recv()

    @pl.loop(0, 3)
    def _(i):
        at = pl.ds(pl.multiple_of(384 * i, 128), 384)
        got = nt(ACT[pl.ds(own0, rows), :], WU[at, :]) + mix[:, at].astype(F32)
        F3[:, at] = (F4[:, at] + got + par[7:8, at]).astype(BF)
    mix_out = pltpu.make_async_copy(F3, mixed_o, outsem.at[0])
    mix_out.start()
    t_loads = [fetch(12, qt_h, WU.at[0:640, 0:1024]), fetch(13, kt_h, WU.at[0:640, 1024:2048])]
    chunk(after_y, 1)
    chunk(after_x, 0)
    o_loads = [fetch(14, ot_h.at[0], ACT.at[0:640, 0:1024]), fetch(15, ot_h.at[1], ACT.at[0:640, 1024:2048])]

    wo_load.wait()
    bg_copy.wait_recv()
    bg_copy.wait_send()
    for copy in mix_sends:
        copy.wait_send()

    @pl.loop(0, 5)
    def _(pair):
        at = pl.ds(pl.multiple_of(128 * pair, 128), 128)
        got = nt(COT[...], WI[at, 0:1152]).astype(BF)
        WI[0:1024, pl.ds(pl.multiple_of(1280 + 128 * pair, 128), 128)] = got
        COTT[at, :] = got.T

    for copy in o_loads:
        copy.wait()

    def proj(col, width, to):
        part = COT[:, col]
        inner[0:576, 0:width] = mm(ACT[0:576, 0:1024], part)
        inner[576:1088, 0:width] = mm(ACT[0:512, 1024:2048], part)
        for sp in range(8):
            block = jnp.concatenate(
                [inner[136 * sp:136 * sp + 136, 0:width], jnp.zeros((8, width), F32)], axis=0)
            go[sp // 2, sp % 2, :, to:to + width] = block.astype(BF)

    ocols = (slice(0, 512), slice(512, 640))

    def ox_copy(k):
        return remote(go.at[:, h.xb, :, ocols[k]], xro.at[:, :, ocols[k]], oxs.at[k], oxr.at[k], h.xdev)

    def oz_copy(k, i, zp):
        return remote(xro.at[zp, :, ocols[k]], zro.at[slot_at(zp), :, ocols[k]],
                      ozs.at[k, i], ozr.at[k, slot_at(zp)], h.zdev(zp))

    def oy_copy(k):
        return remote(yso.at[:, ocols[k]], yro.at[:, ocols[k]], oys.at[k], oyr.at[k], h.ydev)

    for q in range(2):
        proj(pl.ds(pl.multiple_of(512 * c + 256 * q, 256), 256), 256, 256 * q)
    ox_copy(0).start()

    @pl.when(c == 0)
    def _():
        proj(slice(1024, 1152), 128, 512)
        ox_copy(1).start()

    def o_after_x(k):
        ox_copy(k).wait_recv()

        @pl.loop(0, 4)
        def _(zp):
            xro[zp, :, ocols[k]] = (
                xro[zp, :, ocols[k]].astype(F32) + go[zp, x, :, ocols[k]].astype(F32)).astype(BF)
        for i, zp in enumerate(h.peers):
            oz_copy(k, i, zp).start()

    def o_after_z(k):
        for i in range(3):
            ref = zro.at[i, :, ocols[k]]
            remote(ref, ref, ozs.at[k, 0], ozr.at[k, i], h.core).wait_recv()
        cols = ocols[k]
        yso[:, cols] = (
            (xro[z, :, cols].astype(F32) + zro[0, :, cols].astype(F32))
            + (zro[1, :, cols].astype(F32) + zro[2, :, cols].astype(F32))).astype(BF)
        oy_copy(k).start()

    def o_after_y(k):
        oy_copy(k).wait_recv()
        F4[288:432, ocols[k]] = yso[:, ocols[k]].astype(F32) + yro[:, ocols[k]].astype(F32)

    def both(step, main, more):
        for k in main:
            step(k)

        @pl.when(c == 0)
        def _():
            for k in more:
                step(k)

    q_loads.append(fetch(10, mb_h, inner))
    for copy in q_loads + t_loads:
        copy.wait()
    ACT[:, 1536:1920] = jnp.zeros((1024, 384), BF)
    WI[512:640, 0:1024] = jnp.zeros((128, 1024), BF)

    def attend(head):
        pair = head // 2
        parity = lax.rem(head, 2)
        both_heads = pl.ds(pl.multiple_of(pair * 128, 128), 128)
        feat = pl.ds(pl.multiple_of(head * 64, 64), 64)
        on_rows = lax.broadcasted_iota(jnp.int32, (128, 256), 0) // 64 == parity
        on_lanes = lax.broadcasted_iota(jnp.int32, (256, 128), 1) // 64 == parity
        zero = jnp.zeros((), BF)
        qcol = both_heads
        kcol = pl.ds(pl.multiple_of(640 + pair * 128, 128), 128)
        vcol = pl.ds(pl.multiple_of(1280 + pair * 128, 128), 128)

        @pl.when(parity == 0)
        def _():
            acck[...] = jnp.zeros_like(acck)
            accv[...] = jnp.zeros_like(accv)
        top = 0
        for b in range(4):
            start = max(0, b - 2)
            width = (b + 1 - start) * 256
            keys = slice(start * 256, start * 256 + width)
            cols = slice(b * 256, b * 256 + 256)
            scores = mm(IG[keys, kcol], jnp.where(on_rows, WU[both_heads, cols], zero))
            probs = jnp.exp(scores + inner[top:top + width, :] - lse[pl.ds(head, 1), cols])
            top += width
            grads = mm(IG[keys, vcol], jnp.where(on_rows, COTT[both_heads, cols], zero))
            terms = jnp.sum(probs * grads, axis=0, keepdims=True)
            sgrad = (probs * (grads - terms)).astype(BF)
            accv[keys, :] = accv[keys, :] + mm(
                probs.astype(BF), jnp.where(on_lanes, WI[cols, vcol], zero))
            acck[keys, :] = acck[keys, :] + mm(
                sgrad, jnp.where(on_lanes, IG[cols, qcol], zero))
            WI[feat, cols] = (
                mm(WU[feat, 1024 + start * 256:1024 + start * 256 + width], sgrad) * 0.125
            ).astype(BF)

        @pl.when((parity == 1) | (head == 8 - c))
        def _():
            kto = pl.ds(pl.multiple_of(jnp.where(pair < 4, 512 + 128 * pair, 1664), 128), 128)
            vto = pl.ds(pl.multiple_of(jnp.where(pair < 4, 1024 + 128 * pair, 1792), 128), 128)
            ACT[:, kto] = acck[...].astype(BF)
            ACT[:, vto] = accv[...].astype(BF)

    def heads(low, high):
        @pl.loop(low, high)
        def _(head):
            attend(head)

    heads(0, 2)
    chunk(after_y, 2)
    chunk(after_x, 1)
    chunk(after_z, 0)
    both(o_after_x, (0,), (1,))
    heads(2, 5)
    chunk(after_y, 3)
    chunk(after_x, 2)
    chunk(after_z, 1)
    both(o_after_z, (0,), (1,))
    heads(5, 9 - c)

    @pl.loop(0, 4)
    def _(pair):
        at = pl.ds(pl.multiple_of(128 * pair, 128), 128)
        ACT[:, at] = WI[at, 0:1024].T

    @pl.when(c == 0)
    def _():
        ACT[:, 1536:1664] = WI[512:640, 0:1024].T
    wa_load = fetch(16, wa_h, WI.at[:, 0:1920])
    x_load = fetch(17, x_h, COT.at[0:512])

    acols = (slice(0, 512), slice(512, 1024), slice(1024, 1536), slice(1536, 1920))

    def ax_copy(k, i, zp):
        return remote(WU.at[rows_of(2 * zp + h.xb), acols[k]], xra.at[zp, :, acols[k]],
                      axs.at[k, i], axr.at[k, zp], h.xdev)

    def az_copy(k, i, zp):
        return remote(xra.at[zp, :, acols[k]], zra.at[slot_at(zp), :, acols[k]],
                      azs.at[k, i], azr.at[k, slot_at(zp)], h.zdev(zp))

    def ay_copy(k):
        return remote(ysa.at[:, acols[k]], yra.at[:, acols[k]], ays.at[k], ayr.at[k], h.ydev)

    def qkv_weights(k):
        cols = acols[k]

        @pl.loop(0, 2)
        def _(half):
            at = pl.ds(pl.multiple_of(576 * half, 576), 576)
            for col in range(cols.start, cols.stop, 256):
                part = slice(col, min(col + 256, cols.stop))
                WU[at, part] = mm(N2T[at, :], ACT[:, part]).astype(BF)
        for i, zp in enumerate(h.peers + [z]):
            ax_copy(k, i, zp).start()

    def a_after_x(k):
        cols = acols[k]
        for i, zp in enumerate(h.peers + [z]):
            ref = xra.at[zp, :, cols]
            remote(ref, ref, axs.at[k, 0], axr.at[k, zp], h.core).wait_recv()
            xra[zp, :, cols] = (
                xra[zp, :, cols].astype(F32) + WU[rows_of(2 * zp + x), cols].astype(F32)).astype(BF)
            if i < 3:
                az_copy(k, i, zp).start()

    def a_after_z(k):
        cols = acols[k]
        for i in range(3):
            ref = zra.at[i, :, cols]
            remote(ref, ref, azs.at[k, 0], azr.at[k, i], h.core).wait_recv()
        ysa[:, cols] = (
            (xra[z, :, cols].astype(F32) + zra[0, :, cols].astype(F32))
            + (zra[1, :, cols].astype(F32) + zra[2, :, cols].astype(F32))).astype(BF)
        ay_copy(k).start()

    def a_after_y(k):
        ay_copy(k).wait_recv()
        cols = acols[k]
        for n, col in enumerate(range(cols.start, cols.stop, 256)):
            part = slice(col, min(col + 256, cols.stop))
            at = 144 * (2 * k + n)
            inner[at:at + 144, 0:part.stop - part.start] = (
                ysa[:, part].astype(F32) + yra[:, part].astype(F32))

    both(qkv_weights, (0, 1, 2), (3,))

    mix_out.wait()
    wa_load.wait()

    def n1_copy(i):
        at = pl.ds(pl.multiple_of(384 * i, 128), 384)
        return remote(F3.at[:, at], F2.at[:, at], dsend.at[7 + i], drecv.at[7 + i], h.core)

    @pl.loop(0, 3)
    def _(i):
        at = pl.ds(pl.multiple_of(384 * i, 128), 384)
        F3[:, at] = nt(ACT[pl.ds(sib0, rows), 0:1920], WI[at, 0:1920]).astype(BF)
        n1_copy(i).start()

    @pl.loop(0, 4)
    def _(i):
        at = pl.ds(pl.multiple_of(256 * i, 256), 256)
        inner[pl.ds(pl.multiple_of(512 * i, 512), 512), :] = nt(
            ACT[pl.ds(own0, rows), 0:1920], WI[at, 0:1920])
    part = nt(ACT[pl.ds(own0, rows), 0:1920], WI[1024:1152, 0:1920])
    inner[2048:2304, 0:128] = part[0:256]
    inner[2048:2304, 128:256] = part[256:512]
    n1_sends = [n1_copy(i) for i in range(3)]

    @pl.loop(0, 15)
    def _(i):
        at = pl.ds(pl.multiple_of(128 * i, 128), 128)
        sg[0:1, at] = jnp.sum(ACT[:, at].astype(F32), axis=0, keepdims=True)
    chunk(after_x, 3)
    chunk(after_z, 2)
    chunk(after_y, 4)
    x_load.wait()
    for copy in n1_sends:
        copy.wait_recv()
    tok_outs = []
    for i in range(4):
        at = slice(128 * i, 128 * i + 128)
        last = slice(2048 + 128 * (i % 2), 2176 + 128 * (i % 2))
        part = jnp.concatenate(
            [inner[512 * j + 128 * i:512 * j + 128 * i + 128, :] for j in range(4)]
            + [inner[last, 128 * (i // 2):128 * (i // 2) + 128]], axis=1)
        grad = part + F2[at, :].astype(F32)
        v = COT[at, :].astype(F32)
        mean = jnp.sum(v, axis=1, keepdims=True) * (1.0 / count)
        spread = (v - mean) * mask
        rstd = lax.rsqrt(jnp.sum(spread * spread, axis=1, keepdims=True) * (1.0 / count) + EPS)
        hat = spread * rstd
        scaled = grad * par[0:1, :]
        F1[at, :] = F1[at, :] + rstd * (
            scaled - jnp.sum(scaled, axis=1, keepdims=True) * (1.0 / count)
            - hat * (jnp.sum(scaled * hat, axis=1, keepdims=True) * (1.0 / count))) * mask
        sg[1:2, 0:1152] = sg[1:2, 0:1152] + jnp.sum(grad * hat, axis=0, keepdims=True)
        sg[2:3, 0:1152] = sg[2:3, 0:1152] + jnp.sum(grad, axis=0, keepdims=True)
        copy = pltpu.make_async_copy(F1.at[at], tokens_o.at[at], outsem.at[2 + i])
        copy.start()
        tok_outs.append(copy)

    sgx_copy = remote(sg, sgx, gsend.at[0], grecv.at[0], h.xdev)
    sgx_copy.start()
    both(a_after_x, (0, 1, 2), (3,))
    both(o_after_y, (0,), (1,))
    sgx_copy.wait()
    sgx[...] = sgx[...] + sg[...]

    def sgz_copy(i, zp):
        return remote(sgx, sgz.at[slot_at(zp)], gsend.at[1 + i], grecv.at[1 + slot_at(zp)], h.zdev(zp))

    for i, zp in enumerate(h.peers):
        sgz_copy(i, zp).start()
    chunk(after_z, 3)
    chunk(after_x, 4)

    finals = []

    def finish(n, src, out):
        local = pltpu.make_async_copy(src, out.at[c], finloc.at[n])
        local.start()
        over = remote(src, out.at[c], finsend.at[n], finrecv.at[n], h.core)
        over.start()
        finals.append((local, over))

    both(a_after_z, (0, 1, 2), (3,))
    finish(0, F4.at[288:432, 0:640], proj_o)
    for i in range(3):
        remote(sgz.at[i], sgz.at[i], gsend.at[1], grecv.at[1 + i], h.core).wait_recv()
    for i, zp in enumerate(h.peers):
        sgz_copy(i, zp).wait_send()
    sg[...] = (sgx[...] + sgz[0]) + (sgz[1] + sgz[2])
    sgy_copy = remote(sg, sgy, gsend.at[4], grecv.at[4], h.ydev)
    sgy_copy.start()
    chunk(after_z, 4)
    finish(1, F4.at[0:144], out_o)
    finish(2, F4.at[144:288], in_o)
    sgy_copy.wait()
    sgx[...] = sg[...] + sgy[...]
    finish(3, sgx, sums_o)
    both(a_after_y, (0, 1, 2), (3,))
    finish(4, inner.at[0:1152], qkv_o)

    for copy in tok_outs:
        copy.wait()
    for copy in n1_sends:
        copy.wait_send()

    def drain(m, k):
        y_copy(m, k).wait_send()
        x_copy(m, k).wait_send()
        for i, zp in enumerate(h.peers):
            z_copy(m, k, i, zp).wait_send()

    for k in range(5):
        chunk(drain, k)

    def o_drain(k):
        ox_copy(k).wait_send()
        oy_copy(k).wait_send()
        for i, zp in enumerate(h.peers):
            oz_copy(k, i, zp).wait_send()

    both(o_drain, (0,), (1,))

    def a_drain(k):
        ay_copy(k).wait_send()
        for i, zp in enumerate(h.peers + [z]):
            ax_copy(k, i, zp).wait_send()
            if i < 3:
                az_copy(k, i, zp).wait_send()

    both(a_drain, (0, 1, 2), (3,))
    for local, over in finals:
        local.wait()
        over.wait()


def run_backward(x, lanes, kept):
    (wa, wo, wi, wu, n1t, n2t, cott, cot, qn, kn, vn, qt, kt, ot, lse, mid, inner, par, mb) = kept
    hbm = pl.BlockSpec(memory_space=pltpu.HBM)
    vmem = pl.BlockSpec(memory_space=pltpu.VMEM)
    sds = jax.ShapeDtypeStruct
    V = pltpu.VMEM
    dma = pltpu.SemaphoreType.DMA
    shapes = [
        sds((512, 1152), BF), sds((512, 1152), F32), sds((2, 144, 1152), F32),
        sds((2, 144, 1152), F32), sds((2, 1152, 256), F32), sds((2, 144, 640), F32),
        sds((2, 8, 1920), F32), sds((4, 2, 144, 2304), BF), sds((4, 2, 144, 2304), BF),
    ]
    scratch = [
        V((1152, 2304), BF), V((1152, 2304), BF), V((1024, 2304), BF), V((1024, 2304), BF),
        V((1024, 1152), BF), V((1152, 1024), BF), V((1152, 1024), BF), V((2304, 256), F32),
        V((512, 1152), F32), V((512, 1152), BF), V((512, 1152), BF), V((512, 1152), F32),
        V((512, 1152), BF), V((2, 4, 2, 144, 1152), BF), V((2, 4, 144, 1152), BF),
        V((2, 3, 144, 1152), BF), V((2, 4, 2, 144, 256), BF),
        V((1024, 128), F32), V((1024, 128), F32),
        V((4, 144, 1920), BF), V((3, 144, 1920), BF), V((144, 1920), BF), V((144, 1920), BF),
        V((4, 2, 144, 640), BF), V((4, 144, 640), BF), V((3, 144, 640), BF), V((144, 640), BF),
        V((144, 640), BF),
        V((8, 1920), F32), V((8, 1920), F32), V((3, 8, 1920), F32), V((8, 1920), F32), V((8, 256), F32),
        dma((18,)), dma((2,)), dma((2,)), dma((1,)),
        dma((2, 5)), dma((2, 5)), dma((2, 5)), dma((2, 5)), dma((2, 5, 3)), dma((2, 5, 3)),
        dma((4, 4)), dma((4, 4)), dma((4, 3)), dma((4, 3)), dma((4,)), dma((4,)),
        dma((2,)), dma((2,)), dma((2, 3)), dma((2, 3)), dma((2,)), dma((2,)),
        dma((5,)), dma((5,)), dma((10,)), dma((10,)), dma((6,)), dma((5,)), dma((5,)), dma((5,)),
    ]
    return pl.pallas_call(
        backward_kernel, out_shape=shapes, in_specs=[vmem] * 3 + [hbm] * 18,
        out_specs=[hbm] * len(shapes), scratch_shapes=scratch,
        compiler_params=pltpu.CompilerParams(
            collective_id=1, has_side_effects=True, vmem_limit_bytes=65300 << 10),
        cost_estimate=pl.CostEstimate(flops=40 * 10**9, bytes_accessed=80 * 10**6, transcendentals=2 * 10**7),
        name="backward",
    )(par, lse, lanes, wa, wo, wi, wu, n1t, n2t, cott, cot, qn, kn, vn, qt, kt, ot, mid, inner, mb, x)


def join_features(matrix):
    rows = matrix.shape[0]
    return matrix.reshape(rows, 8, BR)[:, :, :136].reshape(rows, 1088)


def join_heads(pair, col):
    start, more = {"q": (0, 1536), "k": (512, 1664), "v": (1024, 1792)}[col]
    return [pair[0][:, start:start + 512], pair[0][:, more:more + 64], pair[1][:, start:start + 512]]


def fused(tokens, segment_ids, norm_gains, norm_shifts, biases, w_qkv, w_o, w_in, b_in, w_out,
          cotangent):
    c = lax.axis_index("ctx")
    s = lax.axis_index("shard")
    x, lanes, kept = run_forward(tokens, segment_ids, norm_gains, norm_shifts, biases, w_qkv, w_o,
                                 w_in, b_in, w_out, cotangent)
    mixed, tokens_grad, out_g, in_g, qkv_g, proj_g, sums, _, _ = run_backward(x, lanes, kept)
    half = lambda blocks: lax.dynamic_slice_in_dim(blocks, c * 68, 68, axis=1)
    mine = half(qkv_g.reshape(16, 144, 256)).reshape(2, 8, 68, 256)
    mine = jnp.concatenate([mine[:, n] for n in range(8)], axis=2)[:, :, :1920]
    w_qkv_grad = jnp.concatenate(
        join_heads(mine, "q") + join_heads(mine, "k") + join_heads(mine, "v"), axis=1)
    mine = half(proj_g)
    w_o_grad = join_features(jnp.concatenate(
        [mine[0, :, :512], mine[1, :, :512], mine[0, :, 512:]], axis=1))
    mine = half(in_g)
    w_in_grad = jnp.concatenate([mine[0], mine[1][:, :1024]], axis=1)
    mine = half(out_g)
    w_out_grad = jnp.concatenate([mine[0], mine[1][:, :1024]], axis=1).T
    line = jnp.concatenate([in_g[0, 136:137], in_g[1, 136:137, :1024]], axis=1)
    b_in_grad = lax.dynamic_slice_in_dim(line, (2 * s + c) * 136, 136, axis=1)
    rows = sums[0] + sums[1]
    features = lax.dynamic_slice_in_dim(rows, s * BR + c * 68, 68, axis=1)
    first = sums[:, 0:1]
    heads = jnp.concatenate([jnp.concatenate(join_heads(first, n), axis=1) for n in ("q", "v")], axis=0)
    heads = lax.dynamic_slice_in_dim(heads, (2 * s + c) * 68, 68, axis=1)
    gains = jnp.concatenate([features[1:2], features[3:4]], axis=0)
    shifts = jnp.concatenate([features[2:3], features[4:5]], axis=0)
    biases_grad = jnp.concatenate([heads, features[6:7], features[5:6]], axis=0)
    return (join_features(mixed)[None], join_features(tokens_grad)[None], gains, shifts, biases_grad,
            w_qkv_grad, w_o_grad, w_in_grad, b_in_grad, w_out_grad)


def per_device(
    tokens, segment_ids, norm_gains, norm_shifts, biases, w_qkv, w_o, w_in, b_in, w_out, cotangent
):
    rows_here = tokens.shape[1]
    score_scale = HEAD_DIM ** (-0.5)
    gains_full, shifts_full, bias_full, qkv_full, proj_full, up_full, down_full = (
        lax.all_gather(norm_gains, "shard", axis=1, tiled=True),
        lax.all_gather(norm_shifts, "shard", axis=1, tiled=True),
        lax.all_gather(biases, "shard", axis=1, tiled=True),
        lax.all_gather(w_qkv, "shard", axis=0, tiled=True),
        lax.all_gather(w_o, "shard", axis=0, tiled=True),
        lax.all_gather(w_in, "shard", axis=0, tiled=True),
        lax.all_gather(w_out, "shard", axis=1, tiled=True),
    )
    gains_full = gains_full.astype(jnp.float32)
    shifts_full = shifts_full.astype(jnp.float32)
    bias_full = bias_full.astype(jnp.float32)
    hidden = tokens[0].astype(jnp.float32)
    normed, norm_back_one = jax.vjp(layer_norm, hidden, gains_full[0], shifts_full[0])
    normed_low = normed.astype(jnp.bfloat16)
    projected = jnp.dot(normed_low, qkv_full, preferred_element_type=jnp.float32)
    queries = (projected[:, :D] + bias_full[0]).astype(jnp.bfloat16)
    key_rows = projected[:, D : 2 * D].astype(jnp.bfloat16)
    value_rows = (projected[:, 2 * D :] + bias_full[1]).astype(jnp.bfloat16)
    all_keys, all_values = (
        lax.all_gather(key_rows, "ctx", axis=0, tiled=True),
        lax.all_gather(value_rows, "ctx", axis=0, tiled=True),
    )
    seq_length = all_keys.shape[0]
    offset = lax.axis_index("ctx") * rows_here
    key_segments = segment_ids[0]
    query_segments = lax.dynamic_slice_in_dim(key_segments, offset, rows_here)
    query_position = offset + lax.iota(jnp.int32, rows_here)
    key_position = lax.iota(jnp.int32, seq_length)
    allowed = (key_position[None, :] <= query_position[:, None]) & (
        key_segments[None, :] == query_segments[:, None]
    )
    query_heads = split_heads(queries)
    key_heads = split_heads(all_keys)
    value_heads = split_heads(all_values)

    def head_scores(query_head, key_head):
        scores = (
            jnp.einsum("qd,kd->qk", query_head, key_head, preferred_element_type=jnp.float32)
            * score_scale
        )
        return jnp.where(allowed, scores, -1e30)

    def head_forward(operands):
        query_head, key_head, value_head = operands
        masked = head_scores(query_head, key_head)
        highest = jnp.max(masked, axis=1, keepdims=True)
        weights = jnp.exp(masked - highest)
        summed = jnp.sum(weights, axis=1, keepdims=True)
        probabilities = (weights / summed).astype(jnp.bfloat16)
        result = jnp.dot(probabilities, value_head, preferred_element_type=jnp.float32)
        return (result, (highest + jnp.log(summed))[:, 0])

    head_out, log_total = lax.map(head_forward, (query_heads, key_heads, value_heads))
    attended = merge_heads(head_out).astype(jnp.bfloat16)
    middle = (
        hidden + jnp.dot(attended, proj_full, preferred_element_type=jnp.float32) + bias_full[2]
    )
    normed_two, norm_back_two = jax.vjp(layer_norm, middle, gains_full[1], shifts_full[1])
    normed_two_low = normed_two.astype(jnp.bfloat16)
    mlp_inputs = lax.all_gather(normed_two_low, "tp", axis=0, tiled=True)
    inner_values = jnp.dot(mlp_inputs, up_full, preferred_element_type=jnp.float32) + b_in.astype(
        jnp.float32
    )
    active, gelu_back = jax.vjp(gelu_tanh, inner_values)
    active_low = active.astype(jnp.bfloat16)
    mixed_rows = (
        middle
        + lax.psum_scatter(
            jnp.dot(active_low, down_full, preferred_element_type=jnp.float32).astype(jnp.bfloat16),
            "tp",
            scatter_dimension=0,
            tiled=True,
        ).astype(jnp.float32)
        + bias_full[3]
    )
    mixed_out = mixed_rows.astype(jnp.bfloat16)[None]
    grad_low = cotangent[0]
    grad_out = grad_low.astype(jnp.float32)
    grad_rows = lax.all_gather(grad_low, "tp", axis=0, tiled=True)
    down_grad = contract_rows(active_low, grad_rows)
    out_bias_grad = jnp.sum(grad_out, axis=0)
    active_grad = contract_cols(grad_rows, down_full)
    inner_grad = gelu_back(active_grad)[0].astype(jnp.bfloat16)
    up_grad = contract_rows(mlp_inputs, inner_grad)
    in_bias_grad = jnp.sum(inner_grad.astype(jnp.float32), axis=0)
    normed_two_grad = lax.psum_scatter(
        contract_cols(inner_grad, up_full), "tp", scatter_dimension=0, tiled=True
    )
    middle_part, gain_two_grad, shift_two_grad = norm_back_two(normed_two_grad)
    middle_grad = grad_out + middle_part
    branch_grad = middle_grad.astype(jnp.bfloat16)
    proj_grad = contract_rows(attended, branch_grad)
    attn_bias_grad = jnp.sum(branch_grad.astype(jnp.float32), axis=0)
    attended_grad = split_heads(contract_cols(branch_grad, proj_full).astype(jnp.bfloat16))

    def head_backward(operands):
        query_head, key_head, value_head, grad_head, log_head = operands
        masked = head_scores(query_head, key_head)
        probabilities = jnp.exp(masked - log_head[:, None])
        probs_grad = jnp.einsum(
            "qd,kd->qk", grad_head, value_head, preferred_element_type=jnp.float32
        )
        row_terms = jnp.sum(probabilities * probs_grad, axis=1, keepdims=True)
        scores_grad = (probabilities * (probs_grad - row_terms)).astype(jnp.bfloat16)
        query_grad = (
            jnp.dot(scores_grad, key_head, preferred_element_type=jnp.float32) * score_scale
        )
        key_grad = (
            jnp.einsum("qk,qd->kd", scores_grad, query_head, preferred_element_type=jnp.float32)
            * score_scale
        )
        value_grad = jnp.einsum(
            "qk,qd->kd",
            probabilities.astype(jnp.bfloat16),
            grad_head,
            preferred_element_type=jnp.float32,
        )
        return (query_grad, key_grad, value_grad)

    query_grads, key_grads, value_grads = lax.map(
        head_backward, (query_heads, key_heads, value_heads, attended_grad, log_total)
    )
    key_summed, value_summed = (
        lax.psum_scatter(
            merge_heads(key_grads).astype(jnp.bfloat16), "ctx", scatter_dimension=0, tiled=True
        ).astype(jnp.float32),
        lax.psum_scatter(
            merge_heads(value_grads).astype(jnp.bfloat16), "ctx", scatter_dimension=0, tiled=True
        ).astype(jnp.float32),
    )
    query_low = merge_heads(query_grads).astype(jnp.bfloat16)
    value_low = value_summed.astype(jnp.bfloat16)
    qkv_grad = jnp.concatenate([query_low, key_summed.astype(jnp.bfloat16), value_low], axis=1)
    qkv_weight_grad = contract_rows(normed_low, qkv_grad)
    query_bias_grad = jnp.sum(query_low.astype(jnp.float32), axis=0)
    value_bias_grad = jnp.sum(value_low.astype(jnp.float32), axis=0)
    normed_grad = contract_cols(qkv_grad, qkv_full)
    hidden_part, gain_one_grad, shift_one_grad = norm_back_one(normed_grad)
    tokens_grad = (middle_grad + hidden_part)[None]
    gains_grad = jnp.stack([gain_one_grad, gain_two_grad])
    shifts_grad = jnp.stack([shift_one_grad, shift_two_grad])
    biases_grad = jnp.stack([query_bias_grad, value_bias_grad, attn_bias_grad, out_bias_grad])
    gains_grad, shifts_grad, biases_grad, qkv_weight_grad, proj_grad = lax.psum(
        (gains_grad, shifts_grad, biases_grad, qkv_weight_grad, proj_grad), "tp"
    )
    (
        gains_grad,
        shifts_grad,
        biases_grad,
        qkv_weight_grad,
        proj_grad,
        up_grad,
        in_bias_grad,
        down_grad,
    ) = (
        lax.psum_scatter(gains_grad, ("shard", "ctx"), scatter_dimension=1, tiled=True),
        lax.psum_scatter(shifts_grad, ("shard", "ctx"), scatter_dimension=1, tiled=True),
        lax.psum_scatter(biases_grad, ("shard", "ctx"), scatter_dimension=1, tiled=True),
        lax.psum_scatter(qkv_weight_grad, ("shard", "ctx"), scatter_dimension=0, tiled=True),
        lax.psum_scatter(proj_grad, ("shard", "ctx"), scatter_dimension=0, tiled=True),
        lax.psum_scatter(up_grad, ("shard", "ctx"), scatter_dimension=0, tiled=True),
        lax.psum_scatter(in_bias_grad, ("shard", "ctx"), scatter_dimension=0, tiled=True),
        lax.psum_scatter(down_grad, ("shard", "ctx"), scatter_dimension=1, tiled=True),
    )
    return (
        mixed_out,
        tokens_grad,
        gains_grad,
        shifts_grad,
        biases_grad,
        qkv_weight_grad,
        proj_grad,
        up_grad,
        in_bias_grad[None],
        down_grad,
    )


def solution(mesh):
    in_specs = (
        P(("shard", "tp"), "ctx", None),
        P(("shard", "tp"), None),
        P(None, "shard"),
        P(None, "shard"),
        P(None, "shard"),
        P("shard", None),
        P("shard", None),
        P("shard", "tp"),
        P("tp"),
        P("tp", "shard"),
        P(("shard", "tp"), "ctx", None),
    )
    out_specs = (
        P(("shard", "tp"), "ctx", None),
        P(("shard", "tp"), "ctx", None),
        P(None, ("shard", "ctx")),
        P(None, ("shard", "ctx")),
        P(None, ("shard", "ctx")),
        P(("shard", "ctx"), None),
        P(("shard", "ctx"), None),
        P(("shard", "ctx"), "tp"),
        P("tp", ("shard", "ctx")),
        P("tp", ("shard", "ctx")),
    )
    fits = dict(mesh.shape) == {"shard": 8, "ctx": 2, "tp": 2}
    return jax.shard_map(
        fused if fits else per_device, mesh=mesh, in_specs=in_specs, out_specs=out_specs, check_vma=False
    )
```

```python
import math

import jax
import jax.numpy as jnp
from jax import lax
from jax.experimental import pallas as pl
from jax.experimental.pallas import tpu as pltpu
from jax.sharding import PartitionSpec as P

D = 1088
HEADS = 17
HEAD_DIM = 64


def layer_norm(values, gain_row, shift_row):
    center = jnp.mean(values, axis=-1, keepdims=True)
    spread = values - center
    variance = jnp.mean(spread * spread, axis=-1, keepdims=True)
    return spread * lax.rsqrt(variance + 1e-05) * gain_row + shift_row


def gelu_tanh(values):
    return (
        0.5
        * values
        * (
            1.0
            + jnp.tanh(math.sqrt(2.0 / math.pi) * (values + 0.044715 * values * values * values))
        )
    )


def contract_rows(left_side, right_side):
    return lax.dot_general(
        left_side, right_side, (((0,), (0,)), ((), ())), preferred_element_type=jnp.float32
    )


def contract_cols(left_side, right_side):
    return lax.dot_general(
        left_side, right_side, (((1,), (1,)), ((), ())), preferred_element_type=jnp.float32
    )


def split_heads(matrix):
    return matrix.reshape(matrix.shape[0], HEADS, HEAD_DIM).transpose(1, 0, 2)


def merge_heads(stacked):
    return stacked.transpose(1, 0, 2).reshape(stacked.shape[1], D)


BF = jnp.bfloat16
F32 = jnp.float32
MESH = pl.DeviceIdType.MESH
EPS = 1e-05
BR = 144
UNIT = 128


def mm(left, right):
    return jnp.dot(left, right, preferred_element_type=F32)


def remote(src, dst, send, recv, device):
    return pltpu.make_async_remote_copy(
        src_ref=src, dst_ref=dst, send_sem=send, recv_sem=recv,
        device_id=device, device_id_type=MESH,
    )


class Place:
    def __init__(self):
        self.s = lax.axis_index("shard")
        self.c = lax.axis_index("ctx")
        self.t = lax.axis_index("tp")
        self.z = self.s // 2
        self.x = self.s - 2 * self.z
        self.xb = 1 - self.x
        self.tb = 1 - self.t
        z = self.z
        self.peers = [
            z + 1 - 2 * lax.rem(z, 2),
            jnp.where(z < 2, 2, 1),
            jnp.where(z < 2, 3, 0),
        ]
        self.core = (self.s, 1 - self.c, self.t)
        self.xdev = (2 * z + self.xb, self.c, self.t)
        self.ydev = (self.s, self.c, self.tb)

    def zdev(self, zp):
        return (2 * zp + self.x, self.c, self.t)

    def greet(self):
        barrier = pltpu.get_barrier_semaphore()
        devices = [self.core, self.xdev, self.ydev] + [self.zdev(p) for p in self.peers]
        for device in devices:
            pl.semaphore_signal(barrier, inc=1, device_id=device, device_id_type=MESH)
        pl.semaphore_wait(barrier, len(devices))


def rows_of(s):
    return pl.ds(pl.multiple_of(s * BR, 16), BR)


class Gather:
    def __init__(self, here, number, own, loc, route, send, recv):
        self.h, self.p, self.own, self.loc, self.route = here, number, own, loc, route
        self.send, self.recv = send, recv
        self.two, self.three = (
            (here.ydev, here.xdev) if route == "zyx" else (here.xdev, here.ydev))
        if route == "zx":
            self.three = None

    def copy(self, src, s, t, device, i):
        return remote(src, self.loc(s, t), self.send.at[self.p, i],
                      self.recv.at[self.p, s * 2 + t], device)

    def take(self, s, t):
        ref = self.loc(s, t)
        self.copy(ref, s, t, self.h.core, 0).wait_recv()

    def along(self, k):
        h = self.h
        to = h.z + jnp.where(h.peers[k] < h.z, 1, -1)
        return (to >= 0) & (to <= 3), h.zdev(jnp.clip(to, 0, 3))

    def own_z(self):
        h = self.h
        pl.when(h.z < 3)(self.copy(self.own, h.s, h.t, h.zdev(jnp.minimum(h.z + 1, 3)), 0).start)
        pl.when(h.z > 0)(self.copy(self.own, h.s, h.t, h.zdev(jnp.maximum(h.z - 1, 0)), 1).start)

    def own_two(self):
        self.copy(self.own, self.h.s, self.h.t, self.two, 5).start()

    def own_three(self):
        if self.route in ("zxy", "zyx"):
            self.copy(self.own, self.h.s, self.h.t, self.three, 10).start()

    def z(self, k):
        h = self.h
        s = 2 * h.peers[k] + h.x
        self.take(s, h.t)
        block = self.loc(s, h.t)
        on, device = self.along(k)
        pl.when(on)(self.copy(block, s, h.t, device, 2 + k).start)
        self.copy(block, s, h.t, self.two, 6 + k).start()
        if self.three:
            self.copy(block, s, h.t, self.three, 11 + k).start()

    def second(self, k):
        h = self.h
        zp = ([h.z] + h.peers)[k]
        s, t = (2 * zp + h.x, h.tb) if self.route == "zyx" else (2 * zp + h.xb, h.t)
        self.take(s, t)
        if self.three:
            self.copy(self.loc(s, t), s, t, self.three, 14 + k).start()

    def third(self, k):
        h = self.h
        zp = ([h.z] + h.peers)[k]
        if self.route == "zyx":
            self.take(2 * zp + h.xb, h.t)
            self.take(2 * zp + h.xb, h.tb)
        elif self.three:
            if not (self.route == "kv" and k == 0):
                self.take(2 * zp + h.x, h.tb)
            self.take(2 * zp + h.xb, h.tb)

    def drain(self):
        h = self.h

        def sent(i):
            return self.copy(self.own, h.s, h.t, h.core, i).wait_send

        pl.when(h.z < 3)(sent(0))
        pl.when(h.z > 0)(sent(1))
        for k in range(3):
            pl.when(self.along(k)[0])(sent(2 + k))
        for i in range(5, 9):
            sent(i)()
        if self.three:
            for i in range(10 if self.route != "kv" else 11, 18):
                sent(i)()


def normalise(x, mask, gain, shift, count):
    mean = jnp.sum(x, axis=1, keepdims=True) * (1.0 / count)
    spread = (x - mean) * mask
    var = jnp.sum(spread * spread, axis=1, keepdims=True) * (1.0 / count)
    return spread * lax.rsqrt(var + EPS) * gain + shift


def forward_kernel(
    x_ref, cot_ref, pa, po, pi, pu, small, bin_ref, segr, segc, lanes,
    wa_o, wo_o, wi_o, wu_o, n1t_o, n2t_o, cot_o, qn_o, kn_o, vn_o, qt_o, kt_o, ot_o,
    lse_o, mid_o, slope_o, act_o, go_o, par_o, mb_o,
    wa, wog, wo, wi, wu, n1, cot, cott, n2, sm, par, bins, qn, kn, vn, qt, kt, vt, mb, ot, att, mid,
    slope, act, tile, stage, lse,
    send, recv, dsend, drecv, ssend, srecv, lsem, osem, isem,
):
    h = Place()
    c, s, t = h.c, h.s, h.t
    rows = x_ref.shape[0]
    length = 2 * rows
    count = 1088
    own = pl.ds(pl.multiple_of(c * rows, rows), rows)
    sib = pl.ds(pl.multiple_of((1 - c) * rows, rows), rows)

    def piece(number, src, buf, route, src_col, col, width):
        if route == "kv":
            own_ref = src.at[:, pl.ds(pl.multiple_of(src_col(t), UNIT), width)]
        else:
            own_ref = src.at[:, pl.ds(src_col, width)]

        def loc(sp, tp):
            where = col(tp)
            if not isinstance(where, int):
                where = pl.multiple_of(where, UNIT)
            return buf.at[rows_of(sp), pl.ds(where, width)]

        return Gather(h, number, own_ref, loc, route, send, recv)

    A = ([piece(0, pa, wa, "zx", 0, lambda tp: 0, 512),
          piece(1, pa, wa, "kv", lambda tp: 512 + 512 * tp, lambda tp: 512 + 512 * tp, 512)],
         [piece(7, pa, wa, "zx", 1536, lambda tp: 1536, 128),
          piece(8, pa, wa, "kv", lambda tp: 1664 + 128 * tp, lambda tp: 1664 + 128 * tp, 128)])
    O = ([piece(2, po, wog.at[c], "zx", 0, lambda tp: 0, 512)],
         [piece(9, po, wog.at[c], "zx", 512, lambda tp: 512, 128)])
    I = ([piece(3, pi, wi, "zxy", 0, lambda tp: 1024 * tp, 640),
          piece(4, pi, wi, "zyx", 640, lambda tp: 1024 * tp + 640, 384)],
         [piece(10, pi, wi, "zyx", 1024, lambda tp: 2048 + 128 * tp, 128)])
    U = ([piece(5, pu, wu, "zxy", 0, lambda tp: 1024 * tp, 640),
          piece(6, pu, wu, "zyx", 640, lambda tp: 1024 * tp + 640, 384)],
         [piece(11, pu, wu, "zyx", 1024, lambda tp: 2048 + 128 * tp, 128)])

    def each(group, stage, *args):
        for p in group[0]:
            getattr(p, stage)(*args)

        @pl.when(c == 0)
        def _():
            for p in group[1]:
                getattr(p, stage)(*args)

    def small_copy(sp, device, i):
        return remote(sm.at[sp], sm.at[sp], ssend.at[i], srecv.at[sp], device)

    @pl.when(c == 1)
    def _():
        wi[:, 2048:2304] = jnp.zeros((1152, 256), BF)
        wu[:, 2048:2304] = jnp.zeros((1152, 256), BF)
        wa[:, 1536:1920] = jnp.zeros((1152, 384), BF)

    local = []

    def fill(src, dst):
        copy = pltpu.make_async_copy(src, dst, lsem.at[len(local)])
        copy.start()
        local.append(copy)

    fill(small, sm.at[s])
    fill(bin_ref, bins.at[t])
    fill(cot_ref, cot.at[own])
    fill(pa, wa.at[rows_of(s)])
    fill(po, wog.at[c, rows_of(s)])
    fill(pi.at[:, 0:1024], wi.at[rows_of(s), pl.ds(pl.multiple_of(t * 1024, UNIT), 1024)])
    fill(pu.at[:, 0:1024], wu.at[rows_of(s), pl.ds(pl.multiple_of(t * 1024, UNIT), 1024)])
    fill(pi.at[:, 1024:1152], wi.at[rows_of(s), pl.ds(pl.multiple_of(2048 + t * 128, UNIT), 128)])
    fill(pu.at[:, 1024:1152], wu.at[rows_of(s), pl.ds(pl.multiple_of(2048 + t * 128, UNIT), 128)])
    h.greet()
    local[0].wait()
    local[1].wait()
    for i, zp in enumerate(h.peers):
        small_copy(s, h.zdev(zp), i).start()
    small_copy(s, h.xdev, 3).start()
    bin_copy = remote(bins.at[t], bins.at[t], ssend.at[7], srecv.at[8], h.ydev)
    bin_copy.start()
    each(A, "own_z")
    each(A, "own_two")
    each(O, "own_z")
    each(I, "own_three")
    local[2].wait()
    cot_copy = remote(cot.at[own], cot.at[own], dsend.at[0], drecv.at[0], h.core)
    cot_copy.start()

    top = 0
    for b in range(4):
        first = max(0, b - 2)
        width = (b + 1 - first) * 256
        kpos = lax.broadcasted_iota(jnp.int32, (width, 256), 0) + first * 256
        qpos = lax.broadcasted_iota(jnp.int32, (width, 256), 1) + b * 256
        seen = (kpos <= qpos) & (
            segc[first * 256:first * 256 + width, 0:1] == segr[0:1, b * 256:b * 256 + 256]
        )
        mb[top:top + width, :] = jnp.where(seen, 0.0, -1e30)
        top += width

    for k, zp in enumerate(h.peers):
        sp = 2 * zp + h.x
        small_copy(sp, h.xdev, 4 + k).wait_recv()
        small_copy(sp, h.xdev, 4 + k).start()
    each(A, "z", 0)
    for zp in [h.z] + h.peers:
        small_copy(2 * zp + h.xb, h.xdev, 0).wait_recv()

    padded = jnp.zeros((8, 1152), F32)
    natural = jnp.zeros((8, 1152), F32)
    for sp in range(8):
        wide = jnp.concatenate([sm[sp], jnp.zeros((8, 896), F32)], axis=1)
        padded = padded + (pltpu.roll(wide, 144 * sp, 1) if sp else wide)
        natural = natural + (pltpu.roll(wide, 136 * sp, 1) if sp else wide)
    par[0:8] = padded
    shifted = pltpu.roll(natural, 576, 1)
    par[8:16] = jnp.where(c == 0, natural, shifted)
    mask = lanes[0:1, :]
    each(A, "second", 0)

    @pl.loop(0, rows // 128)
    def _(i):
        at = pl.ds(pl.multiple_of(i * 128, 128), 128)
        to = pl.ds(pl.multiple_of(c * rows + i * 128, 128), 128)
        n1[to, :] = normalise(
            x_ref[at, :].astype(F32), mask, par[0:1, :], par[2:3, :], count
        ).astype(BF)

    n1_copy = remote(n1.at[own], n1.at[own], dsend.at[1], drecv.at[1], h.core)
    n1_copy.start()

    outs = []

    def flush(src, dst):
        copy = pltpu.make_async_copy(src, dst, osem.at[len(outs)])
        copy.start()
        outs.append(copy)

    flush(par, par_o)
    flush(mb, mb_o)

    def turn(src, dst, i, later):
        slot = i % 2
        if later:
            pltpu.make_async_copy(stage.at[slot], dst.at[:, 0:256], isem.at[slot]).wait()
        stage[slot] = src[256 * i:256 * i + 256, :].T
        pltpu.make_async_copy(
            stage.at[slot], dst.at[:, pl.ds(256 * i, 256)], isem.at[slot]).start()

    each(A, "z", 1)
    each(I, "own_z")
    each(A, "second", 1)
    cot_copy.wait_recv()
    flush(cot, cot_o)
    for i in range(2):
        cott[:, 256 * i:256 * i + 256] = cot[256 * i:256 * i + 256, :].T
    each(A, "z", 2)
    each(O, "own_two")
    each(O, "z", 0)
    each(A, "second", 2)
    n1_copy.wait_recv()
    for i in range(2):
        turn(n1, n1t_o, i, False)
    each(O, "z", 1)
    each(A, "second", 3)
    each(O, "z", 2)
    each(I, "own_two")
    each(I, "z", 0)

    def project(i, col, width, name, first_head):
        at = pl.ds(pl.multiple_of(i * 512, 512), 512)
        got = mm(n1[at, :], wa[:, col:col + width])
        where = 64 * first_head
        if name != "k":
            row = 12 if name == "q" else 13
            got = got + par[row:row + 1, where:where + width]
        low = got.astype(BF)
        if name == "q":
            low = low * jnp.asarray(0.125, BF)
        natural_ref, turned = {"q": (qn, qt), "k": (kn, kt), "v": (vn, vt)}[name]
        turned[where:where + width, at] = low.T
        natural_ref[at, where:where + width] = low

    local[3].wait()
    for j in range(2):
        @pl.loop(0, 2)
        def _(i):
            project(i, 256 * j, 256, "q", 4 * j)
    for k in range(4):
        each(A, "third", k)
    for name, col in (("k", 512), ("v", 1024)):
        for j in range(2):
            @pl.loop(0, 2)
            def _(i):
                project(i, col + 256 * j, 256, name, 4 * j)
    each(I, "z", 1)
    each(U, "own_z")
    each(I, "second", 0)

    @pl.when(c == 0)
    def _():
        for name, col in (("q", 1536), ("k", 1664), ("v", 1792)):
            @pl.loop(0, 2)
            def _(i):
                project(i, col, 128, name, 8)

    @pl.when(c == 1)
    def _():
        for turned in (qt, kt, vt):
            turned[512:640, :] = jnp.zeros((128, length), BF)
        for natural_ref in (qn, kn, vn):
            natural_ref[:, 512:640] = jnp.zeros((length, 128), BF)

    flush(wa, wa_o)
    for src, dst in ((qn, qn_o), (kn, kn_o), (vn, vn_o), (qt, qt_o), (kt, kt_o)):
        flush(src, dst)
    lse[...] = jnp.zeros_like(lse)
    ot[c, 512:640, :] = jnp.zeros((128, length), BF)

    def attend(head):
        feat = pl.ds(pl.multiple_of(head * 64, 64), 64)
        pair = pl.ds(pl.multiple_of(head // 2 * 128, 128), 128)
        mine = lax.broadcasted_iota(jnp.int32, (128, 256), 0) // 64 == lax.rem(head, 2)
        top = 0
        for b in range(4):
            first = max(0, b - 2)
            width = (b + 1 - first) * 256
            keys = slice(first * 256, first * 256 + width)
            cols = slice(b * 256, b * 256 + 256)
            scores = mm(kn[keys, pair], jnp.where(mine, qt[pair, cols], jnp.zeros((), BF)))
            scores = scores + mb[top:top + width, :]
            top += width
            highest = jnp.max(scores, axis=0, keepdims=True)
            weights = jnp.exp(scores - highest)
            total = jnp.sum(weights, axis=0, keepdims=True)
            probs = (weights * (1.0 / total)).astype(BF)
            ot[c, feat, cols] = mm(vt[feat, keys], probs).astype(BF)
            lse[pl.ds(head, 1), cols] = highest + jnp.log(total)

    def heads(low, high):
        @pl.loop(low, high)
        def _(head):
            attend(head)

    each(I, "z", 2)
    each(O, "second", 0)
    heads(0, 2)
    each(O, "second", 1)
    each(O, "second", 2)
    each(I, "second", 1)
    each(U, "own_two")
    each(U, "own_three")
    heads(2, 4)
    each(O, "second", 3)
    local[4].wait()
    wo_copy = remote(wog.at[c], wog.at[c], dsend.at[2], drecv.at[2], h.core)
    wo_copy.start()
    each(I, "second", 2)
    each(U, "z", 0)
    heads(4, 6)
    each(I, "second", 3)
    each(I, "third", 0)
    each(U, "z", 1)
    heads(6, 9 - c)
    each(U, "second", 0)
    each(I, "third", 1)
    each(U, "z", 2)

    flush(lse, lse_o)
    for i in range(2):
        at = pl.ds(pl.multiple_of(c * rows + 256 * i, 256), 256)
        att[c, 256 * i:256 * i + 256, :] = ot[c, :, at].T
    for i in range(2):
        at = pl.ds(pl.multiple_of((1 - c) * rows + 256 * i, 256), 256)
        vt[256 * i:256 * i + 256, 0:640] = ot[c, :, at].T
    att_copy = remote(vt.at[0:rows, 0:640], att.at[c], dsend.at[3], drecv.at[3], h.core)
    att_copy.start()
    ot_copy = remote(ot.at[c], ot.at[c], dsend.at[4], drecv.at[4], h.core)
    ot_copy.start()
    each(U, "second", 1)

    wo_copy.wait_recv()

    def order_rows(half, src, to, width):
        for sp in range(8):
            slope[136 * sp:136 * sp + 136, 0:width] = (
                wog[half, 144 * sp:144 * sp + 144, src:src + width].astype(F32)[0:136])
        wo[0:576, to:to + width] = slope[0:576, 0:width].astype(BF)
        wo[640:1152, to:to + width] = slope[576:1088, 0:width].astype(BF)

    for half in range(2):
        for q in range(2):
            order_rows(half, 256 * q, 512 * half + 256 * q, 256)
    order_rows(0, 512, 1024, 128)
    wo[576:640, :] = jnp.zeros((64, 1152), BF)
    wo[1152:1280, :] = jnp.zeros((128, 1152), BF)
    flush(wo.at[pl.ds(pl.multiple_of(c * 640, 128), 640)], wo_o)
    att_copy.wait_recv()
    att_copy.wait_send()
    each(I, "third", 2)

    @pl.loop(0, 4)
    def _(i):
        at = pl.ds(pl.multiple_of(i * 128, 128), 128)
        to = pl.ds(pl.multiple_of(c * rows + i * 128, 128), 128)
        x = (
            x_ref[at, :].astype(F32)
            + (mm(att[0, at, :], wo[0:640, :]) + mm(att[1, at, :], wo[640:1280, :]))
            + par[6:7, :]
        )
        mid[at, :] = x
        n2[to, :] = normalise(x, mask, par[1:2, :], par[3:4, :], count).astype(BF)

    flush(mid, mid_o)
    n2_copy = remote(n2.at[own], n2.at[own], dsend.at[5], drecv.at[5], h.core)
    n2_copy.start()
    ot_copy.wait_recv()
    flush(ot, ot_o)
    each(U, "second", 2)
    each(I, "third", 3)
    for copy in local[5:]:
        copy.wait()
    flush(wi, wi_o)
    for i in range(2, 4):
        cott[:, 256 * i:256 * i + 256] = cot[256 * i:256 * i + 256, :].T
        turn(n1, n1t_o, i, True)
    n2_copy.wait_recv()
    for i in range(4):
        turn(n2, n2t_o, i, True)
    bin_copy.wait_recv()
    root = math.sqrt(2.0 / math.pi)

    def slot_copies(slot, cols):
        base = pl.multiple_of(1024 * slot, 1024)
        return (
            pltpu.make_async_copy(slope.at[pl.ds(base, 1024)], slope_o.at[:, cols], isem.at[2 + slot]),
            pltpu.make_async_copy(act.at[slot], act_o.at[:, cols], isem.at[4 + slot]),
            pltpu.make_async_copy(tile.at[slot], go_o.at[:, :, :, cols], isem.at[6 + slot]),
        )

    def hidden(i):
        j = jnp.where(i < 4, 4 * h.tb + i, jnp.where(i < 8, 4 * t + i - 4, 8))
        slot = lax.rem(i, 2)
        base = pl.multiple_of(1024 * slot, 1024)
        cols = pl.ds(pl.multiple_of(j * 256, 256), 256)

        @pl.when(i >= 2)
        def _():
            for copy in slot_copies(slot, cols):
                copy.wait()
        half = j // 4
        off = pl.multiple_of(256 * (j - 4 * half), 256)
        bias = jnp.where(
            j < 8,
            bins[pl.ds(jnp.minimum(half, 1), 1), 0:1, pl.ds(jnp.where(j < 8, off, 0), 256)][0],
            jnp.concatenate([bins[0, 0:1, 1024:1152], bins[1, 0:1, 1024:1152]], axis=1),
        )

        @pl.loop(0, 4)
        def _(q):
            at = pl.ds(pl.multiple_of(q * 256, 256), 256)
            v = mm(n2[at, :], wi[:, cols]) + bias
            square = v * v
            bent = jnp.tanh(root * (v + 0.044715 * square * v))
            act[slot, at, :] = (0.5 * v * (1.0 + bent)).astype(BF)
            slope[pl.ds(pl.multiple_of(base + 256 * q, 256), 256), :] = (
                0.5 * (1.0 + bent) + (0.5 * root) * v * (1.0 - bent * bent) * (
                    1.0 + (3.0 * 0.044715) * square))

        @pl.loop(0, 2)
        def _(half):
            got = mm(cott[pl.ds(pl.multiple_of(576 * half, 576), 576), :], act[slot])
            for q in range(4):
                tile[slot, 2 * half + q // 2, q % 2] = got[144 * q:144 * q + 144, :].astype(BF)
        for copy in slot_copies(slot, cols):
            copy.start()

    def units(low, high):
        @pl.loop(low, high)
        def _(i):
            hidden(i)

    units(0, 2)
    each(U, "second", 3)
    each(U, "third", 0)
    units(2, 4)
    each(U, "third", 1)
    units(4, 9 - c)
    each(U, "third", 2)
    each(U, "third", 3)
    flush(wu, wu_o)
    for slot in range(2):
        for copy in slot_copies(slot, pl.ds(0, 256)):
            copy.wait()
    for slot in range(2):
        pltpu.make_async_copy(stage.at[slot], n2t_o.at[:, 0:256], isem.at[slot]).wait()
    for copy in outs:
        copy.wait()
    for i in range(7):
        small_copy(s, h.xdev, i).wait_send()
    for copy in (bin_copy, cot_copy, n1_copy, wo_copy, ot_copy, n2_copy):
        copy.wait_send()
    for group in (A, O, I, U):
        each(group, "drain")


def spread_features(matrix, shards):
    rows, width = matrix.shape
    each = width // shards
    return jnp.pad(matrix.reshape(rows, shards, each), ((0, 0), (0, 0), (0, BR - each))).reshape(
        rows, shards * BR)


def run_forward(tokens, segment_ids, norm_gains, norm_shifts, biases, w_qkv, w_o, w_in, b_in,
                w_out, cotangent):
    c = lax.axis_index("ctx")
    deep = ((0, 8), (0, 0))
    x = spread_features(tokens[0], 8)
    cot = spread_features(cotangent[0], 8)
    qkv = jnp.pad(w_qkv.reshape(136, 3, 1088), ((0, 8), (0, 0), (0, 128)))
    qkv = lax.dynamic_slice_in_dim(qkv, c * 576, 640, axis=2)
    keep = (lax.broadcasted_iota(jnp.int32, (1, 1, 640), 2) < 576)
    qkv = jnp.where(keep, qkv, jnp.zeros((), BF))
    pa = jnp.concatenate([qkv[:, :, :512].reshape(144, 1536), qkv[:, :, 512:].reshape(144, 384)], axis=1)
    po = jnp.pad(spread_features(w_o, 8), deep)
    po = jnp.concatenate([lax.dynamic_slice_in_dim(po, c * 512, 512, axis=1), po[:, 1024:]], axis=1)
    pi = lax.dynamic_slice_in_dim(jnp.pad(w_in, ((0, 8), (0, 128))), c * 1152, 1152, axis=1)
    pu = lax.dynamic_slice_in_dim(jnp.pad(w_out.T, ((0, 8), (0, 128))), c * 1152, 1152, axis=1)
    small = jnp.pad(jnp.concatenate([norm_gains, norm_shifts, biases], axis=0).astype(F32),
                    ((0, 0), (0, 120)))
    bins = lax.dynamic_slice_in_dim(jnp.pad(b_in.astype(F32), (0, 128)), c * 1152, 1152)
    bins = jnp.broadcast_to(bins[None], (8, 1152))
    segr = jnp.broadcast_to(segment_ids, (8, 1024))
    segc = segment_ids.reshape(1024, 1)
    lanes = jnp.broadcast_to(
        (lax.rem(lax.iota(jnp.int32, 1152), BR) < 136).astype(F32)[None], (8, 1152))
    hbm = pl.BlockSpec(memory_space=pltpu.HBM)
    vmem = pl.BlockSpec(memory_space=pltpu.VMEM)
    sds = jax.ShapeDtypeStruct
    shapes = [
        sds((1152, 1920), BF), sds((640, 1152), BF), sds((1152, 2304), BF), sds((1152, 2304), BF),
        sds((1152, 1024), BF), sds((1152, 1024), BF), sds((1024, 1152), BF),
        sds((1024, 640), BF), sds((1024, 640), BF), sds((1024, 640), BF),
        sds((640, 1024), BF), sds((640, 1024), BF), sds((2, 640, 1024), BF),
        sds((16, 1024), F32), sds((512, 1152), F32), sds((1024, 2304), F32), sds((1024, 2304), BF),
        sds((4, 2, 144, 2304), BF), sds((16, 1152), F32), sds((2304, 256), F32),
    ]
    V = pltpu.VMEM
    dma = pltpu.SemaphoreType.DMA
    scratch = [
        V((1152, 1920), BF), V((2, 1152, 640), BF), V((1280, 1152), BF), V((1152, 2304), BF),
        V((1152, 2304), BF), V((1024, 1152), BF), V((1024, 1152), BF), V((1152, 1024), BF),
        V((1024, 1152), BF),
        V((8, 8, 256), F32), V((16, 1152), F32), V((2, 8, 1152), F32),
        V((1024, 640), BF), V((1024, 640), BF), V((1024, 640), BF),
        V((640, 1024), BF), V((640, 1024), BF), V((640, 1024), BF),
        V((2304, 256), F32), V((2, 640, 1024), BF), V((2, 512, 640), BF), V((512, 1152), F32),
        V((2048, 256), F32), V((2, 1024, 256), BF), V((2, 4, 2, 144, 256), BF),
        V((2, 1152, 256), BF), V((16, 1024), F32),
        dma((12, 18)), dma((12, 16)), dma((6,)), dma((6,)), dma((8,)), dma((9,)), dma((9,)),
        dma((16,)), dma((8,)),
    ]
    kept = pl.pallas_call(
        forward_kernel, out_shape=shapes, in_specs=[vmem] * 11, out_specs=[hbm] * len(shapes),
        scratch_shapes=scratch,
        compiler_params=pltpu.CompilerParams(
            collective_id=0, has_side_effects=True, vmem_limit_bytes=63 << 20),
        cost_estimate=pl.CostEstimate(flops=12 * 10**9, bytes_accessed=60 * 10**6, transcendentals=10**7),
        name="forward",
    )(x, cot, pa, po, pi, pu, small, bins, segr, segc, lanes)
    return x, lanes, kept


def nt(left, right):
    return lax.dot_general(left, right, (((1,), (1,)), ((), ())), preferred_element_type=F32)


def backward_kernel(
    par, lse, lanes, wa_h, wo_h, wi_h, wu_h, n1t_h, n2t_h, cot_h, qn_h, kn_h, vn_h, qt_h,
    kt_h, ot_h, mid_h, slope_h, act_h, go_h, mb_h, x_h,
    mixed_o, tokens_o, out_o, in_o, qkv_o, proj_o, sums_o, gi_h,
    WI, WU, ACT, IG, COT, COTT, N2T, inner, F1, F2, F3, F4, mix, yr, xr, x1, y2, zr, tile, held, kept,
    acck, accv, vyr, xra, zra, ysa, yra, go, xro, zro, yso, yro, sg, sgx, sgz, sgy, bsum,
    load, innersem, tilesem, heldsem, ysend, yrecv, xsend, xrecv, isend, irecv, zsend, zrecv,
    axs, axr, azs, azr, ays, ayr, oxs, oxr, ozs, ozr, oys, oyr, gsend, grecv, dsend, drecv,
    outsem, finsend, finrecv, finloc,
):
    h = Place()
    c, s, t, z, x = h.c, h.s, h.t, h.z, h.x
    rows = 512
    count = 1088.0
    own0 = pl.multiple_of(c * rows, rows)
    sib0 = pl.multiple_of((1 - c) * rows, rows)
    n_tiles = 9 - c

    def fetch(n, src, dst):
        copy = pltpu.make_async_copy(src, dst, load.at[n])
        copy.start()
        return copy

    def tile_of(i):
        return jnp.where(i < 4, 4 * h.tb + i, jnp.where(i < 8, 4 * t + i - 4, 8))

    def inner_copy(i):
        slot = lax.rem(i, 2)
        return pltpu.make_async_copy(
            slope_h.at[:, pl.ds(pl.multiple_of(256 * tile_of(i), 256), 256)],
            inner.at[pl.ds(pl.multiple_of(1024 * slot, 1024), 1024)], innersem.at[slot])

    inner_copy(0).start()
    first = [fetch(0, cot_h, COT), fetch(1, wu_h, WU)]
    second = [fetch(3, n2t_h, N2T), fetch(4, wi_h, WI), fetch(5, mid_h, F4), fetch(2, act_h, ACT)]
    h.greet()

    @pl.when(c == 1)
    def _():
        IG[:, 2048:2304] = jnp.zeros((1024, 256), BF)
    sg[...] = jnp.zeros_like(sg)

    def cols_of(k):
        return slice(256 * k, 256 * k + 256) if k < 4 else slice(1024, 1152)

    def theirs(k):
        return pl.ds(pl.multiple_of(1024 * h.tb + 256 * k if k < 4 else 2048 + 128 * h.tb, 128),
                     256 if k < 4 else 128)

    def ours(k):
        return pl.ds(pl.multiple_of(1024 * t + 256 * k if k < 4 else 2048 + 128 * t, 128),
                     256 if k < 4 else 128)

    def slot_at(zp):
        return lax.rem(z - zp + 3, 4)

    def only(k, step):
        if k < 4:
            step()
        else:
            pl.when(c == 0)(step)

    def oy(k):
        return remote(go_h.at[:, :, :, theirs(k)], yr.at[:, :, :, cols_of(k)],
                      ysend.at[0, k], yrecv.at[0, k], h.ydev)

    def ox(k):
        cols = cols_of(k)
        return remote(yr.at[:, h.xb, :, cols], xr.at[:, :, cols], xsend.at[k], xrecv.at[k], h.xdev)

    def z_copy(m, k, i, zp):
        cols = cols_of(k)
        src = (xr, y2)[m]
        return remote(src.at[zp, :, cols], zr.at[m, slot_at(zp), :, cols],
                      zsend.at[m, k, i], zrecv.at[m, k, slot_at(zp)], h.zdev(zp))

    def held_copy(k):
        return pltpu.make_async_copy(
            go_h.at[:, :, :, ours(k)], held.at[:, :, :, 0:256 if k < 4 else 128], heldsem.at[0])

    def OY(k):
        def step():
            cols = cols_of(k)
            width = cols.stop - cols.start
            oy(k).wait_recv()
            held_copy(k).wait()

            @pl.loop(0, 4)
            def _(zp):
                for xp in range(2):
                    yr[zp, xp, :, cols] = (
                        yr[zp, xp, :, cols].astype(F32) + held[zp, xp, :, 0:width].astype(F32)
                    ).astype(BF)
            ox(k).start()
        only(k, step)
        if k < 4:
            only(k + 1, lambda: held_copy(k + 1).start())

    def OX(k):
        def step():
            cols = cols_of(k)
            ox(k).wait_recv()

            @pl.loop(0, 4)
            def _(zp):
                xr[zp, :, cols] = (
                    xr[zp, :, cols].astype(F32) + yr[zp, x, :, cols].astype(F32)).astype(BF)
            for i, zp in enumerate(h.peers):
                z_copy(0, k, i, zp).start()
        only(k, step)

    def LZ(m, k):
        def step():
            cols = cols_of(k)
            for i in range(3):
                ref = zr.at[m, i, :, cols]
                remote(ref, ref, zsend.at[m, k, 0], zrecv.at[m, k, i], h.core).wait_recv()
            src = (xr, y2)[m]
            F4[144 * m:144 * m + 144, cols] = (
                (src[z, :, cols].astype(F32) + zr[m, 0, :, cols].astype(F32))
                + (zr[m, 1, :, cols].astype(F32) + zr[m, 2, :, cols].astype(F32)))
        only(k, step)

    def tile_cols(i):
        return pl.ds(pl.multiple_of(256 * tile_of(i), 256), 256)

    def ix(i):
        cols = tile_cols(i)
        return remote(gi_h.at[:, h.xb, :, cols], x1.at[:, :, cols],
                      isend.at[i], irecv.at[i], h.xdev)

    def iy(k):
        return remote(x1.at[:, :, theirs(k)], y2.at[:, :, cols_of(k)],
                      ysend.at[1, k], yrecv.at[1, k], h.ydev)

    def kept_copy(i):
        return pltpu.make_async_copy(gi_h.at[:, x, :, tile_cols(i)], kept, heldsem.at[1])

    def IX(i):
        def step():
            cols = tile_cols(i)
            ix(i).wait_recv()
            kept_copy(i).wait()

            @pl.loop(0, 4)
            def _(zp):
                x1[zp, :, cols] = (
                    x1[zp, :, cols].astype(F32) + kept[zp].astype(F32)).astype(BF)
            if i < 4:
                iy(i).start()
            if i == 8:
                iy(4).start()
        only(4 if i == 8 else 0, step)
        if i < 8:
            only(4 if i == 7 else 0, lambda: kept_copy(i + 1).start())

    def IY(k):
        def step():
            cols = cols_of(k)
            iy(k).wait_recv()

            @pl.loop(0, 4)
            def _(zp):
                y2[zp, :, cols] = (
                    y2[zp, :, cols].astype(F32) + x1[zp, :, ours(k)].astype(F32)).astype(BF)
            for i, zp in enumerate(h.peers):
                z_copy(1, k, i, zp).start()
        only(k, step)

    for k in range(5):
        only(k, lambda: oy(k).start())
    held_copy(0).start()

    for copy in first:
        copy.wait()

    def hidden(i):
        base = pl.multiple_of(1024 * lax.rem(i, 2), 1024)
        inner_copy(i).wait()

        @pl.when(i + 1 < n_tiles)
        def _():
            inner_copy(i + 1).start()
        cols = pl.ds(pl.multiple_of(256 * tile_of(i), 256), 256)
        bsum[...] = jnp.zeros_like(bsum)

        @pl.loop(0, 4)
        def _(q):
            at = pl.ds(pl.multiple_of(256 * q, 256), 256)
            v = inner[pl.ds(pl.multiple_of(base + 256 * q, 256), 256), :]
            low = (mm(COT[at, :], WU[:, cols]) * v).astype(BF)
            IG[at, cols] = low
            bsum[0:1, :] = bsum[0:1, :] + jnp.sum(low.astype(F32), axis=0, keepdims=True)

        @pl.when(i == 0)
        def _():
            second[0].wait()

        @pl.loop(0, 2)
        def _(half):
            got = mm(N2T[pl.ds(pl.multiple_of(576 * half, 576), 576), :], IG[:, cols])
            line = lax.broadcasted_iota(jnp.int32, (16, 256), 0) == 8
            for q in range(4):
                block = got[144 * q:144 * q + 144, :]
                zp, xp = 2 * half + q // 2, q % 2
                tile[zp, xp, 0:128] = block[0:128].astype(BF)
                tile[zp, xp, 128:144] = jnp.where(line, bsum[0:1, :], block[128:144]).astype(BF)
        copy = pltpu.make_async_copy(tile, gi_h.at[:, :, :, cols], tilesem.at[0])
        copy.start()
        copy.wait()

        ix(i).start()

    def units(low, high):
        @pl.loop(low, high)
        def _(i):
            hidden(i)

    units(0, 5)
    kept_copy(0).start()
    OY(0)
    IX(0)
    units(5, 9 - c)
    IX(1)
    IX(2)

    for copy in second[1:]:
        copy.wait()
    @pl.when(c == 1)
    def _():
        ACT[:, 2048:2304] = jnp.zeros((1024, 256), BF)


    def n2_copy(i):
        at = pl.ds(pl.multiple_of(384 * i, 128), 384)
        return remote(F3.at[:, at], F2.at[:, at], dsend.at[i], drecv.at[i], h.core)

    @pl.loop(0, 3)
    def _(i):
        at = pl.ds(pl.multiple_of(384 * i, 128), 384)
        F3[:, at] = nt(IG[pl.ds(sib0, rows), :], WI[at, :]).astype(BF)
        n2_copy(i).start()

    @pl.loop(0, 3)
    def _(i):
        at = pl.ds(pl.multiple_of(384 * i, 128), 384)
        F1[:, at] = nt(IG[pl.ds(own0, rows), :], WI[at, :])
    n2_sends = [n2_copy(i) for i in range(3)]
    OY(1)
    IX(3)

    wo_load = fetch(6, wo_h, WI.at[0:640, 0:1152])
    q_loads = [fetch(7, qn_h, IG.at[:, 0:640]), fetch(8, kn_h, IG.at[:, 640:1280]),
               fetch(9, vn_h, IG.at[:, 1280:1920]),
               fetch(11, n1t_h, N2T)]


    def mix_copy(i):
        at = pl.ds(pl.multiple_of(384 * i, 128), 384)
        return remote(WI.at[640:1152, at], mix.at[:, at], dsend.at[3 + i], drecv.at[3 + i], h.core)

    @pl.loop(0, 3)
    def _(i):
        at = pl.ds(pl.multiple_of(384 * i, 128), 384)
        WI[640:1152, at] = nt(ACT[pl.ds(sib0, rows), :], WU[at, :]).astype(BF)
        mix_copy(i).start()
    mix_sends = [mix_copy(i) for i in range(3)]

    mask = lanes[0:1, :]
    for copy in n2_sends:
        copy.wait_recv()

    @pl.loop(0, 4)
    def _(q):
        at = pl.ds(pl.multiple_of(128 * q, 128), 128)
        to = pl.ds(pl.multiple_of(own0 + 128 * q, 128), 128)
        grad = F1[at, :] + F2[at, :].astype(F32)
        v = F4[at, :]
        mean = jnp.sum(v, axis=1, keepdims=True) * (1.0 / count)
        spread = (v - mean) * mask
        rstd = lax.rsqrt(jnp.sum(spread * spread, axis=1, keepdims=True) * (1.0 / count) + EPS)
        hat = spread * rstd
        scaled = grad * par[1:2, :]
        grad_out = COT[to, :].astype(F32)
        got = grad_out + rstd * (
            scaled - jnp.sum(scaled, axis=1, keepdims=True) * (1.0 / count)
            - hat * (jnp.sum(scaled * hat, axis=1, keepdims=True) * (1.0 / count))) * mask
        low = got.astype(BF)
        F1[at, :] = got
        COT[to, :] = low
        sg[3:4, 0:1152] = sg[3:4, 0:1152] + jnp.sum(grad * hat, axis=0, keepdims=True)
        sg[4:5, 0:1152] = sg[4:5, 0:1152] + jnp.sum(grad, axis=0, keepdims=True)
        sg[5:6, 0:1152] = sg[5:6, 0:1152] + jnp.sum(grad_out, axis=0, keepdims=True)
        sg[6:7, 0:1152] = sg[6:7, 0:1152] + jnp.sum(low.astype(F32), axis=0, keepdims=True)

    bg_copy = remote(COT.at[pl.ds(own0, rows)], COT.at[pl.ds(own0, rows)], dsend.at[6], drecv.at[6], h.core)
    bg_copy.start()
    IX(4)

    for copy in n2_sends:
        copy.wait_send()
    for copy in mix_sends:
        copy.wait_recv()

    @pl.loop(0, 3)
    def _(i):
        at = pl.ds(pl.multiple_of(384 * i, 128), 384)
        got = nt(ACT[pl.ds(own0, rows), :], WU[at, :]) + mix[:, at].astype(F32)
        F3[:, at] = (F4[:, at] + got + par[7:8, at]).astype(BF)
    mix_out = pltpu.make_async_copy(F3, mixed_o, outsem.at[0])
    mix_out.start()
    t_loads = [fetch(12, qt_h, WU.at[0:640, 0:1024]), fetch(13, kt_h, WU.at[0:640, 1024:2048])]
    OY(2)
    OX(0)
    o_loads = [fetch(14, ot_h.at[0], ACT.at[0:640, 0:1024]), fetch(15, ot_h.at[1], ACT.at[0:640, 1024:2048])]

    wo_load.wait()
    bg_copy.wait_recv()
    bg_copy.wait_send()
    for copy in mix_sends:
        copy.wait_send()

    @pl.loop(0, 5)
    def _(pair):
        at = pl.ds(pl.multiple_of(128 * pair, 128), 128)
        got = nt(COT[...], WI[at, 0:1152]).astype(BF)
        WI[0:1024, pl.ds(pl.multiple_of(1280 + 128 * pair, 128), 128)] = got
        COTT[at, :] = got.T

    IX(5)

    for copy in o_loads:
        copy.wait()

    def proj(col, width, to):
        part = COT[:, col]
        inner[0:576, 0:width] = mm(ACT[0:576, 0:1024], part)
        inner[576:1088, 0:width] = mm(ACT[0:512, 1024:2048], part)
        for sp in range(8):
            block = jnp.concatenate(
                [inner[136 * sp:136 * sp + 136, 0:width], jnp.zeros((8, width), F32)], axis=0)
            go[sp // 2, sp % 2, :, to:to + width] = block.astype(BF)

    ocols = (slice(0, 512), slice(512, 640))

    def ox_copy(k):
        return remote(go.at[:, h.xb, :, ocols[k]], xro.at[:, :, ocols[k]], oxs.at[k], oxr.at[k], h.xdev)

    def oz_copy(k, i, zp):
        return remote(xro.at[zp, :, ocols[k]], zro.at[slot_at(zp), :, ocols[k]],
                      ozs.at[k, i], ozr.at[k, slot_at(zp)], h.zdev(zp))

    def oy_copy(k):
        return remote(yso.at[:, ocols[k]], yro.at[:, ocols[k]], oys.at[k], oyr.at[k], h.ydev)

    for q in range(2):
        proj(pl.ds(pl.multiple_of(512 * c + 256 * q, 256), 256), 256, 256 * q)
    ox_copy(0).start()

    @pl.when(c == 0)
    def _():
        proj(slice(1024, 1152), 128, 512)
        ox_copy(1).start()

    def o_after_x(k):
        ox_copy(k).wait_recv()

        @pl.loop(0, 4)
        def _(zp):
            xro[zp, :, ocols[k]] = (
                xro[zp, :, ocols[k]].astype(F32) + go[zp, x, :, ocols[k]].astype(F32)).astype(BF)
        for i, zp in enumerate(h.peers):
            oz_copy(k, i, zp).start()

    def o_after_z(k):
        for i in range(3):
            ref = zro.at[i, :, ocols[k]]
            remote(ref, ref, ozs.at[k, 0], ozr.at[k, i], h.core).wait_recv()
        cols = ocols[k]
        yso[:, cols] = (
            (xro[z, :, cols].astype(F32) + zro[0, :, cols].astype(F32))
            + (zro[1, :, cols].astype(F32) + zro[2, :, cols].astype(F32))).astype(BF)
        oy_copy(k).start()

    def o_after_y(k):
        oy_copy(k).wait_recv()
        F4[288:432, ocols[k]] = yso[:, ocols[k]].astype(F32) + yro[:, ocols[k]].astype(F32)

    def both(step, main, more):
        for k in main:
            step(k)

        @pl.when(c == 0)
        def _():
            for k in more:
                step(k)

    q_loads.append(fetch(10, mb_h, inner))
    for copy in q_loads + t_loads:
        copy.wait()
    ACT[:, 1536:1920] = jnp.zeros((1024, 384), BF)
    WI[512:640, 0:1024] = jnp.zeros((128, 1024), BF)

    def attend(head):
        pair = head // 2
        parity = lax.rem(head, 2)
        both_heads = pl.ds(pl.multiple_of(pair * 128, 128), 128)
        feat = pl.ds(pl.multiple_of(head * 64, 64), 64)
        on_rows = lax.broadcasted_iota(jnp.int32, (128, 256), 0) // 64 == parity
        on_lanes = lax.broadcasted_iota(jnp.int32, (256, 128), 1) // 64 == parity
        zero = jnp.zeros((), BF)
        qcol = both_heads
        kcol = pl.ds(pl.multiple_of(640 + pair * 128, 128), 128)
        vcol = pl.ds(pl.multiple_of(1280 + pair * 128, 128), 128)

        @pl.when(parity == 0)
        def _():
            acck[...] = jnp.zeros_like(acck)
            accv[...] = jnp.zeros_like(accv)
        top = 0
        for b in range(4):
            start = max(0, b - 2)
            width = (b + 1 - start) * 256
            keys = slice(start * 256, start * 256 + width)
            cols = slice(b * 256, b * 256 + 256)
            scores = mm(IG[keys, kcol], jnp.where(on_rows, WU[both_heads, cols], zero))
            probs = jnp.exp(scores + inner[top:top + width, :] - lse[pl.ds(head, 1), cols])
            top += width
            grads = mm(IG[keys, vcol], jnp.where(on_rows, COTT[both_heads, cols], zero))
            terms = jnp.sum(probs * grads, axis=0, keepdims=True)
            sgrad = (probs * (grads - terms)).astype(BF)
            accv[keys, :] = accv[keys, :] + mm(
                probs.astype(BF), jnp.where(on_lanes, WI[cols, vcol], zero))
            acck[keys, :] = acck[keys, :] + mm(
                sgrad, jnp.where(on_lanes, IG[cols, qcol], zero))
            WI[feat, cols] = (
                mm(WU[feat, 1024 + start * 256:1024 + start * 256 + width], sgrad) * 0.125
            ).astype(BF)

        @pl.when((parity == 1) | (head == 8 - c))
        def _():
            kto = pl.ds(pl.multiple_of(jnp.where(pair < 4, 512 + 128 * pair, 1664), 128), 128)
            vto = pl.ds(pl.multiple_of(jnp.where(pair < 4, 1024 + 128 * pair, 1792), 128), 128)
            ACT[:, kto] = acck[...].astype(BF)
            ACT[:, vto] = accv[...].astype(BF)

    def heads(low, high):
        @pl.loop(low, high)
        def _(head):
            attend(head)

    IX(6)
    heads(0, 2)
    OY(3)
    IX(7)
    heads(2, 4)
    OY(4)
    IX(8)
    IY(0)
    heads(4, 6)
    IY(1)
    LZ(0, 0)
    OX(1)
    heads(6, 9 - c)
    IY(2)

    @pl.loop(0, 4)
    def _(pair):
        at = pl.ds(pl.multiple_of(128 * pair, 128), 128)
        ACT[:, at] = WI[at, 0:1024].T

    @pl.when(c == 0)
    def _():
        ACT[:, 1536:1664] = WI[512:640, 0:1024].T
    wa_load = fetch(16, wa_h, WI.at[:, 0:1920])
    x_load = fetch(17, x_h, COT.at[0:512])

    acols = (slice(0, 512), slice(512, 640))

    def qcols(k):
        return slice(0, 512) if k == 0 else slice(1536, 1664)

    def vcols(k, tp):
        start = 512 + 512 * tp if k == 0 else 1664 + 128 * tp
        return pl.ds(pl.multiple_of(start, 128), 512 if k == 0 else 128)

    def weights(start, width):
        @pl.loop(0, 2)
        def _(half):
            at = pl.ds(pl.multiple_of(576 * half, 576), 576)
            for col in range(0, width, 256):
                part = pl.ds(pl.multiple_of(start + col, 128), min(256, width))
                WU[at, part] = mm(N2T[at, :], ACT[:, part]).astype(BF)

    def vy(k):
        return remote(WU.at[:, vcols(k, h.tb)], vyr.at[:, acols[k]], ays.at[k], ayr.at[k], h.ydev)

    def ax(m, k, i, zp):
        at = rows_of(2 * zp + h.xb)
        src = WU.at[at, qcols(k)] if m == 0 else vyr.at[at, acols[k]]
        return remote(src, xra.at[m, zp, :, acols[k]], axs.at[m, k, i], axr.at[m, k, zp], h.xdev)

    def az(m, k, i, zp):
        return remote(xra.at[m, zp, :, acols[k]], zra.at[m, slot_at(zp), :, acols[k]],
                      azs.at[m, k, i], azr.at[m, k, slot_at(zp)], h.zdev(zp))

    def ay(m, k):
        return remote(ysa.at[m, :, acols[k]], yra.at[m, :, acols[k]],
                      ays.at[2 + 2 * m + k], ayr.at[2 + 2 * m + k], h.ydev)

    def VY(k):
        vy(k).wait_recv()
        cols = acols[k]

        @pl.loop(0, 8)
        def _(sp):
            at = rows_of(sp)
            vyr[at, cols] = (
                vyr[at, cols].astype(F32) + WU[at, vcols(k, t)].astype(F32)).astype(BF)
        for i, zp in enumerate(h.peers + [z]):
            ax(1, k, i, zp).start()

    def AX(m, k):
        cols = acols[k]
        for i, zp in enumerate(h.peers + [z]):
            ref = xra.at[m, zp, :, cols]
            remote(ref, ref, axs.at[m, k, 0], axr.at[m, k, zp], h.core).wait_recv()
            at = rows_of(2 * zp + x)
            mine = WU[at, qcols(k)] if m == 0 else vyr[at, cols]
            xra[m, zp, :, cols] = (
                xra[m, zp, :, cols].astype(F32) + mine.astype(F32)).astype(BF)
            if i < 3:
                az(m, k, i, zp).start()

    def AZ(m, k):
        cols = acols[k]
        for i in range(3):
            ref = zra.at[m, i, :, cols]
            remote(ref, ref, azs.at[m, k, 0], azr.at[m, k, i], h.core).wait_recv()
        ysa[m, :, cols] = (
            (xra[m, z, :, cols].astype(F32) + zra[m, 0, :, cols].astype(F32))
            + (zra[m, 1, :, cols].astype(F32) + zra[m, 2, :, cols].astype(F32))).astype(BF)
        ay(m, k).start()

    def place(block, start, width, value):
        for n in range(0, width, 256):
            at = pl.ds(pl.multiple_of(144 * (block + n // 256), 16), 144)
            size = min(256, width)
            inner[at, start:start + size] = value[:, n:n + size]

    def AY(m, k):
        ay(m, k).wait_recv()
        cols = acols[k]
        width = cols.stop - cols.start
        mine, other = ysa[m, :, cols].astype(F32), yra[m, :, cols].astype(F32)
        if m == 0:
            place(0 if k == 0 else 6, 0, width, mine + other)
        elif k == 0:
            place(2 + 2 * t, 0, width, mine)
            place(2 + 2 * h.tb, 0, width, other)
        else:
            inner[864:1008, 128:256] = jnp.where(t == 0, mine, other)
            inner[1008:1152, 0:128] = jnp.where(t == 0, other, mine)

    def pair(step, *args):
        step(*args, 0)

        @pl.when(c == 0)
        def _():
            step(*args, 1)

    weights(512 + 512 * h.tb, 512)
    vy(0).start()

    @pl.when(c == 0)
    def _():
        weights(1664 + 128 * h.tb, 128)
        vy(1).start()
    weights(512 + 512 * t, 512)
    pl.when(c == 0)(lambda: weights(1664 + 128 * t, 128))
    weights(0, 512)
    for i, zp in enumerate(h.peers + [z]):
        ax(0, 0, i, zp).start()

    @pl.when(c == 0)
    def _():
        weights(1536, 128)
        for i, zp in enumerate(h.peers + [z]):
            ax(0, 1, i, zp).start()
    IY(3)
    IY(4)
    OX(2)
    both(o_after_x, (0,), (1,))

    mix_out.wait()
    wa_load.wait()

    def n1_copy(i):
        at = pl.ds(pl.multiple_of(384 * i, 128), 384)
        return remote(F3.at[:, at], F2.at[:, at], dsend.at[7 + i], drecv.at[7 + i], h.core)

    @pl.loop(0, 3)
    def _(i):
        at = pl.ds(pl.multiple_of(384 * i, 128), 384)
        F3[:, at] = nt(ACT[pl.ds(sib0, rows), 0:1920], WI[at, 0:1920]).astype(BF)
        n1_copy(i).start()

    @pl.loop(0, 4)
    def _(i):
        at = pl.ds(pl.multiple_of(256 * i, 256), 256)
        inner[pl.ds(pl.multiple_of(512 * i, 512), 512), :] = nt(
            ACT[pl.ds(own0, rows), 0:1920], WI[at, 0:1920])
    part = nt(ACT[pl.ds(own0, rows), 0:1920], WI[1024:1152, 0:1920])
    inner[2048:2304, 0:128] = part[0:256]
    inner[2048:2304, 128:256] = part[256:512]
    n1_sends = [n1_copy(i) for i in range(3)]

    @pl.loop(0, 15)
    def _(i):
        at = pl.ds(pl.multiple_of(128 * i, 128), 128)
        sg[0:1, at] = jnp.sum(ACT[:, at].astype(F32), axis=0, keepdims=True)
    OX(3)
    OX(4)
    LZ(0, 1)
    for n in range(3):
        LZ(1, n)
    both(o_after_z, (0,), (1,))
    pair(VY)
    x_load.wait()
    for copy in n1_sends:
        copy.wait_recv()
    tok_outs = []
    for i in range(4):
        at = slice(128 * i, 128 * i + 128)
        last = slice(2048 + 128 * (i % 2), 2176 + 128 * (i % 2))
        part = jnp.concatenate(
            [inner[512 * j + 128 * i:512 * j + 128 * i + 128, :] for j in range(4)]
            + [inner[last, 128 * (i // 2):128 * (i // 2) + 128]], axis=1)
        grad = part + F2[at, :].astype(F32)
        v = COT[at, :].astype(F32)
        mean = jnp.sum(v, axis=1, keepdims=True) * (1.0 / count)
        spread = (v - mean) * mask
        rstd = lax.rsqrt(jnp.sum(spread * spread, axis=1, keepdims=True) * (1.0 / count) + EPS)
        hat = spread * rstd
        scaled = grad * par[0:1, :]
        F1[at, :] = F1[at, :] + rstd * (
            scaled - jnp.sum(scaled, axis=1, keepdims=True) * (1.0 / count)
            - hat * (jnp.sum(scaled * hat, axis=1, keepdims=True) * (1.0 / count))) * mask
        sg[1:2, 0:1152] = sg[1:2, 0:1152] + jnp.sum(grad * hat, axis=0, keepdims=True)
        sg[2:3, 0:1152] = sg[2:3, 0:1152] + jnp.sum(grad, axis=0, keepdims=True)
        copy = pltpu.make_async_copy(F1.at[at], tokens_o.at[at], outsem.at[2 + i])
        copy.start()
        tok_outs.append(copy)

    sgx_copy = remote(sg, sgx, gsend.at[0], grecv.at[0], h.xdev)
    sgx_copy.start()
    pair(AX, 0)
    sgx_copy.wait()
    sgx[...] = sgx[...] + sg[...]

    def sgz_copy(i, zp):
        return remote(sgx, sgz.at[slot_at(zp)], gsend.at[1 + i], grecv.at[1 + slot_at(zp)], h.zdev(zp))

    for i, zp in enumerate(h.peers):
        sgz_copy(i, zp).start()
    both(o_after_y, (0,), (1,))
    for n in range(2, 5):
        LZ(0, n)
    for n in range(3, 5):
        LZ(1, n)

    finals = []

    def finish(n, src, out):
        local = pltpu.make_async_copy(src, out.at[c], finloc.at[n])
        local.start()
        over = remote(src, out.at[c], finsend.at[n], finrecv.at[n], h.core)
        over.start()
        finals.append((local, over))

    finish(0, F4.at[288:432, 0:640], proj_o)
    finish(1, F4.at[0:144], out_o)
    finish(2, F4.at[144:288], in_o)
    pair(AX, 1)
    pair(AZ, 0)
    for i in range(3):
        remote(sgz.at[i], sgz.at[i], gsend.at[1], grecv.at[1 + i], h.core).wait_recv()
    for i, zp in enumerate(h.peers):
        sgz_copy(i, zp).wait_send()
    sg[...] = (sgx[...] + sgz[0]) + (sgz[1] + sgz[2])
    sgy_copy = remote(sg, sgy, gsend.at[4], grecv.at[4], h.ydev)
    sgy_copy.start()
    pair(AZ, 1)
    sgy_copy.wait()
    sgx[...] = sg[...] + sgy[...]
    finish(3, sgx, sums_o)
    pair(AY, 0)
    pair(AY, 1)
    finish(4, inner.at[0:1152], qkv_o)

    for copy in tok_outs:
        copy.wait()
    for copy in n1_sends:
        copy.wait_send()

    def drain(k):
        oy(k).wait_send()
        ox(k).wait_send()
        iy(k).wait_send()
        for m in range(2):
            for i, zp in enumerate(h.peers):
                z_copy(m, k, i, zp).wait_send()

    for n in range(5):
        only(n, lambda: drain(n))
    for n in range(9):
        only(4 if n == 8 else 0, lambda: ix(n).wait_send())

    def o_drain(k):
        ox_copy(k).wait_send()
        oy_copy(k).wait_send()
        for i, zp in enumerate(h.peers):
            oz_copy(k, i, zp).wait_send()

    both(o_drain, (0,), (1,))

    def a_drain(k):
        vy(k).wait_send()
        for m in range(2):
            ay(m, k).wait_send()
            for i, zp in enumerate(h.peers + [z]):
                ax(m, k, i, zp).wait_send()
                if i < 3:
                    az(m, k, i, zp).wait_send()

    pair(a_drain)
    for local, over in finals:
        local.wait()
        over.wait()


def run_backward(x, lanes, saved):
    (wa, wo, wi, wu, n1t, n2t, cot, qn, kn, vn, qt, kt, ot, lse, mid, slope, act, go, par, mb) = saved
    hbm = pl.BlockSpec(memory_space=pltpu.HBM)
    vmem = pl.BlockSpec(memory_space=pltpu.VMEM)
    sds = jax.ShapeDtypeStruct
    V = pltpu.VMEM
    dma = pltpu.SemaphoreType.DMA
    shapes = [
        sds((512, 1152), BF), sds((512, 1152), F32), sds((2, 144, 1152), F32),
        sds((2, 144, 1152), F32), sds((2, 1152, 256), F32), sds((2, 144, 640), F32),
        sds((2, 8, 1920), F32), sds((4, 2, 144, 2304), BF),
    ]
    scratch = [
        V((1152, 2304), BF), V((1152, 2304), BF), V((1024, 2304), BF), V((1024, 2304), BF),
        V((1024, 1152), BF), V((640, 1024), BF), V((1152, 1024), BF), V((2304, 256), F32),
        V((512, 1152), F32), V((512, 1152), BF), V((512, 1152), BF), V((512, 1152), F32),
        V((512, 1152), BF), V((4, 2, 144, 1152), BF), V((4, 144, 1152), BF), V((4, 144, 2304), BF), V((4, 144, 1152), BF),
        V((2, 3, 144, 1152), BF), V((4, 2, 144, 256), BF), V((4, 2, 144, 256), BF), V((4, 144, 256), BF),
        V((1024, 128), F32), V((1024, 128), F32),
        V((1152, 640), BF), V((2, 4, 144, 640), BF), V((2, 3, 144, 640), BF), V((2, 144, 640), BF), V((2, 144, 640), BF),
        V((4, 2, 144, 640), BF), V((4, 144, 640), BF), V((3, 144, 640), BF), V((144, 640), BF),
        V((144, 640), BF),
        V((8, 1920), F32), V((8, 1920), F32), V((3, 8, 1920), F32), V((8, 1920), F32), V((8, 256), F32),
        dma((18,)), dma((2,)), dma((1,)), dma((2,)),
        dma((2, 5)), dma((2, 5)), dma((5,)), dma((5,)), dma((9,)), dma((9,)), dma((2, 5, 3)), dma((2, 5, 3)),
        dma((2, 2, 4)), dma((2, 2, 4)), dma((2, 2, 3)), dma((2, 2, 3)), dma((6,)), dma((6,)),
        dma((2,)), dma((2,)), dma((2, 3)), dma((2, 3)), dma((2,)), dma((2,)),
        dma((5,)), dma((5,)), dma((10,)), dma((10,)), dma((6,)), dma((5,)), dma((5,)), dma((5,)),
    ]
    return pl.pallas_call(
        backward_kernel, out_shape=shapes, in_specs=[vmem] * 3 + [hbm] * 19,
        out_specs=[hbm] * len(shapes), scratch_shapes=scratch,
        compiler_params=pltpu.CompilerParams(
            collective_id=1, has_side_effects=True, vmem_limit_bytes=65300 << 10),
        cost_estimate=pl.CostEstimate(flops=40 * 10**9, bytes_accessed=80 * 10**6, transcendentals=2 * 10**7),
        name="backward",
    )(par, lse, lanes, wa, wo, wi, wu, n1t, n2t, cot, qn, kn, vn, qt, kt, ot, mid, slope, act, go, mb, x)


def join_features(matrix):
    rows = matrix.shape[0]
    return matrix.reshape(rows, 8, BR)[:, :, :136].reshape(rows, 1088)


def join_heads(pair, col):
    start, more = {"q": (0, 1536), "k": (512, 1664), "v": (1024, 1792)}[col]
    return [pair[0][:, start:start + 512], pair[0][:, more:more + 64], pair[1][:, start:start + 512]]


def fused(tokens, segment_ids, norm_gains, norm_shifts, biases, w_qkv, w_o, w_in, b_in, w_out,
          cotangent):
    c = lax.axis_index("ctx")
    s = lax.axis_index("shard")
    x, lanes, kept = run_forward(tokens, segment_ids, norm_gains, norm_shifts, biases, w_qkv, w_o,
                                 w_in, b_in, w_out, cotangent)
    mixed, tokens_grad, out_g, in_g, qkv_g, proj_g, sums, _ = run_backward(x, lanes, kept)
    half = lambda blocks: lax.dynamic_slice_in_dim(blocks, c * 68, 68, axis=1)
    mine = half(qkv_g.reshape(16, 144, 256)).reshape(2, 8, 68, 256)
    mine = jnp.concatenate([mine[:, n] for n in range(8)], axis=2)[:, :, :1920]
    w_qkv_grad = jnp.concatenate(
        join_heads(mine, "q") + join_heads(mine, "k") + join_heads(mine, "v"), axis=1)
    mine = half(proj_g)
    w_o_grad = join_features(jnp.concatenate(
        [mine[0, :, :512], mine[1, :, :512], mine[0, :, 512:]], axis=1))
    mine = half(in_g)
    w_in_grad = jnp.concatenate([mine[0], mine[1][:, :1024]], axis=1)
    mine = half(out_g)
    w_out_grad = jnp.concatenate([mine[0], mine[1][:, :1024]], axis=1).T
    line = jnp.concatenate([in_g[0, 136:137], in_g[1, 136:137, :1024]], axis=1)
    b_in_grad = lax.dynamic_slice_in_dim(line, (2 * s + c) * 136, 136, axis=1)
    rows = sums[0] + sums[1]
    features = lax.dynamic_slice_in_dim(rows, s * BR + c * 68, 68, axis=1)
    first = sums[:, 0:1]
    heads = jnp.concatenate([jnp.concatenate(join_heads(first, n), axis=1) for n in ("q", "v")], axis=0)
    heads = lax.dynamic_slice_in_dim(heads, (2 * s + c) * 68, 68, axis=1)
    gains = jnp.concatenate([features[1:2], features[3:4]], axis=0)
    shifts = jnp.concatenate([features[2:3], features[4:5]], axis=0)
    biases_grad = jnp.concatenate([heads, features[6:7], features[5:6]], axis=0)
    return (join_features(mixed)[None], join_features(tokens_grad)[None], gains, shifts, biases_grad,
            w_qkv_grad, w_o_grad, w_in_grad, b_in_grad, w_out_grad)


def per_device(
    tokens, segment_ids, norm_gains, norm_shifts, biases, w_qkv, w_o, w_in, b_in, w_out, cotangent
):
    rows_here = tokens.shape[1]
    score_scale = HEAD_DIM ** (-0.5)
    gains_full, shifts_full, bias_full, qkv_full, proj_full, up_full, down_full = (
        lax.all_gather(norm_gains, "shard", axis=1, tiled=True),
        lax.all_gather(norm_shifts, "shard", axis=1, tiled=True),
        lax.all_gather(biases, "shard", axis=1, tiled=True),
        lax.all_gather(w_qkv, "shard", axis=0, tiled=True),
        lax.all_gather(w_o, "shard", axis=0, tiled=True),
        lax.all_gather(w_in, "shard", axis=0, tiled=True),
        lax.all_gather(w_out, "shard", axis=1, tiled=True),
    )
    gains_full = gains_full.astype(jnp.float32)
    shifts_full = shifts_full.astype(jnp.float32)
    bias_full = bias_full.astype(jnp.float32)
    hidden = tokens[0].astype(jnp.float32)
    normed, norm_back_one = jax.vjp(layer_norm, hidden, gains_full[0], shifts_full[0])
    normed_low = normed.astype(jnp.bfloat16)
    projected = jnp.dot(normed_low, qkv_full, preferred_element_type=jnp.float32)
    queries = (projected[:, :D] + bias_full[0]).astype(jnp.bfloat16)
    key_rows = projected[:, D : 2 * D].astype(jnp.bfloat16)
    value_rows = (projected[:, 2 * D :] + bias_full[1]).astype(jnp.bfloat16)
    all_keys, all_values = (
        lax.all_gather(key_rows, "ctx", axis=0, tiled=True),
        lax.all_gather(value_rows, "ctx", axis=0, tiled=True),
    )
    seq_length = all_keys.shape[0]
    offset = lax.axis_index("ctx") * rows_here
    key_segments = segment_ids[0]
    query_segments = lax.dynamic_slice_in_dim(key_segments, offset, rows_here)
    query_position = offset + lax.iota(jnp.int32, rows_here)
    key_position = lax.iota(jnp.int32, seq_length)
    allowed = (key_position[None, :] <= query_position[:, None]) & (
        key_segments[None, :] == query_segments[:, None]
    )
    query_heads = split_heads(queries)
    key_heads = split_heads(all_keys)
    value_heads = split_heads(all_values)

    def head_scores(query_head, key_head):
        scores = (
            jnp.einsum("qd,kd->qk", query_head, key_head, preferred_element_type=jnp.float32)
            * score_scale
        )
        return jnp.where(allowed, scores, -1e30)

    def head_forward(operands):
        query_head, key_head, value_head = operands
        masked = head_scores(query_head, key_head)
        highest = jnp.max(masked, axis=1, keepdims=True)
        weights = jnp.exp(masked - highest)
        summed = jnp.sum(weights, axis=1, keepdims=True)
        probabilities = (weights / summed).astype(jnp.bfloat16)
        result = jnp.dot(probabilities, value_head, preferred_element_type=jnp.float32)
        return (result, (highest + jnp.log(summed))[:, 0])

    head_out, log_total = lax.map(head_forward, (query_heads, key_heads, value_heads))
    attended = merge_heads(head_out).astype(jnp.bfloat16)
    middle = (
        hidden + jnp.dot(attended, proj_full, preferred_element_type=jnp.float32) + bias_full[2]
    )
    normed_two, norm_back_two = jax.vjp(layer_norm, middle, gains_full[1], shifts_full[1])
    normed_two_low = normed_two.astype(jnp.bfloat16)
    mlp_inputs = lax.all_gather(normed_two_low, "tp", axis=0, tiled=True)
    inner_values = jnp.dot(mlp_inputs, up_full, preferred_element_type=jnp.float32) + b_in.astype(
        jnp.float32
    )
    active, gelu_back = jax.vjp(gelu_tanh, inner_values)
    active_low = active.astype(jnp.bfloat16)
    mixed_rows = (
        middle
        + lax.psum_scatter(
            jnp.dot(active_low, down_full, preferred_element_type=jnp.float32).astype(jnp.bfloat16),
            "tp",
            scatter_dimension=0,
            tiled=True,
        ).astype(jnp.float32)
        + bias_full[3]
    )
    mixed_out = mixed_rows.astype(jnp.bfloat16)[None]
    grad_low = cotangent[0]
    grad_out = grad_low.astype(jnp.float32)
    grad_rows = lax.all_gather(grad_low, "tp", axis=0, tiled=True)
    down_grad = contract_rows(active_low, grad_rows)
    out_bias_grad = jnp.sum(grad_out, axis=0)
    active_grad = contract_cols(grad_rows, down_full)
    inner_grad = gelu_back(active_grad)[0].astype(jnp.bfloat16)
    up_grad = contract_rows(mlp_inputs, inner_grad)
    in_bias_grad = jnp.sum(inner_grad.astype(jnp.float32), axis=0)
    normed_two_grad = lax.psum_scatter(
        contract_cols(inner_grad, up_full), "tp", scatter_dimension=0, tiled=True
    )
    middle_part, gain_two_grad, shift_two_grad = norm_back_two(normed_two_grad)
    middle_grad = grad_out + middle_part
    branch_grad = middle_grad.astype(jnp.bfloat16)
    proj_grad = contract_rows(attended, branch_grad)
    attn_bias_grad = jnp.sum(branch_grad.astype(jnp.float32), axis=0)
    attended_grad = split_heads(contract_cols(branch_grad, proj_full).astype(jnp.bfloat16))

    def head_backward(operands):
        query_head, key_head, value_head, grad_head, log_head = operands
        masked = head_scores(query_head, key_head)
        probabilities = jnp.exp(masked - log_head[:, None])
        probs_grad = jnp.einsum(
            "qd,kd->qk", grad_head, value_head, preferred_element_type=jnp.float32
        )
        row_terms = jnp.sum(probabilities * probs_grad, axis=1, keepdims=True)
        scores_grad = (probabilities * (probs_grad - row_terms)).astype(jnp.bfloat16)
        query_grad = (
            jnp.dot(scores_grad, key_head, preferred_element_type=jnp.float32) * score_scale
        )
        key_grad = (
            jnp.einsum("qk,qd->kd", scores_grad, query_head, preferred_element_type=jnp.float32)
            * score_scale
        )
        value_grad = jnp.einsum(
            "qk,qd->kd",
            probabilities.astype(jnp.bfloat16),
            grad_head,
            preferred_element_type=jnp.float32,
        )
        return (query_grad, key_grad, value_grad)

    query_grads, key_grads, value_grads = lax.map(
        head_backward, (query_heads, key_heads, value_heads, attended_grad, log_total)
    )
    key_summed, value_summed = (
        lax.psum_scatter(
            merge_heads(key_grads).astype(jnp.bfloat16), "ctx", scatter_dimension=0, tiled=True
        ).astype(jnp.float32),
        lax.psum_scatter(
            merge_heads(value_grads).astype(jnp.bfloat16), "ctx", scatter_dimension=0, tiled=True
        ).astype(jnp.float32),
    )
    query_low = merge_heads(query_grads).astype(jnp.bfloat16)
    value_low = value_summed.astype(jnp.bfloat16)
    qkv_grad = jnp.concatenate([query_low, key_summed.astype(jnp.bfloat16), value_low], axis=1)
    qkv_weight_grad = contract_rows(normed_low, qkv_grad)
    query_bias_grad = jnp.sum(query_low.astype(jnp.float32), axis=0)
    value_bias_grad = jnp.sum(value_low.astype(jnp.float32), axis=0)
    normed_grad = contract_cols(qkv_grad, qkv_full)
    hidden_part, gain_one_grad, shift_one_grad = norm_back_one(normed_grad)
    tokens_grad = (middle_grad + hidden_part)[None]
    gains_grad = jnp.stack([gain_one_grad, gain_two_grad])
    shifts_grad = jnp.stack([shift_one_grad, shift_two_grad])
    biases_grad = jnp.stack([query_bias_grad, value_bias_grad, attn_bias_grad, out_bias_grad])
    gains_grad, shifts_grad, biases_grad, qkv_weight_grad, proj_grad = lax.psum(
        (gains_grad, shifts_grad, biases_grad, qkv_weight_grad, proj_grad), "tp"
    )
    (
        gains_grad,
        shifts_grad,
        biases_grad,
        qkv_weight_grad,
        proj_grad,
        up_grad,
        in_bias_grad,
        down_grad,
    ) = (
        lax.psum_scatter(gains_grad, ("shard", "ctx"), scatter_dimension=1, tiled=True),
        lax.psum_scatter(shifts_grad, ("shard", "ctx"), scatter_dimension=1, tiled=True),
        lax.psum_scatter(biases_grad, ("shard", "ctx"), scatter_dimension=1, tiled=True),
        lax.psum_scatter(qkv_weight_grad, ("shard", "ctx"), scatter_dimension=0, tiled=True),
        lax.psum_scatter(proj_grad, ("shard", "ctx"), scatter_dimension=0, tiled=True),
        lax.psum_scatter(up_grad, ("shard", "ctx"), scatter_dimension=0, tiled=True),
        lax.psum_scatter(in_bias_grad, ("shard", "ctx"), scatter_dimension=0, tiled=True),
        lax.psum_scatter(down_grad, ("shard", "ctx"), scatter_dimension=1, tiled=True),
    )
    return (
        mixed_out,
        tokens_grad,
        gains_grad,
        shifts_grad,
        biases_grad,
        qkv_weight_grad,
        proj_grad,
        up_grad,
        in_bias_grad[None],
        down_grad,
    )


def solution(mesh):
    in_specs = (
        P(("shard", "tp"), "ctx", None),
        P(("shard", "tp"), None),
        P(None, "shard"),
        P(None, "shard"),
        P(None, "shard"),
        P("shard", None),
        P("shard", None),
        P("shard", "tp"),
        P("tp"),
        P("tp", "shard"),
        P(("shard", "tp"), "ctx", None),
    )
    out_specs = (
        P(("shard", "tp"), "ctx", None),
        P(("shard", "tp"), "ctx", None),
        P(None, ("shard", "ctx")),
        P(None, ("shard", "ctx")),
        P(None, ("shard", "ctx")),
        P(("shard", "ctx"), None),
        P(("shard", "ctx"), None),
        P(("shard", "ctx"), "tp"),
        P("tp", ("shard", "ctx")),
        P("tp", ("shard", "ctx")),
    )
    fits = dict(mesh.shape) == {"shard": 8, "ctx": 2, "tp": 2}
    return jax.shard_map(
        fused if fits else per_device, mesh=mesh, in_specs=in_specs, out_specs=out_specs, check_vma=False
    )
```

```python
import math

import jax
import jax.numpy as jnp
from jax import lax
from jax.experimental import pallas as pl
from jax.experimental.pallas import tpu as pltpu
from jax.sharding import PartitionSpec as P

D = 1088
HEADS = 17
HEAD_DIM = 64


def layer_norm(values, gain_row, shift_row):
    center = jnp.mean(values, axis=-1, keepdims=True)
    spread = values - center
    variance = jnp.mean(spread * spread, axis=-1, keepdims=True)
    return spread * lax.rsqrt(variance + 1e-05) * gain_row + shift_row


def gelu_tanh(values):
    return (
        0.5
        * values
        * (
            1.0
            + jnp.tanh(math.sqrt(2.0 / math.pi) * (values + 0.044715 * values * values * values))
        )
    )


def contract_rows(left_side, right_side):
    return lax.dot_general(
        left_side, right_side, (((0,), (0,)), ((), ())), preferred_element_type=jnp.float32
    )


def contract_cols(left_side, right_side):
    return lax.dot_general(
        left_side, right_side, (((1,), (1,)), ((), ())), preferred_element_type=jnp.float32
    )


def split_heads(matrix):
    return matrix.reshape(matrix.shape[0], HEADS, HEAD_DIM).transpose(1, 0, 2)


def merge_heads(stacked):
    return stacked.transpose(1, 0, 2).reshape(stacked.shape[1], D)


BF = jnp.bfloat16
F32 = jnp.float32
MESH = pl.DeviceIdType.MESH
EPS = 1e-05
BR = 144
UNIT = 128


def mm(left, right):
    return jnp.dot(left, right, preferred_element_type=F32)


def remote(src, dst, send, recv, device):
    return pltpu.make_async_remote_copy(
        src_ref=src, dst_ref=dst, send_sem=send, recv_sem=recv,
        device_id=device, device_id_type=MESH,
    )


class Place:
    def __init__(self):
        self.s = lax.axis_index("shard")
        self.c = lax.axis_index("ctx")
        self.t = lax.axis_index("tp")
        self.z = self.s // 2
        self.x = self.s - 2 * self.z
        self.xb = 1 - self.x
        self.tb = 1 - self.t
        z = self.z
        self.peers = [
            z + 1 - 2 * lax.rem(z, 2),
            jnp.where(z < 2, 2, 1),
            jnp.where(z < 2, 3, 0),
        ]
        self.core = (self.s, 1 - self.c, self.t)
        self.xdev = (2 * z + self.xb, self.c, self.t)
        self.ydev = (self.s, self.c, self.tb)

    def zdev(self, zp):
        return (2 * zp + self.x, self.c, self.t)

    def greet(self):
        barrier = pltpu.get_barrier_semaphore()
        devices = [self.core, self.xdev, self.ydev] + [self.zdev(p) for p in self.peers]
        for device in devices:
            pl.semaphore_signal(barrier, inc=1, device_id=device, device_id_type=MESH)
        pl.semaphore_wait(barrier, len(devices))


def rows_of(s):
    return pl.ds(pl.multiple_of(s * BR, 16), BR)


class Gather:
    def __init__(self, here, number, own, loc, route, send, recv):
        self.h, self.p, self.own, self.loc, self.route = here, number, own, loc, route
        self.send, self.recv = send, recv
        self.two, self.three = (
            (here.ydev, here.xdev) if route == "zyx" else (here.xdev, here.ydev))
        if route == "zx":
            self.three = None

    def copy(self, src, s, t, device, i):
        return remote(src, self.loc(s, t), self.send.at[self.p, i],
                      self.recv.at[self.p, s * 2 + t], device)

    def take(self, s, t):
        ref = self.loc(s, t)
        self.copy(ref, s, t, self.h.core, 0).wait_recv()

    def along(self, k):
        h = self.h
        to = h.z + jnp.where(h.peers[k] < h.z, 1, -1)
        return (to >= 0) & (to <= 3), h.zdev(jnp.clip(to, 0, 3))

    def own_z(self):
        h = self.h
        pl.when(h.z < 3)(self.copy(self.own, h.s, h.t, h.zdev(jnp.minimum(h.z + 1, 3)), 0).start)
        pl.when(h.z > 0)(self.copy(self.own, h.s, h.t, h.zdev(jnp.maximum(h.z - 1, 0)), 1).start)

    def own_two(self):
        self.copy(self.own, self.h.s, self.h.t, self.two, 5).start()

    def own_three(self):
        if self.route in ("zxy", "zyx"):
            self.copy(self.own, self.h.s, self.h.t, self.three, 10).start()

    def z(self, k):
        h = self.h
        s = 2 * h.peers[k] + h.x
        self.take(s, h.t)
        block = self.loc(s, h.t)
        on, device = self.along(k)
        pl.when(on)(self.copy(block, s, h.t, device, 2 + k).start)
        self.copy(block, s, h.t, self.two, 6 + k).start()
        if self.three:
            self.copy(block, s, h.t, self.three, 11 + k).start()

    def second(self, k):
        h = self.h
        zp = ([h.z] + h.peers)[k]
        s, t = (2 * zp + h.x, h.tb) if self.route == "zyx" else (2 * zp + h.xb, h.t)
        self.take(s, t)
        if self.three:
            self.copy(self.loc(s, t), s, t, self.three, 14 + k).start()

    def third(self, k):
        h = self.h
        zp = ([h.z] + h.peers)[k]
        if self.route == "zyx":
            self.take(2 * zp + h.xb, h.t)
            self.take(2 * zp + h.xb, h.tb)
        elif self.three:
            if not (self.route == "kv" and k == 0):
                self.take(2 * zp + h.x, h.tb)
            self.take(2 * zp + h.xb, h.tb)

    def drain(self):
        h = self.h

        def sent(i):
            return self.copy(self.own, h.s, h.t, h.core, i).wait_send

        pl.when(h.z < 3)(sent(0))
        pl.when(h.z > 0)(sent(1))
        for k in range(3):
            pl.when(self.along(k)[0])(sent(2 + k))
        for i in range(5, 9):
            sent(i)()
        if self.three:
            for i in range(10 if self.route != "kv" else 11, 18):
                sent(i)()


def real_features():
    lane = lax.broadcasted_iota(jnp.int32, (1, 1152), 1)
    return (lax.rem(lane, BR) < 136).astype(F32)


def normalise(x, mask, gain, shift, count):
    mean = jnp.sum(x, axis=1, keepdims=True) * (1.0 / count)
    spread = (x - mean) * mask
    var = jnp.sum(spread * spread, axis=1, keepdims=True) * (1.0 / count)
    return spread * lax.rsqrt(var + EPS) * gain + shift


def forward_kernel(
    seg, gains, shifts, biases, b_in, tok_h, cot_h, w_qkv_h, w_o_h, w_in_h, w_out_h,
    wa_o, wo_o, wi_o, wu_o, n1t_o, n2t_o, cot_o, qn_o, kn_o, vn_o, qt_o, kt_o, ot_o,
    lse_o, mid_o, slope_o, act_o, go_o, par_o, mb_o, x_o,
    wa, wog, wo, wi, wu, n1, cot, cott, n2, sm, par, bins, qn, kn, vn, qt, kt, vt, mb, ot, att, mid,
    slope, act, tile, stage, lse, x_ref, segr, segc,
    tok, cot_in, w_qkv, w_o, w_in, w_out, spread,
    send, recv, dsend, drecv, ssend, srecv, lsem, osem, isem,
):
    h = Place()
    c, s, t = h.c, h.s, h.t
    rows = 512
    length = 2 * rows
    count = 1088
    own = pl.ds(pl.multiple_of(c * rows, rows), rows)
    sib = pl.ds(pl.multiple_of((1 - c) * rows, rows), rows)

    def piece(number, buf, route, col, width):
        def loc(sp, tp):
            where = col(tp)
            if not isinstance(where, int):
                where = pl.multiple_of(where, UNIT)
            return buf.at[rows_of(sp), pl.ds(where, width)]

        return Gather(h, number, loc(s, t), loc, route, send, recv)

    A = ([piece(0, wa, "zx", lambda tp: 0, 512),
          piece(1, wa, "kv", lambda tp: 512 + 512 * tp, 512)],
         [piece(7, wa, "zx", lambda tp: 1536, 128),
          piece(8, wa, "kv", lambda tp: 1664 + 128 * tp, 128)])
    O = ([piece(2, wog.at[c], "zx", lambda tp: 0, 512)],
         [piece(9, wog.at[c], "zx", lambda tp: 512, 128)])
    I = ([piece(3, wi, "zxy", lambda tp: 1024 * tp, 640),
          piece(4, wi, "zyx", lambda tp: 1024 * tp + 640, 384)],
         [piece(10, wi, "zyx", lambda tp: 2048 + 128 * tp, 128)])
    U = ([piece(5, wu, "zxy", lambda tp: 1024 * tp, 640),
          piece(6, wu, "zyx", lambda tp: 1024 * tp + 640, 384)],
         [piece(11, wu, "zyx", lambda tp: 2048 + 128 * tp, 128)])

    def each(group, stage, *args):
        for p in group[0]:
            getattr(p, stage)(*args)

        @pl.when(c == 0)
        def _():
            for p in group[1]:
                getattr(p, stage)(*args)

    def small_copy(sp, device, i):
        return remote(sm.at[sp], sm.at[sp], ssend.at[i], srecv.at[sp], device)

    loads = [pltpu.make_async_copy(src, dst, lsem.at[n]) for n, (src, dst) in enumerate((
        (w_qkv_h, w_qkv), (w_o_h, w_o), (tok_h, tok), (w_in_h, w_in), (w_out_h, w_out),
        (cot_h, cot_in)))]
    for copy in loads:
        copy.start()
    wide = lambda v: v.astype(F32)

    def deep(v):
        return jnp.concatenate([v, jnp.zeros((8, v.shape[1]), F32)], axis=0).astype(BF)

    def either(make):
        pl.when(c == 0)(lambda: make(0))
        pl.when(c == 1)(lambda: make(1))

    @pl.when(c == 1)
    def _():
        wi[:, 2048:2304] = jnp.zeros((1152, 256), BF)
        wu[:, 2048:2304] = jnp.zeros((1152, 256), BF)
        wa[:, 1536:1920] = jnp.zeros((1152, 384), BF)

    sm[s] = jnp.zeros((8, 256), F32)
    sm[s, 0:2, 0:136] = wide(gains[...])
    sm[s, 2:4, 0:136] = wide(shifts[...])
    sm[s, 4:8, 0:136] = wide(biases[...])
    loads[0].wait()

    def columns(core):
        for i in range(3):
            base = 1088 * i + 576 * core
            wa[rows_of(s), 512 * i:512 * i + 512] = deep(wide(w_qkv[:, base:base + 512]))
            if core == 0:
                wa[rows_of(s), 1536 + 128 * i:1664 + 128 * i] = deep(jnp.concatenate(
                    [wide(w_qkv[:, base + 512:base + 576]), jnp.zeros((136, 64), F32)], axis=1))

    either(columns)
    h.greet()
    for i, zp in enumerate(h.peers):
        small_copy(s, h.zdev(zp), i).start()
    small_copy(s, h.xdev, 3).start()
    each(A, "own_z")
    each(A, "own_two")
    feature = lax.broadcasted_iota(jnp.int32, (1088, 1), 0)
    place = feature + 8 * (feature // 136)
    spread[...] = (lax.broadcasted_iota(jnp.int32, (1088, 1152), 1) == place).astype(BF)
    loads[1].wait()

    def o_columns(core):
        at = slice(512 * core, 512 * core + 512)
        wog[core, rows_of(s), 0:512] = deep(mm(w_o[...], spread[:, at]))
        if core == 0:
            wog[core, rows_of(s), 512:640] = deep(mm(w_o[...], spread[:, 1024:1152]))

    either(o_columns)
    each(O, "own_z")
    for copy in loads[3:5]:
        copy.wait()

    def own_units(core):
        low = 1152 * core
        for src, dst in ((w_in, wi), (w_out, wu)):
            dst[rows_of(s), pl.ds(pl.multiple_of(t * 1024, UNIT), 1024)] = deep(
                wide(src[:, low:low + 1024]))
            if core == 0:
                dst[rows_of(s), pl.ds(pl.multiple_of(2048 + t * 128, UNIT), 128)] = deep(
                    wide(src[:, 1024:1152]))
        size = 1152 - 128 * core
        bins[t, :, 0:size] = jnp.broadcast_to(wide(b_in[0:1, low:low + size]), (8, size))
        if core == 1:
            bins[t, :, 1024:1152] = jnp.zeros((8, 128), F32)

    either(own_units)
    bin_copy = remote(bins.at[t], bins.at[t], ssend.at[7], srecv.at[8], h.ydev)
    bin_copy.start()
    each(I, "own_three")

    def spread_out(src, dst, to):
        @pl.loop(0, 3)
        def _(i):
            at = pl.ds(pl.multiple_of(384 * i, UNIT), 384)
            dst[to, at] = lax.dot_general(
                src[...], spread[:, at], (((0,), (0,)), ((), ())), preferred_element_type=F32
            ).astype(BF)

    loads[2].wait()
    spread_out(tok, x_ref, pl.ds(0, rows))
    ids = jnp.broadcast_to(seg[...], (8, 1024))
    segr[...] = ids
    segc[...] = ids.T

    top = 0
    for b in range(4):
        first = max(0, b - 2)
        width = (b + 1 - first) * 256
        kpos = lax.broadcasted_iota(jnp.int32, (width, 256), 0) + first * 256
        qpos = lax.broadcasted_iota(jnp.int32, (width, 256), 1) + b * 256
        seen = (kpos <= qpos) & (
            segc[first * 256:first * 256 + width, 0:1] == segr[0:1, b * 256:b * 256 + 256]
        )
        mb[top:top + width, :] = jnp.where(seen, 0.0, -1e30)
        top += width

    for k, zp in enumerate(h.peers):
        sp = 2 * zp + h.x
        small_copy(sp, h.xdev, 4 + k).wait_recv()
        small_copy(sp, h.xdev, 4 + k).start()
    each(A, "z", 0)
    for zp in [h.z] + h.peers:
        small_copy(2 * zp + h.xb, h.xdev, 0).wait_recv()

    padded = jnp.zeros((8, 1152), F32)
    natural = jnp.zeros((8, 1152), F32)
    for sp in range(8):
        wide = jnp.concatenate([sm[sp], jnp.zeros((8, 896), F32)], axis=1)
        padded = padded + (pltpu.roll(wide, 144 * sp, 1) if sp else wide)
        natural = natural + (pltpu.roll(wide, 136 * sp, 1) if sp else wide)
    par[0:8] = padded
    shifted = pltpu.roll(natural, 576, 1)
    par[8:16] = jnp.where(c == 0, natural, shifted)
    mask = real_features()
    each(A, "second", 0)
    loads[5].wait()
    spread_out(cot_in, cot, own)
    cot_copy = remote(cot.at[own], cot.at[own], dsend.at[0], drecv.at[0], h.core)
    cot_copy.start()

    @pl.loop(0, rows // 128)
    def _(i):
        at = pl.ds(pl.multiple_of(i * 128, 128), 128)
        to = pl.ds(pl.multiple_of(c * rows + i * 128, 128), 128)
        n1[to, :] = normalise(
            x_ref[at, :].astype(F32), mask, par[0:1, :], par[2:3, :], count
        ).astype(BF)

    n1_copy = remote(n1.at[own], n1.at[own], dsend.at[1], drecv.at[1], h.core)
    n1_copy.start()

    outs = []

    def flush(src, dst):
        copy = pltpu.make_async_copy(src, dst, osem.at[len(outs)])
        copy.start()
        outs.append(copy)

    flush(par, par_o)
    flush(mb, mb_o)
    flush(x_ref, x_o)

    def turn(src, dst, i, later):
        slot = i % 2
        if later:
            pltpu.make_async_copy(stage.at[slot], dst.at[:, 0:256], isem.at[slot]).wait()
        stage[slot] = src[256 * i:256 * i + 256, :].T
        pltpu.make_async_copy(
            stage.at[slot], dst.at[:, pl.ds(256 * i, 256)], isem.at[slot]).start()

    each(A, "z", 1)
    each(I, "own_z")
    each(A, "second", 1)
    cot_copy.wait_recv()
    flush(cot, cot_o)
    for i in range(2):
        cott[:, 256 * i:256 * i + 256] = cot[256 * i:256 * i + 256, :].T
    each(A, "z", 2)
    each(O, "own_two")
    each(O, "z", 0)
    each(A, "second", 2)
    n1_copy.wait_recv()
    for i in range(2):
        turn(n1, n1t_o, i, False)
    each(O, "z", 1)
    each(A, "second", 3)
    each(O, "z", 2)
    each(I, "own_two")
    each(I, "z", 0)

    def project(i, col, width, name, first_head):
        at = pl.ds(pl.multiple_of(i * 512, 512), 512)
        got = mm(n1[at, :], wa[:, col:col + width])
        where = 64 * first_head
        if name != "k":
            row = 12 if name == "q" else 13
            got = got + par[row:row + 1, where:where + width]
        low = got.astype(BF)
        if name == "q":
            low = low * jnp.asarray(0.125, BF)
        natural_ref, turned = {"q": (qn, qt), "k": (kn, kt), "v": (vn, vt)}[name]
        turned[where:where + width, at] = low.T
        natural_ref[at, where:where + width] = low

    for j in range(2):
        @pl.loop(0, 2)
        def _(i):
            project(i, 256 * j, 256, "q", 4 * j)
    for k in range(4):
        each(A, "third", k)
    for name, col in (("k", 512), ("v", 1024)):
        for j in range(2):
            @pl.loop(0, 2)
            def _(i):
                project(i, col + 256 * j, 256, name, 4 * j)
    each(I, "z", 1)
    each(U, "own_z")
    each(I, "second", 0)

    @pl.when(c == 0)
    def _():
        for name, col in (("q", 1536), ("k", 1664), ("v", 1792)):
            @pl.loop(0, 2)
            def _(i):
                project(i, col, 128, name, 8)

    @pl.when(c == 1)
    def _():
        for turned in (qt, kt, vt):
            turned[512:640, :] = jnp.zeros((128, length), BF)
        for natural_ref in (qn, kn, vn):
            natural_ref[:, 512:640] = jnp.zeros((length, 128), BF)

    flush(wa, wa_o)
    for src, dst in ((qn, qn_o), (kn, kn_o), (vn, vn_o), (qt, qt_o), (kt, kt_o)):
        flush(src, dst)
    lse[...] = jnp.zeros_like(lse)
    ot[c, 512:640, :] = jnp.zeros((128, length), BF)

    def attend(head):
        feat = pl.ds(pl.multiple_of(head * 64, 64), 64)
        pair = pl.ds(pl.multiple_of(head // 2 * 128, 128), 128)
        mine = lax.broadcasted_iota(jnp.int32, (128, 256), 0) // 64 == lax.rem(head, 2)
        top = 0
        for b in range(4):
            first = max(0, b - 2)
            width = (b + 1 - first) * 256
            keys = slice(first * 256, first * 256 + width)
            cols = slice(b * 256, b * 256 + 256)
            scores = mm(kn[keys, pair], jnp.where(mine, qt[pair, cols], jnp.zeros((), BF)))
            scores = scores + mb[top:top + width, :]
            top += width
            highest = jnp.max(scores, axis=0, keepdims=True)
            weights = jnp.exp(scores - highest)
            total = jnp.sum(weights, axis=0, keepdims=True)
            probs = (weights * (1.0 / total)).astype(BF)
            ot[c, feat, cols] = mm(vt[feat, keys], probs).astype(BF)
            lse[pl.ds(head, 1), cols] = highest + jnp.log(total)

    def heads(low, high):
        @pl.loop(low, high)
        def _(head):
            attend(head)

    each(I, "z", 2)
    each(O, "second", 0)
    heads(0, 2)
    each(O, "second", 1)
    each(O, "second", 2)
    each(I, "second", 1)
    each(U, "own_two")
    each(U, "own_three")
    heads(2, 4)
    each(O, "second", 3)
    wo_copy = remote(wog.at[c], wog.at[c], dsend.at[2], drecv.at[2], h.core)
    wo_copy.start()
    each(I, "second", 2)
    each(U, "z", 0)
    heads(4, 6)
    each(I, "second", 3)
    each(I, "third", 0)
    each(U, "z", 1)
    heads(6, 9 - c)
    each(U, "second", 0)
    each(I, "third", 1)
    each(U, "z", 2)

    flush(lse, lse_o)
    for i in range(2):
        at = pl.ds(pl.multiple_of(c * rows + 256 * i, 256), 256)
        att[c, 256 * i:256 * i + 256, :] = ot[c, :, at].T
    for i in range(2):
        at = pl.ds(pl.multiple_of((1 - c) * rows + 256 * i, 256), 256)
        vt[256 * i:256 * i + 256, 0:640] = ot[c, :, at].T
    att_copy = remote(vt.at[0:rows, 0:640], att.at[c], dsend.at[3], drecv.at[3], h.core)
    att_copy.start()
    ot_copy = remote(ot.at[c], ot.at[c], dsend.at[4], drecv.at[4], h.core)
    ot_copy.start()
    each(U, "second", 1)

    wo_copy.wait_recv()

    def order_rows(half, src, to, width):
        for sp in range(8):
            slope[136 * sp:136 * sp + 136, 0:width] = (
                wog[half, 144 * sp:144 * sp + 144, src:src + width].astype(F32)[0:136])
        wo[0:576, to:to + width] = slope[0:576, 0:width].astype(BF)
        wo[640:1152, to:to + width] = slope[576:1088, 0:width].astype(BF)

    for half in range(2):
        for q in range(2):
            order_rows(half, 256 * q, 512 * half + 256 * q, 256)
    order_rows(0, 512, 1024, 128)
    wo[576:640, :] = jnp.zeros((64, 1152), BF)
    wo[1152:1280, :] = jnp.zeros((128, 1152), BF)
    flush(wo.at[pl.ds(pl.multiple_of(c * 640, 128), 640)], wo_o)
    att_copy.wait_recv()
    att_copy.wait_send()
    each(I, "third", 2)

    @pl.loop(0, 4)
    def _(i):
        at = pl.ds(pl.multiple_of(i * 128, 128), 128)
        to = pl.ds(pl.multiple_of(c * rows + i * 128, 128), 128)
        x = (
            x_ref[at, :].astype(F32)
            + (mm(att[0, at, :], wo[0:640, :]) + mm(att[1, at, :], wo[640:1280, :]))
            + par[6:7, :]
        )
        mid[at, :] = x
        n2[to, :] = normalise(x, mask, par[1:2, :], par[3:4, :], count).astype(BF)

    flush(mid, mid_o)
    n2_copy = remote(n2.at[own], n2.at[own], dsend.at[5], drecv.at[5], h.core)
    n2_copy.start()
    ot_copy.wait_recv()
    flush(ot, ot_o)
    each(U, "second", 2)
    each(I, "third", 3)
    flush(wi, wi_o)
    for i in range(2, 4):
        cott[:, 256 * i:256 * i + 256] = cot[256 * i:256 * i + 256, :].T
        turn(n1, n1t_o, i, True)
    n2_copy.wait_recv()
    for i in range(4):
        turn(n2, n2t_o, i, True)
    bin_copy.wait_recv()
    root = math.sqrt(2.0 / math.pi)

    def slot_copies(slot, cols):
        base = pl.multiple_of(1024 * slot, 1024)
        return (
            pltpu.make_async_copy(slope.at[pl.ds(base, 1024)], slope_o.at[:, cols], isem.at[2 + slot]),
            pltpu.make_async_copy(act.at[slot], act_o.at[:, cols], isem.at[4 + slot]),
            pltpu.make_async_copy(tile.at[slot], go_o.at[:, :, :, cols], isem.at[6 + slot]),
        )

    def hidden(i):
        j = jnp.where(i < 4, 4 * h.tb + i, jnp.where(i < 8, 4 * t + i - 4, 8))
        slot = lax.rem(i, 2)
        base = pl.multiple_of(1024 * slot, 1024)
        cols = pl.ds(pl.multiple_of(j * 256, 256), 256)

        @pl.when(i >= 2)
        def _():
            for copy in slot_copies(slot, cols):
                copy.wait()
        half = j // 4
        off = pl.multiple_of(256 * (j - 4 * half), 256)
        bias = jnp.where(
            j < 8,
            bins[pl.ds(jnp.minimum(half, 1), 1), 0:1, pl.ds(jnp.where(j < 8, off, 0), 256)][0],
            jnp.concatenate([bins[0, 0:1, 1024:1152], bins[1, 0:1, 1024:1152]], axis=1),
        )

        @pl.loop(0, 4)
        def _(q):
            at = pl.ds(pl.multiple_of(q * 256, 256), 256)
            v = mm(n2[at, :], wi[:, cols]) + bias
            square = v * v
            bent = jnp.tanh(root * (v + 0.044715 * square * v))
            act[slot, at, :] = (0.5 * v * (1.0 + bent)).astype(BF)
            slope[pl.ds(pl.multiple_of(base + 256 * q, 256), 256), :] = (
                0.5 * (1.0 + bent) + (0.5 * root) * v * (1.0 - bent * bent) * (
                    1.0 + (3.0 * 0.044715) * square))

        @pl.loop(0, 2)
        def _(half):
            got = mm(cott[pl.ds(pl.multiple_of(576 * half, 576), 576), :], act[slot])
            for q in range(4):
                tile[slot, 2 * half + q // 2, q % 2] = got[144 * q:144 * q + 144, :].astype(BF)
        for copy in slot_copies(slot, cols):
            copy.start()

    def units(low, high):
        @pl.loop(low, high)
        def _(i):
            hidden(i)

    units(0, 2)
    each(U, "second", 3)
    each(U, "third", 0)
    units(2, 4)
    each(U, "third", 1)
    units(4, 9 - c)
    each(U, "third", 2)
    each(U, "third", 3)
    flush(wu, wu_o)
    for slot in range(2):
        for copy in slot_copies(slot, pl.ds(0, 256)):
            copy.wait()
    for slot in range(2):
        pltpu.make_async_copy(stage.at[slot], n2t_o.at[:, 0:256], isem.at[slot]).wait()
    for copy in outs:
        copy.wait()
    for i in range(7):
        small_copy(s, h.xdev, i).wait_send()
    for copy in (bin_copy, cot_copy, n1_copy, wo_copy, ot_copy, n2_copy):
        copy.wait_send()
    for group in (A, O, I, U):
        each(group, "drain")


def run_forward(tokens, segment_ids, norm_gains, norm_shifts, biases, w_qkv, w_o, w_in, b_in,
                w_out, cotangent):
    hbm = pl.BlockSpec(memory_space=pltpu.HBM)
    vmem = pl.BlockSpec(memory_space=pltpu.VMEM)
    sds = jax.ShapeDtypeStruct
    shapes = [
        sds((1152, 1920), BF), sds((640, 1152), BF), sds((1152, 2304), BF), sds((1152, 2304), BF),
        sds((1152, 1024), BF), sds((1152, 1024), BF), sds((1024, 1152), BF),
        sds((1024, 640), BF), sds((1024, 640), BF), sds((1024, 640), BF),
        sds((640, 1024), BF), sds((640, 1024), BF), sds((2, 640, 1024), BF),
        sds((16, 1024), F32), sds((512, 1152), F32), sds((1024, 2304), F32), sds((1024, 2304), BF),
        sds((4, 2, 144, 2304), BF), sds((16, 1152), F32), sds((2304, 256), F32), sds((512, 1152), BF),
    ]
    V = pltpu.VMEM
    dma = pltpu.SemaphoreType.DMA
    scratch = [
        V((1152, 1920), BF), V((2, 1152, 640), BF), V((1280, 1152), BF), V((1152, 2304), BF),
        V((1152, 2304), BF), V((1024, 1152), BF), V((1024, 1152), BF), V((1152, 1024), BF),
        V((1024, 1152), BF),
        V((8, 8, 256), F32), V((16, 1152), F32), V((2, 8, 1152), F32),
        V((1024, 640), BF), V((1024, 640), BF), V((1024, 640), BF),
        V((640, 1024), BF), V((640, 1024), BF), V((640, 1024), BF),
        V((2304, 256), F32), V((2, 640, 1024), BF), V((2, 512, 640), BF), V((512, 1152), F32),
        V((2048, 256), F32), V((2, 1024, 256), BF), V((2, 4, 2, 144, 256), BF),
        V((2, 1152, 256), BF), V((16, 1024), F32), V((512, 1152), BF), V((8, 1024), jnp.int32), V((1024, 8), jnp.int32),
        V((1088, 512), BF), V((1088, 512), BF), V((136, 3264), BF), V((136, 1088), BF),
        V((136, 2176), BF), V((136, 2176), BF), V((1088, 1152), BF),
        dma((12, 18)), dma((12, 16)), dma((6,)), dma((6,)), dma((8,)), dma((9,)), dma((12,)),
        dma((17,)), dma((8,)),
    ]
    kept = pl.pallas_call(
        forward_kernel, out_shape=shapes, in_specs=[vmem] * 5 + [hbm] * 6, out_specs=[hbm] * len(shapes),
        scratch_shapes=scratch,
        compiler_params=pltpu.CompilerParams(
            collective_id=0, has_side_effects=True, vmem_limit_bytes=63 << 20),
        cost_estimate=pl.CostEstimate(flops=12 * 10**9, bytes_accessed=60 * 10**6, transcendentals=10**7),
        name="forward",
    )(segment_ids, norm_gains, norm_shifts, biases, b_in.reshape(1, -1), tokens[0].T, cotangent[0].T,
      w_qkv, w_o, w_in, w_out.T)
    return kept


def nt(left, right):
    return lax.dot_general(left, right, (((1,), (1,)), ((), ())), preferred_element_type=F32)


def backward_kernel(
    par, lse, wa_h, wo_h, wi_h, wu_h, n1t_h, n2t_h, cot_h, qn_h, kn_h, vn_h, qt_h,
    kt_h, ot_h, mid_h, slope_h, act_h, go_h, mb_h, x_h,
    mixed_o, tokens_o, out_o, in_o, qkv_o, proj_o, sums_o,
    WI, WU, ACT, IG, COT, COTT, N2T, inner, F1, F2, F3, F4, mix, yr, xr, x1, y2, zr, gi, held,
    acck, accv, vyr, xra, zra, ysa, yra, go, xro, zro, yso, yro, sg, sgx, sgz, sgy, bsum,
    load, innersem, heldsem, ysend, yrecv, xsend, xrecv, isend, irecv, zsend, zrecv,
    axs, axr, azs, azr, ays, ayr, oxs, oxr, ozs, ozr, oys, oyr, gsend, grecv, dsend, drecv,
    outsem, finsend, finrecv, finloc,
):
    h = Place()
    c, s, t, z, x = h.c, h.s, h.t, h.z, h.x
    rows = 512
    count = 1088.0
    own0 = pl.multiple_of(c * rows, rows)
    sib0 = pl.multiple_of((1 - c) * rows, rows)
    n_tiles = 9 - c

    def fetch(n, src, dst):
        copy = pltpu.make_async_copy(src, dst, load.at[n])
        copy.start()
        return copy

    def tile_of(i):
        return jnp.where(i < 4, 4 * h.tb + i, jnp.where(i < 8, 4 * t + i - 4, 8))

    def inner_copy(i):
        slot = lax.rem(i, 2)
        return pltpu.make_async_copy(
            slope_h.at[:, pl.ds(pl.multiple_of(256 * tile_of(i), 256), 256)],
            inner.at[pl.ds(pl.multiple_of(1024 * slot, 1024), 1024)], innersem.at[slot])

    inner_copy(0).start()
    first = [fetch(0, cot_h, COT), fetch(1, wu_h, WU)]
    h.greet()

    @pl.when(c == 1)
    def _():
        IG[:, 2048:2304] = jnp.zeros((1024, 256), BF)
    sg[...] = jnp.zeros_like(sg)

    def cols_of(k):
        return slice(256 * k, 256 * k + 256) if k < 4 else slice(1024, 1152)

    def theirs(k):
        return pl.ds(pl.multiple_of(1024 * h.tb + 256 * k if k < 4 else 2048 + 128 * h.tb, 128),
                     256 if k < 4 else 128)

    def ours(k):
        return pl.ds(pl.multiple_of(1024 * t + 256 * k if k < 4 else 2048 + 128 * t, 128),
                     256 if k < 4 else 128)

    def slot_at(zp):
        return lax.rem(z - zp + 3, 4)

    def only(k, step):
        if k < 4:
            step()
        else:
            pl.when(c == 0)(step)

    def oy(k):
        return remote(go_h.at[:, :, :, theirs(k)], yr.at[:, :, :, cols_of(k)],
                      ysend.at[0, k], yrecv.at[0, k], h.ydev)

    def ox(k):
        cols = cols_of(k)
        return remote(yr.at[:, h.xb, :, cols], xr.at[:, :, cols], xsend.at[k], xrecv.at[k], h.xdev)

    def z_copy(m, k, i, zp):
        cols = cols_of(k)
        src = (xr, y2)[m]
        return remote(src.at[zp, :, cols], zr.at[m, slot_at(zp), :, cols],
                      zsend.at[m, k, i], zrecv.at[m, k, slot_at(zp)], h.zdev(zp))

    def held_copy(k):
        return pltpu.make_async_copy(
            go_h.at[:, :, :, ours(k)], held.at[:, :, :, 0:256 if k < 4 else 128], heldsem.at[0])

    def OY(k):
        def step():
            cols = cols_of(k)
            width = cols.stop - cols.start
            oy(k).wait_recv()
            held_copy(k).wait()

            @pl.loop(0, 4)
            def _(zp):
                for xp in range(2):
                    yr[zp, xp, :, cols] = (
                        yr[zp, xp, :, cols].astype(F32) + held[zp, xp, :, 0:width].astype(F32)
                    ).astype(BF)
            ox(k).start()
        only(k, step)
        if k < 4:
            only(k + 1, lambda: held_copy(k + 1).start())

    def OX(k):
        def step():
            cols = cols_of(k)
            ox(k).wait_recv()

            @pl.loop(0, 4)
            def _(zp):
                xr[zp, :, cols] = (
                    xr[zp, :, cols].astype(F32) + yr[zp, x, :, cols].astype(F32)).astype(BF)
            for i, zp in enumerate(h.peers):
                z_copy(0, k, i, zp).start()
        only(k, step)

    def LZ(m, k):
        def step():
            cols = cols_of(k)
            for i in range(3):
                ref = zr.at[m, i, :, cols]
                remote(ref, ref, zsend.at[m, k, 0], zrecv.at[m, k, i], h.core).wait_recv()
            src = (xr, y2)[m]
            F4[144 * m:144 * m + 144, cols] = (
                (src[z, :, cols].astype(F32) + zr[m, 0, :, cols].astype(F32))
                + (zr[m, 1, :, cols].astype(F32) + zr[m, 2, :, cols].astype(F32)))
        only(k, step)

    def tile_cols(i):
        return pl.ds(pl.multiple_of(256 * tile_of(i), 256), 256)

    def ix(i):
        cols = tile_cols(i)
        return remote(gi.at[:, h.xb, :, cols], x1.at[:, :, cols],
                      isend.at[i], irecv.at[i], h.xdev)

    def iy(k):
        return remote(x1.at[:, :, theirs(k)], y2.at[:, :, cols_of(k)],
                      ysend.at[1, k], yrecv.at[1, k], h.ydev)

    def IX(i):
        def step():
            cols = tile_cols(i)
            ix(i).wait_recv()

            @pl.loop(0, 4)
            def _(zp):
                x1[zp, :, cols] = (
                    x1[zp, :, cols].astype(F32) + gi[zp, x, :, cols].astype(F32)).astype(BF)
            if i < 4:
                iy(i).start()
            if i == 8:
                iy(4).start()
        only(4 if i == 8 else 0, step)

    def IY(k):
        def step():
            cols = cols_of(k)
            iy(k).wait_recv()

            @pl.loop(0, 4)
            def _(zp):
                y2[zp, :, cols] = (
                    y2[zp, :, cols].astype(F32) + x1[zp, :, ours(k)].astype(F32)).astype(BF)
            for i, zp in enumerate(h.peers):
                z_copy(1, k, i, zp).start()
        only(k, step)

    for k in range(5):
        only(k, lambda: oy(k).start())
    held_copy(0).start()

    for copy in first:
        copy.wait()
    second = [fetch(3, n2t_h, N2T), fetch(4, wi_h, WI), fetch(5, mid_h, F4), fetch(2, act_h, ACT)]

    def hidden(i):
        base = pl.multiple_of(1024 * lax.rem(i, 2), 1024)
        inner_copy(i).wait()

        @pl.when(i + 1 < n_tiles)
        def _():
            inner_copy(i + 1).start()
        cols = pl.ds(pl.multiple_of(256 * tile_of(i), 256), 256)
        bsum[...] = jnp.zeros_like(bsum)

        @pl.loop(0, 4)
        def _(q):
            at = pl.ds(pl.multiple_of(256 * q, 256), 256)
            v = inner[pl.ds(pl.multiple_of(base + 256 * q, 256), 256), :]
            low = (mm(COT[at, :], WU[:, cols]) * v).astype(BF)
            IG[at, cols] = low
            bsum[0:1, :] = bsum[0:1, :] + jnp.sum(low.astype(F32), axis=0, keepdims=True)

        @pl.when(i == 0)
        def _():
            second[0].wait()

        @pl.loop(0, 2)
        def _(half):
            got = mm(N2T[pl.ds(pl.multiple_of(576 * half, 576), 576), :], IG[:, cols])
            line = lax.broadcasted_iota(jnp.int32, (16, 256), 0) == 8
            for q in range(4):
                block = got[144 * q:144 * q + 144, :]
                zp, xp = 2 * half + q // 2, q % 2
                gi[zp, xp, 0:128, cols] = block[0:128].astype(BF)
                gi[zp, xp, 128:144, cols] = jnp.where(line, bsum[0:1, :], block[128:144]).astype(BF)

        ix(i).start()

    def units(low, high):
        @pl.loop(low, high)
        def _(i):
            hidden(i)

    units(0, 5)
    OY(0)
    IX(0)
    units(5, 9 - c)
    IX(1)
    IX(2)

    for copy in second[1:]:
        copy.wait()
    @pl.when(c == 1)
    def _():
        ACT[:, 2048:2304] = jnp.zeros((1024, 256), BF)


    def n2_copy(i):
        at = pl.ds(pl.multiple_of(384 * i, 128), 384)
        return remote(F3.at[:, at], F2.at[:, at], dsend.at[i], drecv.at[i], h.core)

    @pl.loop(0, 3)
    def _(i):
        at = pl.ds(pl.multiple_of(384 * i, 128), 384)
        F3[:, at] = nt(IG[pl.ds(sib0, rows), :], WI[at, :]).astype(BF)
        n2_copy(i).start()

    @pl.loop(0, 3)
    def _(i):
        at = pl.ds(pl.multiple_of(384 * i, 128), 384)
        F1[:, at] = nt(IG[pl.ds(own0, rows), :], WI[at, :])
    n2_sends = [n2_copy(i) for i in range(3)]
    OY(1)
    IX(3)

    wo_load = fetch(6, wo_h, WI.at[0:640, 0:1152])
    q_loads = [fetch(7, qn_h, IG.at[:, 0:640]), fetch(8, kn_h, IG.at[:, 640:1280]),
               fetch(9, vn_h, IG.at[:, 1280:1920]),
               fetch(10, mb_h, inner), fetch(11, n1t_h, N2T)]


    def mix_copy(i):
        at = pl.ds(pl.multiple_of(384 * i, 128), 384)
        return remote(WI.at[640:1152, at], mix.at[:, at], dsend.at[3 + i], drecv.at[3 + i], h.core)

    @pl.loop(0, 3)
    def _(i):
        at = pl.ds(pl.multiple_of(384 * i, 128), 384)
        WI[640:1152, at] = nt(ACT[pl.ds(sib0, rows), :], WU[at, :]).astype(BF)
        mix_copy(i).start()
    mix_sends = [mix_copy(i) for i in range(3)]

    mask = real_features()
    for copy in n2_sends:
        copy.wait_recv()

    @pl.loop(0, 16)
    def _(q):
        at = pl.ds(pl.multiple_of(32 * q, 32), 32)
        to = pl.ds(pl.multiple_of(own0 + 32 * q, 32), 32)
        grad = F1[at, :] + F2[at, :].astype(F32)
        v = F4[at, :]
        mean = jnp.sum(v, axis=1, keepdims=True) * (1.0 / count)
        spread = (v - mean) * mask
        rstd = lax.rsqrt(jnp.sum(spread * spread, axis=1, keepdims=True) * (1.0 / count) + EPS)
        hat = spread * rstd
        scaled = grad * par[1:2, :]
        grad_out = COT[to, :].astype(F32)
        got = grad_out + rstd * (
            scaled - jnp.sum(scaled, axis=1, keepdims=True) * (1.0 / count)
            - hat * (jnp.sum(scaled * hat, axis=1, keepdims=True) * (1.0 / count))) * mask
        low = got.astype(BF)
        F1[at, :] = got
        COT[to, :] = low
        sg[3:4, 0:1152] = sg[3:4, 0:1152] + jnp.sum(grad * hat, axis=0, keepdims=True)
        sg[4:5, 0:1152] = sg[4:5, 0:1152] + jnp.sum(grad, axis=0, keepdims=True)
        sg[5:6, 0:1152] = sg[5:6, 0:1152] + jnp.sum(grad_out, axis=0, keepdims=True)
        sg[6:7, 0:1152] = sg[6:7, 0:1152] + jnp.sum(low.astype(F32), axis=0, keepdims=True)

    bg_copy = remote(COT.at[pl.ds(own0, rows)], COT.at[pl.ds(own0, rows)], dsend.at[6], drecv.at[6], h.core)
    bg_copy.start()
    IX(4)

    for copy in n2_sends:
        copy.wait_send()
    for copy in mix_sends:
        copy.wait_recv()

    @pl.loop(0, 3)
    def _(i):
        at = pl.ds(pl.multiple_of(384 * i, 128), 384)
        got = nt(ACT[pl.ds(own0, rows), :], WU[at, :]) + mix[:, at].astype(F32)
        F3[:, at] = (F4[:, at] + got + par[7:8, at]).astype(BF)
    mix_out = pltpu.make_async_copy(F3, mixed_o, outsem.at[0])
    mix_out.start()
    t_loads = [fetch(12, qt_h, WU.at[0:640, 0:1024]), fetch(13, kt_h, WU.at[0:640, 1024:2048])]
    OY(2)
    OX(0)
    o_loads = [fetch(14, ot_h.at[0], ACT.at[0:640, 0:1024]), fetch(15, ot_h.at[1], ACT.at[0:640, 1024:2048])]

    wo_load.wait()
    bg_copy.wait_recv()
    bg_copy.wait_send()
    for copy in mix_sends:
        copy.wait_send()

    @pl.loop(0, 5)
    def _(pair):
        at = pl.ds(pl.multiple_of(128 * pair, 128), 128)
        got = nt(COT[...], WI[at, 0:1152]).astype(BF)
        WI[0:1024, pl.ds(pl.multiple_of(1280 + 128 * pair, 128), 128)] = got
        COTT[at, :] = got.T

    IX(5)

    for copy in o_loads:
        copy.wait()

    def proj(col, to):
        part = COT[:, col]
        acck[0:576, :] = mm(ACT[0:576, 0:1024], part)
        acck[576:1088, :] = mm(ACT[0:512, 1024:2048], part)
        for sp in range(8):
            block = jnp.concatenate([acck[136 * sp:136 * sp + 136, :], jnp.zeros((8, 128), F32)], axis=0)
            go[sp // 2, sp % 2, :, to:to + 128] = block.astype(BF)

    ocols = (slice(0, 512), slice(512, 640))

    def ox_copy(k):
        return remote(go.at[:, h.xb, :, ocols[k]], xro.at[:, :, ocols[k]], oxs.at[k], oxr.at[k], h.xdev)

    def oz_copy(k, i, zp):
        return remote(xro.at[zp, :, ocols[k]], zro.at[slot_at(zp), :, ocols[k]],
                      ozs.at[k, i], ozr.at[k, slot_at(zp)], h.zdev(zp))

    def oy_copy(k):
        return remote(yso.at[:, ocols[k]], yro.at[:, ocols[k]], oys.at[k], oyr.at[k], h.ydev)

    for q in range(4):
        proj(pl.ds(pl.multiple_of(512 * c + 128 * q, 128), 128), 128 * q)
    ox_copy(0).start()

    @pl.when(c == 0)
    def _():
        proj(slice(1024, 1152), 512)
        ox_copy(1).start()

    def o_after_x(k):
        ox_copy(k).wait_recv()

        @pl.loop(0, 4)
        def _(zp):
            xro[zp, :, ocols[k]] = (
                xro[zp, :, ocols[k]].astype(F32) + go[zp, x, :, ocols[k]].astype(F32)).astype(BF)
        for i, zp in enumerate(h.peers):
            oz_copy(k, i, zp).start()

    def o_after_z(k):
        for i in range(3):
            ref = zro.at[i, :, ocols[k]]
            remote(ref, ref, ozs.at[k, 0], ozr.at[k, i], h.core).wait_recv()
        cols = ocols[k]
        yso[:, cols] = (
            (xro[z, :, cols].astype(F32) + zro[0, :, cols].astype(F32))
            + (zro[1, :, cols].astype(F32) + zro[2, :, cols].astype(F32))).astype(BF)
        oy_copy(k).start()

    def o_after_y(k):
        oy_copy(k).wait_recv()
        F4[288:432, ocols[k]] = yso[:, ocols[k]].astype(F32) + yro[:, ocols[k]].astype(F32)

    def both(step, main, more):
        for k in main:
            step(k)

        @pl.when(c == 0)
        def _():
            for k in more:
                step(k)

    for copy in q_loads + t_loads:
        copy.wait()
    ACT[:, 1536:1920] = jnp.zeros((1024, 384), BF)
    WI[512:640, 0:1024] = jnp.zeros((128, 1024), BF)

    def attend(head):
        pair = head // 2
        parity = lax.rem(head, 2)
        both_heads = pl.ds(pl.multiple_of(pair * 128, 128), 128)
        feat = pl.ds(pl.multiple_of(head * 64, 64), 64)
        on_rows = lax.broadcasted_iota(jnp.int32, (128, 256), 0) // 64 == parity
        on_lanes = lax.broadcasted_iota(jnp.int32, (256, 128), 1) // 64 == parity
        zero = jnp.zeros((), BF)
        qcol = both_heads
        kcol = pl.ds(pl.multiple_of(640 + pair * 128, 128), 128)
        vcol = pl.ds(pl.multiple_of(1280 + pair * 128, 128), 128)

        @pl.when(parity == 0)
        def _():
            acck[0:1024, :] = jnp.zeros((1024, 128), F32)
            accv[...] = jnp.zeros_like(accv)
        top = 0
        for b in range(4):
            start = max(0, b - 2)
            width = (b + 1 - start) * 256
            keys = slice(start * 256, start * 256 + width)
            cols = slice(b * 256, b * 256 + 256)
            scores = mm(IG[keys, kcol], jnp.where(on_rows, WU[both_heads, cols], zero))
            probs = jnp.exp(scores + inner[top:top + width, :] - lse[pl.ds(head, 1), cols])
            top += width
            grads = mm(IG[keys, vcol], jnp.where(on_rows, COTT[both_heads, cols], zero))
            terms = jnp.sum(probs * grads, axis=0, keepdims=True)
            sgrad = (probs * (grads - terms)).astype(BF)
            accv[keys, :] = accv[keys, :] + mm(
                probs.astype(BF), jnp.where(on_lanes, WI[cols, vcol], zero))
            acck[keys, :] = acck[keys, :] + mm(
                sgrad, jnp.where(on_lanes, IG[cols, qcol], zero))
            WI[feat, cols] = (
                mm(WU[feat, 1024 + start * 256:1024 + start * 256 + width], sgrad) * 0.125
            ).astype(BF)

        @pl.when((parity == 1) | (head == 8 - c))
        def _():
            kto = pl.ds(pl.multiple_of(jnp.where(pair < 4, 512 + 128 * pair, 1664), 128), 128)
            vto = pl.ds(pl.multiple_of(jnp.where(pair < 4, 1024 + 128 * pair, 1792), 128), 128)
            ACT[:, kto] = acck[0:1024, :].astype(BF)
            ACT[:, vto] = accv[...].astype(BF)

    def heads(low, high):
        @pl.loop(low, high)
        def _(head):
            attend(head)

    acols = (slice(0, 256), slice(256, 512), slice(512, 640))

    def qcols(k):
        return slice(256 * k, 256 * k + 256) if k < 2 else slice(1536, 1664)

    def vcols(k, tp):
        start = 512 + 512 * tp + 256 * k if k < 2 else 1664 + 128 * tp
        return pl.ds(pl.multiple_of(start, 128), 256 if k < 2 else 128)

    def weights(cols):
        @pl.loop(0, 2)
        def _(half):
            got = mm(N2T[pl.ds(pl.multiple_of(576 * half, 576), 576), :], ACT[:, cols])
            for q in range(4):
                gi[2 * half + q // 2, q % 2, :, cols] = got[144 * q:144 * q + 144, :].astype(BF)

    def vy(k):
        return remote(gi.at[:, :, :, vcols(k, h.tb)], vyr.at[:, :, :, acols[k]], ays.at[k], ayr.at[k],
                      h.ydev)

    def ax(m, k):
        src = gi.at[:, h.xb, :, qcols(k)] if m == 0 else vyr.at[:, h.xb, :, acols[k]]
        return remote(src, xra.at[m, :, :, acols[k]], axs.at[m, k], axr.at[m, k], h.xdev)

    def az(m, k, i, zp):
        return remote(xra.at[m, zp, :, acols[k]], zra.at[m, slot_at(zp), :, acols[k]],
                      azs.at[m, k, i], azr.at[m, k, slot_at(zp)], h.zdev(zp))

    def ay(m, k):
        return remote(ysa.at[m, :, acols[k]], yra.at[m, :, acols[k]],
                      ays.at[3 + 3 * m + k], ayr.at[3 + 3 * m + k], h.ydev)

    def VY(k):
        vy(k).wait_recv()
        cols = acols[k]

        @pl.loop(0, 4)
        def _(zp):
            for xp in range(2):
                vyr[zp, xp, :, cols] = (
                    vyr[zp, xp, :, cols].astype(F32) + gi[zp, xp, :, vcols(k, t)].astype(F32)
                ).astype(BF)
        ax(1, k).start()

    def AX(m, k):
        cols = acols[k]
        ax(m, k).wait_recv()

        @pl.loop(0, 4)
        def _(zp):
            mine = gi[zp, x, :, qcols(k)] if m == 0 else vyr[zp, x, :, cols]
            xra[m, zp, :, cols] = (
                xra[m, zp, :, cols].astype(F32) + mine.astype(F32)).astype(BF)
        for i, zp in enumerate(h.peers):
            az(m, k, i, zp).start()

    def AZ(m, k):
        cols = acols[k]
        for i in range(3):
            ref = zra.at[m, i, :, cols]
            remote(ref, ref, azs.at[m, k, 0], azr.at[m, k, i], h.core).wait_recv()
        ysa[m, :, cols] = (
            (xra[m, z, :, cols].astype(F32) + zra[m, 0, :, cols].astype(F32))
            + (zra[m, 1, :, cols].astype(F32) + zra[m, 2, :, cols].astype(F32))).astype(BF)
        ay(m, k).start()

    def AY(m, k):
        ay(m, k).wait_recv()
        cols = acols[k]
        mine, other = ysa[m, :, cols].astype(F32), yra[m, :, cols].astype(F32)
        if k < 2:
            blocks = [(k, mine + other)] if m == 0 else [(2 + 2 * t + k, mine), (2 + 2 * h.tb + k, other)]
            for block, value in blocks:
                inner[pl.ds(pl.multiple_of(144 * block, 16), 144), :] = value
        elif m == 0:
            inner[864:1008, 0:128] = mine + other
        else:
            inner[864:1008, 128:256] = jnp.where(t == 0, mine, other)
            inner[1008:1152, 0:128] = jnp.where(t == 0, other, mine)

    def group(k):
        weights(vcols(k, h.tb))
        vy(k).start()
        weights(qcols(k))
        ax(0, k).start()
        weights(vcols(k, t))

    def turn(pair):
        at = slice(128 * pair, 128 * pair + 128)
        ACT[:, at if pair < 4 else slice(1536, 1664)] = WI[at, 0:1024].T

    def more(step, *args):
        @pl.when(c == 0)
        def _():
            step(*args, 2)

    IX(6)
    heads(0, 2)
    OY(3)
    IX(7)
    IX(8)
    heads(2, 4)
    turn(0)
    turn(1)
    for n in range(9):
        only(4 if n == 8 else 0, lambda: ix(n).wait_send())
    group(0)
    OY(4)
    IY(0)
    heads(4, 6)
    IY(1)
    LZ(0, 0)
    OX(1)
    heads(6, 8)
    turn(2)
    turn(3)
    group(1)
    IY(2)
    heads(8, 9 - c)

    @pl.when(c == 0)
    def _():
        turn(4)
        group(2)
    wa_load = fetch(16, wa_h, WI.at[:, 0:1920])
    x_load = fetch(17, x_h, COT.at[0:512])
    IY(3)
    IY(4)
    OX(2)
    both(o_after_x, (0,), (1,))

    mix_out.wait()
    wa_load.wait()

    def n1_copy(i):
        at = pl.ds(pl.multiple_of(384 * i, 128), 384)
        return remote(F3.at[:, at], F2.at[:, at], dsend.at[7 + i], drecv.at[7 + i], h.core)

    @pl.loop(0, 3)
    def _(i):
        at = pl.ds(pl.multiple_of(384 * i, 128), 384)
        F3[:, at] = nt(ACT[pl.ds(sib0, rows), 0:1920], WI[at, 0:1920]).astype(BF)
        n1_copy(i).start()

    @pl.loop(0, 4)
    def _(i):
        at = pl.ds(pl.multiple_of(256 * i, 256), 256)
        inner[pl.ds(pl.multiple_of(512 * i, 512), 512), :] = nt(
            ACT[pl.ds(own0, rows), 0:1920], WI[at, 0:1920])
    part = nt(ACT[pl.ds(own0, rows), 0:1920], WI[1024:1152, 0:1920])
    inner[2048:2304, 0:128] = part[0:256]
    inner[2048:2304, 128:256] = part[256:512]
    n1_sends = [n1_copy(i) for i in range(3)]

    @pl.loop(0, 15)
    def _(i):
        at = pl.ds(pl.multiple_of(128 * i, 128), 128)
        sg[0:1, at] = jnp.sum(ACT[:, at].astype(F32), axis=0, keepdims=True)
    OX(3)
    OX(4)
    VY(0)
    LZ(0, 1)
    VY(1)
    for n in range(3):
        LZ(1, n)
    both(o_after_z, (0,), (1,))
    more(VY)
    AX(0, 0)
    AX(0, 1)
    x_load.wait()
    for copy in n1_sends:
        copy.wait_recv()

    @pl.loop(0, 16)
    def _(i):
        at = pl.ds(pl.multiple_of(32 * i, 32), 32)
        half = i // 8
        tail = inner[pl.ds(pl.multiple_of(2048 + 32 * (i - 8 * half), 32), 32),
                     pl.ds(pl.multiple_of(128 * half, 128), 128)]
        part = jnp.concatenate(
            [inner[pl.ds(pl.multiple_of(512 * j + 32 * i, 32), 32), :] for j in range(4)] + [tail],
            axis=1)
        grad = part + F2[at, :].astype(F32)
        v = COT[at, :].astype(F32)
        mean = jnp.sum(v, axis=1, keepdims=True) * (1.0 / count)
        spread = (v - mean) * mask
        rstd = lax.rsqrt(jnp.sum(spread * spread, axis=1, keepdims=True) * (1.0 / count) + EPS)
        hat = spread * rstd
        scaled = grad * par[0:1, :]
        F1[at, :] = F1[at, :] + rstd * (
            scaled - jnp.sum(scaled, axis=1, keepdims=True) * (1.0 / count)
            - hat * (jnp.sum(scaled * hat, axis=1, keepdims=True) * (1.0 / count))) * mask
        sg[1:2, 0:1152] = sg[1:2, 0:1152] + jnp.sum(grad * hat, axis=0, keepdims=True)
        sg[2:3, 0:1152] = sg[2:3, 0:1152] + jnp.sum(grad, axis=0, keepdims=True)

    tok_outs = [pltpu.make_async_copy(F1, tokens_o, outsem.at[1])]
    tok_outs[0].start()

    sgx_copy = remote(sg, sgx, gsend.at[0], grecv.at[0], h.xdev)
    sgx_copy.start()
    more(AX, 0)
    sgx_copy.wait()
    sgx[...] = sgx[...] + sg[...]

    def sgz_copy(i, zp):
        return remote(sgx, sgz.at[slot_at(zp)], gsend.at[1 + i], grecv.at[1 + slot_at(zp)], h.zdev(zp))

    for i, zp in enumerate(h.peers):
        sgz_copy(i, zp).start()
    both(o_after_y, (0,), (1,))
    for n in range(2, 5):
        LZ(0, n)
    for n in range(3, 5):
        LZ(1, n)

    finals = []

    def deliver(n, src, out):
        local = pltpu.make_async_copy(src, out.at[c], finloc.at[n])
        local.start()
        over = remote(src, out.at[c], finsend.at[n], finrecv.at[n], h.core)
        over.start()
        finals.append((local, over))

    deliver(0, F4.at[288:432, 0:640], proj_o)
    deliver(1, F4.at[0:144], out_o)
    deliver(2, F4.at[144:288], in_o)
    AX(1, 0)
    AX(1, 1)
    more(AX, 1)
    AZ(0, 0)
    AZ(0, 1)
    more(AZ, 0)
    for i in range(3):
        remote(sgz.at[i], sgz.at[i], gsend.at[1], grecv.at[1 + i], h.core).wait_recv()
    for i, zp in enumerate(h.peers):
        sgz_copy(i, zp).wait_send()
    sg[...] = (sgx[...] + sgz[0]) + (sgz[1] + sgz[2])
    sgy_copy = remote(sg, sgy, gsend.at[4], grecv.at[4], h.ydev)
    sgy_copy.start()
    AZ(1, 0)
    AZ(1, 1)
    more(AZ, 1)
    sgy_copy.wait()
    sgx[...] = sg[...] + sgy[...]
    deliver(3, sgx, sums_o)
    for m in range(2):
        AY(m, 0)
        AY(m, 1)
        more(AY, m)
    deliver(4, inner.at[0:1152], qkv_o)

    for copy in tok_outs:
        copy.wait()
    for copy in n1_sends:
        copy.wait_send()

    def drain(k):
        oy(k).wait_send()
        ox(k).wait_send()
        iy(k).wait_send()
        for m in range(2):
            for i, zp in enumerate(h.peers):
                z_copy(m, k, i, zp).wait_send()

    for n in range(5):
        only(n, lambda: drain(n))

    def o_drain(k):
        ox_copy(k).wait_send()
        oy_copy(k).wait_send()
        for i, zp in enumerate(h.peers):
            oz_copy(k, i, zp).wait_send()

    both(o_drain, (0,), (1,))

    def a_drain(k):
        vy(k).wait_send()
        for m in range(2):
            ay(m, k).wait_send()
            ax(m, k).wait_send()
            for i, zp in enumerate(h.peers):
                az(m, k, i, zp).wait_send()

    a_drain(0)
    a_drain(1)
    more(a_drain)
    for local, over in finals:
        local.wait()
        over.wait()


def run_backward(saved):
    (wa, wo, wi, wu, n1t, n2t, cot, qn, kn, vn, qt, kt, ot, lse, mid, slope, act, go, par, mb, x) = saved
    hbm = pl.BlockSpec(memory_space=pltpu.HBM)
    vmem = pl.BlockSpec(memory_space=pltpu.VMEM)
    sds = jax.ShapeDtypeStruct
    V = pltpu.VMEM
    dma = pltpu.SemaphoreType.DMA
    shapes = [
        sds((512, 1152), BF), sds((512, 1152), F32), sds((2, 144, 1152), F32),
        sds((2, 144, 1152), F32), sds((2, 1152, 256), F32), sds((2, 144, 640), F32),
        sds((2, 8, 1920), F32),
    ]
    scratch = [
        V((1152, 2304), BF), V((1152, 2304), BF), V((1024, 2304), BF), V((1024, 2304), BF),
        V((1024, 1152), BF), V((640, 1024), BF), V((1152, 1024), BF), V((2304, 256), F32),
        V((512, 1152), F32), V((512, 1152), BF), V((512, 1152), BF), V((512, 1152), F32),
        V((512, 1152), BF), V((4, 2, 144, 1152), BF), V((4, 144, 1152), BF), V((4, 144, 2304), BF), V((4, 144, 1152), BF),
        V((2, 3, 144, 1152), BF), V((4, 2, 144, 2304), BF), V((4, 2, 144, 256), BF),
        V((1088, 128), F32), V((1024, 128), F32),
        V((4, 2, 144, 640), BF), V((2, 4, 144, 640), BF), V((2, 3, 144, 640), BF), V((2, 144, 640), BF), V((2, 144, 640), BF),
        V((4, 2, 144, 640), BF), V((4, 144, 640), BF), V((3, 144, 640), BF), V((144, 640), BF),
        V((144, 640), BF),
        V((8, 1920), F32), V((8, 1920), F32), V((3, 8, 1920), F32), V((8, 1920), F32), V((8, 256), F32),
        dma((18,)), dma((2,)), dma((1,)),
        dma((2, 5)), dma((2, 5)), dma((5,)), dma((5,)), dma((9,)), dma((9,)), dma((2, 5, 3)), dma((2, 5, 3)),
        dma((2, 3)), dma((2, 3)), dma((2, 3, 3)), dma((2, 3, 3)), dma((9,)), dma((9,)),
        dma((2,)), dma((2,)), dma((2, 3)), dma((2, 3)), dma((2,)), dma((2,)),
        dma((5,)), dma((5,)), dma((10,)), dma((10,)), dma((6,)), dma((5,)), dma((5,)), dma((5,)),
    ]
    return pl.pallas_call(
        backward_kernel, out_shape=shapes, in_specs=[vmem] * 2 + [hbm] * 19,
        out_specs=[hbm] * len(shapes), scratch_shapes=scratch,
        compiler_params=pltpu.CompilerParams(
            collective_id=1, has_side_effects=True, vmem_limit_bytes=65300 << 10),
        cost_estimate=pl.CostEstimate(flops=40 * 10**9, bytes_accessed=80 * 10**6, transcendentals=2 * 10**7),
        name="backward",
    )(par, lse, wa, wo, wi, wu, n1t, n2t, cot, qn, kn, vn, qt, kt, ot, mid, slope, act, go, mb, x)


def finish_kernel(mixed_h, tokens_h, out_h, in_h, qkv_h, proj_h, sums_h,
                  mixed, tokens, gains, shifts, biases, w_qkv, w_o, w_in, b_in, w_out,
                  mixed_in, tokens_in, out_in, in_in, qkv_in, proj_in, sums_in, line, isem):
    c = lax.axis_index("ctx")
    s = lax.axis_index("shard")
    loads = [pltpu.make_async_copy(src, dst, isem.at[n]) for n, (src, dst) in enumerate((
        (tokens_h, tokens_in), (mixed_h, mixed_in), (qkv_h, qkv_in), (out_h, out_in), (in_h, in_in),
        (proj_h, proj_in), (sums_h, sums_in)))]
    for copy in loads:
        copy.start()

    def turned(v):
        v = v.T
        return jnp.concatenate([v[144 * q:144 * q + 136] for q in range(8)], axis=0)

    loads[0].wait()
    loads[1].wait()
    for i in range(4):
        at = slice(128 * i, 128 * i + 128)
        tokens[:, at] = turned(tokens_in[at, :])
        mixed[:, at] = turned(mixed_in[at, :].astype(F32)).astype(BF)

    def join(v):
        block = lax.broadcasted_iota(jnp.int32, v.shape, 1) // 136
        got = v
        for q in range(1, 8):
            got = jnp.where(block == q, pltpu.roll(v, 1152 - 8 * q, 1), got)
        return got[:, 0:1088]

    def heads(core, n):
        yield 2 * n, 0, 256, 0
        yield 2 * n + 1, 0, 256, 256
        if core == 0:
            yield 6 + n // 2, 128 * (n % 2), 64, 512

    for copy in loads[2:]:
        copy.wait()

    def for_core(core):
        at = slice(68 * core, 68 * core + 68)
        for n in range(3):
            for owner in range(2):
                for block, start, width, to in heads(owner, n):
                    to = 1088 * n + 576 * owner + to
                    w_qkv[:, to:to + width] = qkv_in[
                        owner, 144 * block + at.start:144 * block + at.stop, start:start + width]
        wide = jnp.concatenate(
            [proj_in[0, at, 0:512], proj_in[1, at, 0:512], proj_in[0, at, 512:640]], axis=1)
        w_o[...] = join(wide)
        w_in[:, 0:1152] = in_in[0, at, :]
        w_in[:, 1152:2176] = in_in[1, at, 0:1024]
        w_out[:, 0:1152] = out_in[0, at, :]
        w_out[:, 1152:2176] = out_in[1, at, 0:1024]

    pl.when(c == 0)(lambda: for_core(0))
    pl.when(c == 1)(lambda: for_core(1))

    rows = sums_in[0] + sums_in[1]
    mine = pltpu.roll(rows, 1920 - (s * BR + c * 68), 1)[:, 0:68]
    gains[0:1, :] = mine[1:2]
    gains[1:2, :] = mine[3:4]
    shifts[0:1, :] = mine[2:3]
    shifts[1:2, :] = mine[4:5]
    biases[2:3, :] = mine[6:7]
    biases[3:4, :] = mine[5:6]
    for n, row in ((0, 0), (2, 1)):
        start, more = 512 * n, 1536 + 128 * n
        line[:, 0:512] = sums_in[0, :, start:start + 512]
        line[:, 512:576] = sums_in[0, :, more:more + 64]
        line[:, 576:1088] = sums_in[1, :, start:start + 512]
        got = pltpu.roll(line[:, 0:1152], 1152 - (2 * s + c) * 68, 1)[:, 0:68]
        biases[row:row + 1, :] = got[0:1]
    line[:, 0:1152] = in_in[0, 136:144, :]
    line[:, 1152:2176] = in_in[1, 136:144, 0:1024]
    b_in[...] = pltpu.roll(line[...], 2176 - (2 * s + c) * 136, 1)[0:1, 0:136]


def finish(mixed, tokens_grad, out_g, in_g, qkv_g, proj_g, sums):
    sds = jax.ShapeDtypeStruct
    shapes = [
        sds((1088, 512), BF), sds((1088, 512), F32), sds((2, 68), F32), sds((2, 68), F32),
        sds((4, 68), F32), sds((68, 3264), F32), sds((68, 1088), F32), sds((68, 2176), F32),
        sds((1, 136), F32), sds((68, 2176), F32),
    ]
    vmem = pl.BlockSpec(memory_space=pltpu.VMEM)
    hbm = pl.BlockSpec(memory_space=pltpu.HBM)
    given = (mixed, tokens_grad, out_g, in_g, qkv_g, proj_g, sums)
    got = pl.pallas_call(
        finish_kernel, out_shape=shapes, in_specs=[hbm] * 7, out_specs=[vmem] * len(shapes),
        scratch_shapes=[pltpu.VMEM(v.shape, v.dtype) for v in given] + [
            pltpu.VMEM((8, 2176), F32), pltpu.SemaphoreType.DMA((7,))],
        compiler_params=pltpu.CompilerParams(vmem_limit_bytes=63 << 20), name="finish",
    )(*given)
    return (got[0].T[None], got[1].T[None]) + tuple(got[2:9]) + (got[9].T,)


def fused(tokens, segment_ids, norm_gains, norm_shifts, biases, w_qkv, w_o, w_in, b_in, w_out,
          cotangent):
    saved = run_forward(tokens, segment_ids, norm_gains, norm_shifts, biases, w_qkv, w_o, w_in,
                        b_in, w_out, cotangent)
    sums = run_backward(saved)
    return finish(*sums)


def per_device(
    tokens, segment_ids, norm_gains, norm_shifts, biases, w_qkv, w_o, w_in, b_in, w_out, cotangent
):
    rows_here = tokens.shape[1]
    score_scale = HEAD_DIM ** (-0.5)
    gains_full, shifts_full, bias_full, qkv_full, proj_full, up_full, down_full = (
        lax.all_gather(norm_gains, "shard", axis=1, tiled=True),
        lax.all_gather(norm_shifts, "shard", axis=1, tiled=True),
        lax.all_gather(biases, "shard", axis=1, tiled=True),
        lax.all_gather(w_qkv, "shard", axis=0, tiled=True),
        lax.all_gather(w_o, "shard", axis=0, tiled=True),
        lax.all_gather(w_in, "shard", axis=0, tiled=True),
        lax.all_gather(w_out, "shard", axis=1, tiled=True),
    )
    gains_full = gains_full.astype(jnp.float32)
    shifts_full = shifts_full.astype(jnp.float32)
    bias_full = bias_full.astype(jnp.float32)
    hidden = tokens[0].astype(jnp.float32)
    normed, norm_back_one = jax.vjp(layer_norm, hidden, gains_full[0], shifts_full[0])
    normed_low = normed.astype(jnp.bfloat16)
    projected = jnp.dot(normed_low, qkv_full, preferred_element_type=jnp.float32)
    queries = (projected[:, :D] + bias_full[0]).astype(jnp.bfloat16)
    key_rows = projected[:, D : 2 * D].astype(jnp.bfloat16)
    value_rows = (projected[:, 2 * D :] + bias_full[1]).astype(jnp.bfloat16)
    all_keys, all_values = (
        lax.all_gather(key_rows, "ctx", axis=0, tiled=True),
        lax.all_gather(value_rows, "ctx", axis=0, tiled=True),
    )
    seq_length = all_keys.shape[0]
    offset = lax.axis_index("ctx") * rows_here
    key_segments = segment_ids[0]
    query_segments = lax.dynamic_slice_in_dim(key_segments, offset, rows_here)
    query_position = offset + lax.iota(jnp.int32, rows_here)
    key_position = lax.iota(jnp.int32, seq_length)
    allowed = (key_position[None, :] <= query_position[:, None]) & (
        key_segments[None, :] == query_segments[:, None]
    )
    query_heads = split_heads(queries)
    key_heads = split_heads(all_keys)
    value_heads = split_heads(all_values)

    def head_scores(query_head, key_head):
        scores = (
            jnp.einsum("qd,kd->qk", query_head, key_head, preferred_element_type=jnp.float32)
            * score_scale
        )
        return jnp.where(allowed, scores, -1e30)

    def head_forward(operands):
        query_head, key_head, value_head = operands
        masked = head_scores(query_head, key_head)
        highest = jnp.max(masked, axis=1, keepdims=True)
        weights = jnp.exp(masked - highest)
        summed = jnp.sum(weights, axis=1, keepdims=True)
        probabilities = (weights / summed).astype(jnp.bfloat16)
        result = jnp.dot(probabilities, value_head, preferred_element_type=jnp.float32)
        return (result, (highest + jnp.log(summed))[:, 0])

    head_out, log_total = lax.map(head_forward, (query_heads, key_heads, value_heads))
    attended = merge_heads(head_out).astype(jnp.bfloat16)
    middle = (
        hidden + jnp.dot(attended, proj_full, preferred_element_type=jnp.float32) + bias_full[2]
    )
    normed_two, norm_back_two = jax.vjp(layer_norm, middle, gains_full[1], shifts_full[1])
    normed_two_low = normed_two.astype(jnp.bfloat16)
    mlp_inputs = lax.all_gather(normed_two_low, "tp", axis=0, tiled=True)
    inner_values = jnp.dot(mlp_inputs, up_full, preferred_element_type=jnp.float32) + b_in.astype(
        jnp.float32
    )
    active, gelu_back = jax.vjp(gelu_tanh, inner_values)
    active_low = active.astype(jnp.bfloat16)
    mixed_rows = (
        middle
        + lax.psum_scatter(
            jnp.dot(active_low, down_full, preferred_element_type=jnp.float32).astype(jnp.bfloat16),
            "tp",
            scatter_dimension=0,
            tiled=True,
        ).astype(jnp.float32)
        + bias_full[3]
    )
    mixed_out = mixed_rows.astype(jnp.bfloat16)[None]
    grad_low = cotangent[0]
    grad_out = grad_low.astype(jnp.float32)
    grad_rows = lax.all_gather(grad_low, "tp", axis=0, tiled=True)
    down_grad = contract_rows(active_low, grad_rows)
    out_bias_grad = jnp.sum(grad_out, axis=0)
    active_grad = contract_cols(grad_rows, down_full)
    inner_grad = gelu_back(active_grad)[0].astype(jnp.bfloat16)
    up_grad = contract_rows(mlp_inputs, inner_grad)
    in_bias_grad = jnp.sum(inner_grad.astype(jnp.float32), axis=0)
    normed_two_grad = lax.psum_scatter(
        contract_cols(inner_grad, up_full), "tp", scatter_dimension=0, tiled=True
    )
    middle_part, gain_two_grad, shift_two_grad = norm_back_two(normed_two_grad)
    middle_grad = grad_out + middle_part
    branch_grad = middle_grad.astype(jnp.bfloat16)
    proj_grad = contract_rows(attended, branch_grad)
    attn_bias_grad = jnp.sum(branch_grad.astype(jnp.float32), axis=0)
    attended_grad = split_heads(contract_cols(branch_grad, proj_full).astype(jnp.bfloat16))

    def head_backward(operands):
        query_head, key_head, value_head, grad_head, log_head = operands
        masked = head_scores(query_head, key_head)
        probabilities = jnp.exp(masked - log_head[:, None])
        probs_grad = jnp.einsum(
            "qd,kd->qk", grad_head, value_head, preferred_element_type=jnp.float32
        )
        row_terms = jnp.sum(probabilities * probs_grad, axis=1, keepdims=True)
        scores_grad = (probabilities * (probs_grad - row_terms)).astype(jnp.bfloat16)
        query_grad = (
            jnp.dot(scores_grad, key_head, preferred_element_type=jnp.float32) * score_scale
        )
        key_grad = (
            jnp.einsum("qk,qd->kd", scores_grad, query_head, preferred_element_type=jnp.float32)
            * score_scale
        )
        value_grad = jnp.einsum(
            "qk,qd->kd",
            probabilities.astype(jnp.bfloat16),
            grad_head,
            preferred_element_type=jnp.float32,
        )
        return (query_grad, key_grad, value_grad)

    query_grads, key_grads, value_grads = lax.map(
        head_backward, (query_heads, key_heads, value_heads, attended_grad, log_total)
    )
    key_summed, value_summed = (
        lax.psum_scatter(
            merge_heads(key_grads).astype(jnp.bfloat16), "ctx", scatter_dimension=0, tiled=True
        ).astype(jnp.float32),
        lax.psum_scatter(
            merge_heads(value_grads).astype(jnp.bfloat16), "ctx", scatter_dimension=0, tiled=True
        ).astype(jnp.float32),
    )
    query_low = merge_heads(query_grads).astype(jnp.bfloat16)
    value_low = value_summed.astype(jnp.bfloat16)
    qkv_grad = jnp.concatenate([query_low, key_summed.astype(jnp.bfloat16), value_low], axis=1)
    qkv_weight_grad = contract_rows(normed_low, qkv_grad)
    query_bias_grad = jnp.sum(query_low.astype(jnp.float32), axis=0)
    value_bias_grad = jnp.sum(value_low.astype(jnp.float32), axis=0)
    normed_grad = contract_cols(qkv_grad, qkv_full)
    hidden_part, gain_one_grad, shift_one_grad = norm_back_one(normed_grad)
    tokens_grad = (middle_grad + hidden_part)[None]
    gains_grad = jnp.stack([gain_one_grad, gain_two_grad])
    shifts_grad = jnp.stack([shift_one_grad, shift_two_grad])
    biases_grad = jnp.stack([query_bias_grad, value_bias_grad, attn_bias_grad, out_bias_grad])
    gains_grad, shifts_grad, biases_grad, qkv_weight_grad, proj_grad = lax.psum(
        (gains_grad, shifts_grad, biases_grad, qkv_weight_grad, proj_grad), "tp"
    )
    (
        gains_grad,
        shifts_grad,
        biases_grad,
        qkv_weight_grad,
        proj_grad,
        up_grad,
        in_bias_grad,
        down_grad,
    ) = (
        lax.psum_scatter(gains_grad, ("shard", "ctx"), scatter_dimension=1, tiled=True),
        lax.psum_scatter(shifts_grad, ("shard", "ctx"), scatter_dimension=1, tiled=True),
        lax.psum_scatter(biases_grad, ("shard", "ctx"), scatter_dimension=1, tiled=True),
        lax.psum_scatter(qkv_weight_grad, ("shard", "ctx"), scatter_dimension=0, tiled=True),
        lax.psum_scatter(proj_grad, ("shard", "ctx"), scatter_dimension=0, tiled=True),
        lax.psum_scatter(up_grad, ("shard", "ctx"), scatter_dimension=0, tiled=True),
        lax.psum_scatter(in_bias_grad, ("shard", "ctx"), scatter_dimension=0, tiled=True),
        lax.psum_scatter(down_grad, ("shard", "ctx"), scatter_dimension=1, tiled=True),
    )
    return (
        mixed_out,
        tokens_grad,
        gains_grad,
        shifts_grad,
        biases_grad,
        qkv_weight_grad,
        proj_grad,
        up_grad,
        in_bias_grad[None],
        down_grad,
    )


def solution(mesh):
    in_specs = (
        P(("shard", "tp"), "ctx", None),
        P(("shard", "tp"), None),
        P(None, "shard"),
        P(None, "shard"),
        P(None, "shard"),
        P("shard", None),
        P("shard", None),
        P("shard", "tp"),
        P("tp"),
        P("tp", "shard"),
        P(("shard", "tp"), "ctx", None),
    )
    out_specs = (
        P(("shard", "tp"), "ctx", None),
        P(("shard", "tp"), "ctx", None),
        P(None, ("shard", "ctx")),
        P(None, ("shard", "ctx")),
        P(None, ("shard", "ctx")),
        P(("shard", "ctx"), None),
        P(("shard", "ctx"), None),
        P(("shard", "ctx"), "tp"),
        P("tp", ("shard", "ctx")),
        P("tp", ("shard", "ctx")),
    )
    fits = dict(mesh.shape) == {"shard": 8, "ctx": 2, "tp": 2}
    return jax.shard_map(
        fused if fits else per_device, mesh=mesh, in_specs=in_specs, out_specs=out_specs, check_vma=False
    )
```

```python
import math

import jax
import jax.numpy as jnp
from jax import lax
from jax.experimental import pallas as pl
from jax.experimental.pallas import tpu as pltpu
from jax.sharding import PartitionSpec as P

D = 1088
HEADS = 17
HEAD_DIM = 64


def layer_norm(values, gain_row, shift_row):
    center = jnp.mean(values, axis=-1, keepdims=True)
    spread = values - center
    variance = jnp.mean(spread * spread, axis=-1, keepdims=True)
    return spread * lax.rsqrt(variance + 1e-05) * gain_row + shift_row


def gelu_tanh(values):
    return (
        0.5
        * values
        * (
            1.0
            + jnp.tanh(math.sqrt(2.0 / math.pi) * (values + 0.044715 * values * values * values))
        )
    )


def contract_rows(left_side, right_side):
    return lax.dot_general(
        left_side, right_side, (((0,), (0,)), ((), ())), preferred_element_type=jnp.float32
    )


def contract_cols(left_side, right_side):
    return lax.dot_general(
        left_side, right_side, (((1,), (1,)), ((), ())), preferred_element_type=jnp.float32
    )


def split_heads(matrix):
    return matrix.reshape(matrix.shape[0], HEADS, HEAD_DIM).transpose(1, 0, 2)


def merge_heads(stacked):
    return stacked.transpose(1, 0, 2).reshape(stacked.shape[1], D)


BF = jnp.bfloat16
F32 = jnp.float32
MESH = pl.DeviceIdType.MESH
EPS = 1e-05
BR = 144
UNIT = 128


def mm(left, right):
    return jnp.dot(left, right, preferred_element_type=F32)


def remote(src, dst, send, recv, device):
    return pltpu.make_async_remote_copy(
        src_ref=src, dst_ref=dst, send_sem=send, recv_sem=recv,
        device_id=device, device_id_type=MESH,
    )


class Place:
    def __init__(self):
        self.s = lax.axis_index("shard")
        self.c = lax.axis_index("ctx")
        self.t = lax.axis_index("tp")
        self.z = self.s // 2
        self.x = self.s - 2 * self.z
        self.xb = 1 - self.x
        self.tb = 1 - self.t
        z = self.z
        self.peers = [
            z + 1 - 2 * lax.rem(z, 2),
            jnp.where(z < 2, 2, 1),
            jnp.where(z < 2, 3, 0),
        ]
        self.core = (self.s, 1 - self.c, self.t)
        self.xdev = (2 * z + self.xb, self.c, self.t)
        self.ydev = (self.s, self.c, self.tb)

    def zdev(self, zp):
        return (2 * zp + self.x, self.c, self.t)

    def greet(self):
        barrier = pltpu.get_barrier_semaphore()
        devices = [self.core, self.xdev, self.ydev] + [self.zdev(p) for p in self.peers]
        for device in devices:
            pl.semaphore_signal(barrier, inc=1, device_id=device, device_id_type=MESH)
        pl.semaphore_wait(barrier, len(devices))


def rows_of(s):
    return pl.ds(pl.multiple_of(s * BR, 16), BR)


class Gather:
    def __init__(self, here, number, own, loc, route, send, recv):
        self.h, self.p, self.own, self.loc, self.route = here, number, own, loc, route
        self.send, self.recv = send, recv
        self.two, self.three = (
            (here.ydev, here.xdev) if route == "zyx" else (here.xdev, here.ydev))
        if route == "zx":
            self.three = None

    def copy(self, src, s, t, device, i):
        return remote(src, self.loc(s, t), self.send.at[self.p, i],
                      self.recv.at[self.p, s * 2 + t], device)

    def take(self, s, t):
        ref = self.loc(s, t)
        self.copy(ref, s, t, self.h.core, 0).wait_recv()

    def along(self, k):
        h = self.h
        to = h.z + jnp.where(h.peers[k] < h.z, 1, -1)
        return (to >= 0) & (to <= 3), h.zdev(jnp.clip(to, 0, 3))

    def own_z(self):
        h = self.h
        pl.when(h.z < 3)(self.copy(self.own, h.s, h.t, h.zdev(jnp.minimum(h.z + 1, 3)), 0).start)
        pl.when(h.z > 0)(self.copy(self.own, h.s, h.t, h.zdev(jnp.maximum(h.z - 1, 0)), 1).start)

    def own_two(self):
        self.copy(self.own, self.h.s, self.h.t, self.two, 5).start()

    def own_three(self):
        if self.route in ("zxy", "zyx"):
            self.copy(self.own, self.h.s, self.h.t, self.three, 10).start()

    def z(self, k):
        h = self.h
        s = 2 * h.peers[k] + h.x
        self.take(s, h.t)
        block = self.loc(s, h.t)
        on, device = self.along(k)
        pl.when(on)(self.copy(block, s, h.t, device, 2 + k).start)
        self.copy(block, s, h.t, self.two, 6 + k).start()
        if self.three:
            self.copy(block, s, h.t, self.three, 11 + k).start()

    def second(self, k):
        h = self.h
        zp = ([h.z] + h.peers)[k]
        s, t = (2 * zp + h.x, h.tb) if self.route == "zyx" else (2 * zp + h.xb, h.t)
        self.take(s, t)
        if self.three:
            self.copy(self.loc(s, t), s, t, self.three, 14 + k).start()

    def third(self, k):
        h = self.h
        zp = ([h.z] + h.peers)[k]
        if self.route == "zyx":
            self.take(2 * zp + h.xb, h.t)
            self.take(2 * zp + h.xb, h.tb)
        elif self.three:
            if not (self.route == "kv" and k == 0):
                self.take(2 * zp + h.x, h.tb)
            self.take(2 * zp + h.xb, h.tb)

    def drain(self):
        h = self.h

        def sent(i):
            return self.copy(self.own, h.s, h.t, h.core, i).wait_send

        pl.when(h.z < 3)(sent(0))
        pl.when(h.z > 0)(sent(1))
        for k in range(3):
            pl.when(self.along(k)[0])(sent(2 + k))
        for i in range(5, 9):
            sent(i)()
        if self.three:
            for i in range(10 if self.route != "kv" else 11, 18):
                sent(i)()


def real_features():
    lane = lax.broadcasted_iota(jnp.int32, (1, 1152), 1)
    return (lax.rem(lane, BR) < 136).astype(F32)


def normalise(x, mask, gain, shift, count):
    mean = jnp.sum(x, axis=1, keepdims=True) * (1.0 / count)
    spread = (x - mean) * mask
    var = jnp.sum(spread * spread, axis=1, keepdims=True) * (1.0 / count)
    return spread * lax.rsqrt(var + EPS) * gain + shift


def forward_kernel(
    seg, gains, shifts, biases, b_in, tok_h, cot_h, w_qkv_h, w_o_h, w_in_h, w_out_h,
    wa_o, wo_o, wi_o, wu_o, n1t_o, n2t_o, cot_o, qn_o, kn_o, vn_o, qt_o, kt_o, ot_o,
    lse_o, mid_o, slope_o, act_o, go_o, par_o, mb_o, x_o,
    wa, wog, wo, wi, wu, n1, cot, cott, n2, sm, par, bins, qn, kn, vn, qt, kt, vt, mb, ot, att, mid,
    slope, act, tile, stage, lse, x_ref, segr, segc,
    tok, cot_in, w_qkv, w_o, w_in, w_out, spread,
    send, recv, dsend, drecv, ssend, srecv, lsem, osem, isem,
):
    h = Place()
    c, s, t = h.c, h.s, h.t
    rows = 512
    length = 2 * rows
    count = 1088
    own = pl.ds(pl.multiple_of(c * rows, rows), rows)
    sib = pl.ds(pl.multiple_of((1 - c) * rows, rows), rows)

    def piece(number, buf, route, col, width):
        def loc(sp, tp):
            where = col(tp)
            if not isinstance(where, int):
                where = pl.multiple_of(where, UNIT)
            return buf.at[rows_of(sp), pl.ds(where, width)]

        return Gather(h, number, loc(s, t), loc, route, send, recv)

    A = ([piece(0, wa, "zx", lambda tp: 0, 512),
          piece(1, wa, "kv", lambda tp: 512 + 512 * tp, 512)],
         [piece(7, wa, "zx", lambda tp: 1536, 128),
          piece(8, wa, "kv", lambda tp: 1664 + 128 * tp, 128)])
    O = ([piece(2, wog.at[c], "zx", lambda tp: 0, 512)],
         [piece(9, wog.at[c], "zx", lambda tp: 512, 128)])
    I = ([piece(3, wi, "zxy", lambda tp: 1024 * tp, 640),
          piece(4, wi, "zyx", lambda tp: 1024 * tp + 640, 384)],
         [piece(10, wi, "zyx", lambda tp: 2048 + 128 * tp, 128)])
    U = ([piece(5, wu, "zxy", lambda tp: 1024 * tp, 640),
          piece(6, wu, "zyx", lambda tp: 1024 * tp + 640, 384)],
         [piece(11, wu, "zyx", lambda tp: 2048 + 128 * tp, 128)])

    def each(group, stage, *args):
        for p in group[0]:
            getattr(p, stage)(*args)

        @pl.when(c == 0)
        def _():
            for p in group[1]:
                getattr(p, stage)(*args)

    def small_copy(sp, device, i):
        return remote(sm.at[sp], sm.at[sp], ssend.at[i], srecv.at[sp], device)

    loads = [pltpu.make_async_copy(src, dst, lsem.at[n]) for n, (src, dst) in enumerate((
        (w_qkv_h, w_qkv), (w_o_h, w_o), (tok_h, tok), (w_in_h, w_in), (w_out_h, w_out),
        (cot_h, cot_in)))]
    for copy in loads:
        copy.start()
    wide = lambda v: v.astype(F32)

    def deep(v):
        return jnp.concatenate([v, jnp.zeros((8, v.shape[1]), F32)], axis=0).astype(BF)

    def either(make):
        pl.when(c == 0)(lambda: make(0))
        pl.when(c == 1)(lambda: make(1))

    @pl.when(c == 1)
    def _():
        wi[:, 2048:2304] = jnp.zeros((1152, 256), BF)
        wu[:, 2048:2304] = jnp.zeros((1152, 256), BF)
        wa[:, 1536:1920] = jnp.zeros((1152, 384), BF)

    sm[s] = jnp.zeros((8, 256), F32)
    sm[s, 0:2, 0:136] = wide(gains[...])
    sm[s, 2:4, 0:136] = wide(shifts[...])
    sm[s, 4:8, 0:136] = wide(biases[...])
    loads[0].wait()

    def columns(core):
        for i in range(3):
            base = 1088 * i + 576 * core
            wa[rows_of(s), 512 * i:512 * i + 512] = deep(wide(w_qkv[:, base:base + 512]))
            if core == 0:
                wa[rows_of(s), 1536 + 128 * i:1664 + 128 * i] = deep(jnp.concatenate(
                    [wide(w_qkv[:, base + 512:base + 576]), jnp.zeros((136, 64), F32)], axis=1))

    either(columns)
    h.greet()
    for i, zp in enumerate(h.peers):
        small_copy(s, h.zdev(zp), i).start()
    small_copy(s, h.xdev, 3).start()
    each(A, "own_z")
    each(A, "own_two")
    feature = lax.broadcasted_iota(jnp.int32, (1088, 1), 0)
    place = feature + 8 * (feature // 136)
    spread[...] = (lax.broadcasted_iota(jnp.int32, (1088, 1152), 1) == place).astype(BF)
    loads[1].wait()

    def o_columns(core):
        at = slice(512 * core, 512 * core + 512)
        wog[core, rows_of(s), 0:512] = deep(mm(w_o[...], spread[:, at]))
        if core == 0:
            wog[core, rows_of(s), 512:640] = deep(mm(w_o[...], spread[:, 1024:1152]))

    either(o_columns)
    each(O, "own_z")
    for copy in loads[3:5]:
        copy.wait()

    def own_units(core):
        low = 1152 * core
        for src, dst in ((w_in, wi), (w_out, wu)):
            dst[rows_of(s), pl.ds(pl.multiple_of(t * 1024, UNIT), 1024)] = deep(
                wide(src[:, low:low + 1024]))
            if core == 0:
                dst[rows_of(s), pl.ds(pl.multiple_of(2048 + t * 128, UNIT), 128)] = deep(
                    wide(src[:, 1024:1152]))
        size = 1152 - 128 * core
        bins[t, :, 0:size] = jnp.broadcast_to(wide(b_in[0:1, low:low + size]), (8, size))
        if core == 1:
            bins[t, :, 1024:1152] = jnp.zeros((8, 128), F32)

    either(own_units)
    bin_copy = remote(bins.at[t], bins.at[t], ssend.at[7], srecv.at[8], h.ydev)
    bin_copy.start()
    each(I, "own_three")

    def spread_out(src, dst, to):
        @pl.loop(0, 3)
        def _(i):
            at = pl.ds(pl.multiple_of(384 * i, UNIT), 384)
            dst[to, at] = lax.dot_general(
                src[...], spread[:, at], (((0,), (0,)), ((), ())), preferred_element_type=F32
            ).astype(BF)

    loads[2].wait()
    spread_out(tok, x_ref, pl.ds(0, rows))
    ids = jnp.broadcast_to(seg[...], (8, 1024))
    segr[...] = ids
    segc[...] = ids.T

    top = 0
    for b in range(4):
        first = max(0, b - 2)
        width = (b + 1 - first) * 256
        kpos = lax.broadcasted_iota(jnp.int32, (width, 256), 0) + first * 256
        qpos = lax.broadcasted_iota(jnp.int32, (width, 256), 1) + b * 256
        seen = (kpos <= qpos) & (
            segc[first * 256:first * 256 + width, 0:1] == segr[0:1, b * 256:b * 256 + 256]
        )
        mb[top:top + width, :] = jnp.where(seen, 0.0, -1e30)
        top += width

    for k, zp in enumerate(h.peers):
        sp = 2 * zp + h.x
        small_copy(sp, h.xdev, 4 + k).wait_recv()
        small_copy(sp, h.xdev, 4 + k).start()
    each(A, "z", 0)
    for zp in [h.z] + h.peers:
        small_copy(2 * zp + h.xb, h.xdev, 0).wait_recv()

    padded = jnp.zeros((8, 1152), F32)
    natural = jnp.zeros((8, 1152), F32)
    for sp in range(8):
        wide = jnp.concatenate([sm[sp], jnp.zeros((8, 896), F32)], axis=1)
        padded = padded + (pltpu.roll(wide, 144 * sp, 1) if sp else wide)
        natural = natural + (pltpu.roll(wide, 136 * sp, 1) if sp else wide)
    par[0:8] = padded
    shifted = pltpu.roll(natural, 576, 1)
    par[8:16] = jnp.where(c == 0, natural, shifted)
    mask = real_features()
    each(A, "second", 0)
    loads[5].wait()
    spread_out(cot_in, cot, own)
    cot_copy = remote(cot.at[own], cot.at[own], dsend.at[0], drecv.at[0], h.core)
    cot_copy.start()

    @pl.loop(0, rows // 128)
    def _(i):
        at = pl.ds(pl.multiple_of(i * 128, 128), 128)
        to = pl.ds(pl.multiple_of(c * rows + i * 128, 128), 128)
        n1[to, :] = normalise(
            x_ref[at, :].astype(F32), mask, par[0:1, :], par[2:3, :], count
        ).astype(BF)

    n1_copy = remote(n1.at[own], n1.at[own], dsend.at[1], drecv.at[1], h.core)
    n1_copy.start()

    outs = []

    def flush(src, dst):
        copy = pltpu.make_async_copy(src, dst, osem.at[len(outs)])
        copy.start()
        outs.append(copy)

    flush(par, par_o)
    flush(mb, mb_o)
    flush(x_ref, x_o)

    def turn(src, dst, i, later):
        slot = i % 2
        if later:
            pltpu.make_async_copy(stage.at[slot], dst.at[:, 0:256], isem.at[slot]).wait()
        stage[slot] = src[256 * i:256 * i + 256, :].T
        pltpu.make_async_copy(
            stage.at[slot], dst.at[:, pl.ds(256 * i, 256)], isem.at[slot]).start()

    each(A, "z", 1)
    each(I, "own_z")
    each(A, "second", 1)
    cot_copy.wait_recv()
    flush(cot, cot_o)
    for i in range(2):
        cott[:, 256 * i:256 * i + 256] = cot[256 * i:256 * i + 256, :].T
    each(A, "z", 2)
    each(O, "own_two")
    each(O, "z", 0)
    each(A, "second", 2)
    n1_copy.wait_recv()
    for i in range(2):
        turn(n1, n1t_o, i, False)
    each(O, "z", 1)
    each(A, "second", 3)
    each(O, "z", 2)
    each(I, "own_two")
    each(I, "z", 0)

    def project(i, col, width, name, first_head):
        at = pl.ds(pl.multiple_of(i * 512, 512), 512)
        got = mm(n1[at, :], wa[:, col:col + width])
        where = 64 * first_head
        if name != "k":
            row = 12 if name == "q" else 13
            got = got + par[row:row + 1, where:where + width]
        low = got.astype(BF)
        if name == "q":
            low = low * jnp.asarray(0.125, BF)
        natural_ref, turned = {"q": (qn, qt), "k": (kn, kt), "v": (vn, vt)}[name]
        turned[where:where + width, at] = low.T
        natural_ref[at, where:where + width] = low

    for j in range(2):
        @pl.loop(0, 2)
        def _(i):
            project(i, 256 * j, 256, "q", 4 * j)
    for k in range(4):
        each(A, "third", k)
    for name, col in (("k", 512), ("v", 1024)):
        for j in range(2):
            @pl.loop(0, 2)
            def _(i):
                project(i, col + 256 * j, 256, name, 4 * j)
    each(I, "z", 1)
    each(U, "own_z")
    each(I, "second", 0)

    @pl.when(c == 0)
    def _():
        for name, col in (("q", 1536), ("k", 1664), ("v", 1792)):
            @pl.loop(0, 2)
            def _(i):
                project(i, col, 128, name, 8)

    @pl.when(c == 1)
    def _():
        for turned in (qt, kt, vt):
            turned[512:640, :] = jnp.zeros((128, length), BF)
        for natural_ref in (qn, kn, vn):
            natural_ref[:, 512:640] = jnp.zeros((length, 128), BF)

    flush(wa, wa_o)
    for src, dst in ((qn, qn_o), (kn, kn_o), (vn, vn_o), (qt, qt_o), (kt, kt_o)):
        flush(src, dst)
    lse[...] = jnp.zeros_like(lse)
    ot[c, 512:640, :] = jnp.zeros((128, length), BF)

    def attend(head):
        feat = pl.ds(pl.multiple_of(head * 64, 64), 64)
        pair = pl.ds(pl.multiple_of(head // 2 * 128, 128), 128)
        mine = lax.broadcasted_iota(jnp.int32, (128, 256), 0) // 64 == lax.rem(head, 2)
        top = 0
        for b in range(4):
            first = max(0, b - 2)
            width = (b + 1 - first) * 256
            keys = slice(first * 256, first * 256 + width)
            cols = slice(b * 256, b * 256 + 256)
            scores = mm(kn[keys, pair], jnp.where(mine, qt[pair, cols], jnp.zeros((), BF)))
            scores = scores + mb[top:top + width, :]
            top += width
            highest = jnp.max(scores, axis=0, keepdims=True)
            weights = jnp.exp(scores - highest)
            total = jnp.sum(weights, axis=0, keepdims=True)
            probs = (weights * (1.0 / total)).astype(BF)
            ot[c, feat, cols] = mm(vt[feat, keys], probs).astype(BF)
            lse[pl.ds(head, 1), cols] = highest + jnp.log(total)

    def heads(low, high):
        @pl.loop(low, high)
        def _(head):
            attend(head)

    each(I, "z", 2)
    each(O, "second", 0)
    heads(0, 2)
    each(O, "second", 1)
    each(O, "second", 2)
    each(I, "second", 1)
    each(U, "own_two")
    each(U, "own_three")
    heads(2, 4)
    each(O, "second", 3)
    wo_copy = remote(wog.at[c], wog.at[c], dsend.at[2], drecv.at[2], h.core)
    wo_copy.start()
    each(I, "second", 2)
    each(U, "z", 0)
    heads(4, 6)
    each(I, "second", 3)
    each(I, "third", 0)
    each(U, "z", 1)
    heads(6, 9 - c)
    each(U, "second", 0)
    each(I, "third", 1)
    each(U, "z", 2)

    flush(lse, lse_o)
    for i in range(2):
        at = pl.ds(pl.multiple_of(c * rows + 256 * i, 256), 256)
        att[c, 256 * i:256 * i + 256, :] = ot[c, :, at].T
    for i in range(2):
        at = pl.ds(pl.multiple_of((1 - c) * rows + 256 * i, 256), 256)
        vt[256 * i:256 * i + 256, 0:640] = ot[c, :, at].T
    att_copy = remote(vt.at[0:rows, 0:640], att.at[c], dsend.at[3], drecv.at[3], h.core)
    att_copy.start()
    ot_copy = remote(ot.at[c], ot.at[c], dsend.at[4], drecv.at[4], h.core)
    ot_copy.start()
    each(U, "second", 1)

    wo_copy.wait_recv()

    def order_rows(half, src, to, width):
        for sp in range(8):
            slope[136 * sp:136 * sp + 136, 0:width] = (
                wog[half, 144 * sp:144 * sp + 144, src:src + width].astype(F32)[0:136])
        wo[0:576, to:to + width] = slope[0:576, 0:width].astype(BF)
        wo[640:1152, to:to + width] = slope[576:1088, 0:width].astype(BF)

    for half in range(2):
        for q in range(2):
            order_rows(half, 256 * q, 512 * half + 256 * q, 256)
    order_rows(0, 512, 1024, 128)
    wo[576:640, :] = jnp.zeros((64, 1152), BF)
    wo[1152:1280, :] = jnp.zeros((128, 1152), BF)
    flush(wo.at[pl.ds(pl.multiple_of(c * 640, 128), 640)], wo_o)
    att_copy.wait_recv()
    att_copy.wait_send()
    each(I, "third", 2)

    @pl.loop(0, 4)
    def _(i):
        at = pl.ds(pl.multiple_of(i * 128, 128), 128)
        to = pl.ds(pl.multiple_of(c * rows + i * 128, 128), 128)
        x = (
            x_ref[at, :].astype(F32)
            + (mm(att[0, at, :], wo[0:640, :]) + mm(att[1, at, :], wo[640:1280, :]))
            + par[6:7, :]
        )
        mid[at, :] = x
        n2[to, :] = normalise(x, mask, par[1:2, :], par[3:4, :], count).astype(BF)

    flush(mid, mid_o)
    n2_copy = remote(n2.at[own], n2.at[own], dsend.at[5], drecv.at[5], h.core)
    n2_copy.start()
    ot_copy.wait_recv()
    flush(ot, ot_o)
    for i in range(2, 4):
        cott[:, 256 * i:256 * i + 256] = cot[256 * i:256 * i + 256, :].T
        turn(n1, n1t_o, i, True)
    n2_copy.wait_recv()
    for i in range(4):
        turn(n2, n2t_o, i, True)
    each(I, "third", 3)
    flush(wi, wi_o)
    bin_copy.wait_recv()
    root = math.sqrt(2.0 / math.pi)

    def slot_copies(slot, cols):
        base = pl.multiple_of(1024 * slot, 1024)
        return (
            pltpu.make_async_copy(slope.at[pl.ds(base, 1024)], slope_o.at[:, cols], isem.at[2 + slot]),
            pltpu.make_async_copy(act.at[slot], act_o.at[:, cols], isem.at[4 + slot]),
            pltpu.make_async_copy(tile.at[slot], go_o.at[:, :, :, cols], isem.at[6 + slot]),
        )

    def hidden(i):
        j = jnp.where(i < 4, 4 * h.tb + i, jnp.where(i < 8, 4 * t + i - 4, 8))
        slot = lax.rem(i, 2)
        base = pl.multiple_of(1024 * slot, 1024)
        cols = pl.ds(pl.multiple_of(j * 256, 256), 256)

        @pl.when(i >= 2)
        def _():
            for copy in slot_copies(slot, cols):
                copy.wait()
        half = j // 4
        off = pl.multiple_of(256 * (j - 4 * half), 256)
        bias = jnp.where(
            j < 8,
            bins[pl.ds(jnp.minimum(half, 1), 1), 0:1, pl.ds(jnp.where(j < 8, off, 0), 256)][0],
            jnp.concatenate([bins[0, 0:1, 1024:1152], bins[1, 0:1, 1024:1152]], axis=1),
        )

        @pl.loop(0, 4)
        def _(q):
            at = pl.ds(pl.multiple_of(q * 256, 256), 256)
            v = mm(n2[at, :], wi[:, cols]) + bias
            square = v * v
            bent = jnp.tanh(root * (v + 0.044715 * square * v))
            act[slot, at, :] = (0.5 * v * (1.0 + bent)).astype(BF)
            slope[pl.ds(pl.multiple_of(base + 256 * q, 256), 256), :] = (
                0.5 * (1.0 + bent) + (0.5 * root) * v * (1.0 - bent * bent) * (
                    1.0 + (3.0 * 0.044715) * square))

        @pl.loop(0, 2)
        def _(half):
            got = mm(cott[pl.ds(pl.multiple_of(576 * half, 576), 576), :], act[slot])
            for q in range(4):
                tile[slot, 2 * half + q // 2, q % 2] = got[144 * q:144 * q + 144, :].astype(BF)
        for copy in slot_copies(slot, cols):
            copy.start()

    def units(low, high):
        @pl.loop(low, high)
        def _(i):
            hidden(i)

    units(0, 1)
    each(U, "second", 2)
    units(1, 2)
    each(U, "second", 3)
    units(2, 4)
    each(U, "third", 0)
    units(4, 6)
    each(U, "third", 1)
    units(6, 9 - c)
    each(U, "third", 2)
    each(U, "third", 3)
    flush(wu, wu_o)
    for slot in range(2):
        for copy in slot_copies(slot, pl.ds(0, 256)):
            copy.wait()
    for slot in range(2):
        pltpu.make_async_copy(stage.at[slot], n2t_o.at[:, 0:256], isem.at[slot]).wait()
    for copy in outs:
        copy.wait()
    for i in range(7):
        small_copy(s, h.xdev, i).wait_send()
    for copy in (bin_copy, cot_copy, n1_copy, wo_copy, ot_copy, n2_copy):
        copy.wait_send()
    for group in (A, O, I, U):
        each(group, "drain")


def run_forward(tokens, segment_ids, norm_gains, norm_shifts, biases, w_qkv, w_o, w_in, b_in,
                w_out, cotangent):
    hbm = pl.BlockSpec(memory_space=pltpu.HBM)
    vmem = pl.BlockSpec(memory_space=pltpu.VMEM)
    sds = jax.ShapeDtypeStruct
    shapes = [
        sds((1152, 1920), BF), sds((640, 1152), BF), sds((1152, 2304), BF), sds((1152, 2304), BF),
        sds((1152, 1024), BF), sds((1152, 1024), BF), sds((1024, 1152), BF),
        sds((1024, 640), BF), sds((1024, 640), BF), sds((1024, 640), BF),
        sds((640, 1024), BF), sds((640, 1024), BF), sds((2, 640, 1024), BF),
        sds((16, 1024), F32), sds((512, 1152), F32), sds((1024, 2304), F32), sds((1024, 2304), BF),
        sds((4, 2, 144, 2304), BF), sds((16, 1152), F32), sds((2304, 256), F32), sds((512, 1152), BF),
    ]
    V = pltpu.VMEM
    dma = pltpu.SemaphoreType.DMA
    scratch = [
        V((1152, 1920), BF), V((2, 1152, 640), BF), V((1280, 1152), BF), V((1152, 2304), BF),
        V((1152, 2304), BF), V((1024, 1152), BF), V((1024, 1152), BF), V((1152, 1024), BF),
        V((1024, 1152), BF),
        V((8, 8, 256), F32), V((16, 1152), F32), V((2, 8, 1152), F32),
        V((1024, 640), BF), V((1024, 640), BF), V((1024, 640), BF),
        V((640, 1024), BF), V((640, 1024), BF), V((640, 1024), BF),
        V((2304, 256), F32), V((2, 640, 1024), BF), V((2, 512, 640), BF), V((512, 1152), F32),
        V((2048, 256), F32), V((2, 1024, 256), BF), V((2, 4, 2, 144, 256), BF),
        V((2, 1152, 256), BF), V((16, 1024), F32), V((512, 1152), BF), V((8, 1024), jnp.int32), V((1024, 8), jnp.int32),
        V((1088, 512), BF), V((1088, 512), BF), V((136, 3264), BF), V((136, 1088), BF),
        V((136, 2176), BF), V((136, 2176), BF), V((1088, 1152), BF),
        dma((12, 18)), dma((12, 16)), dma((6,)), dma((6,)), dma((8,)), dma((9,)), dma((12,)),
        dma((17,)), dma((8,)),
    ]
    kept = pl.pallas_call(
        forward_kernel, out_shape=shapes, in_specs=[vmem] * 5 + [hbm] * 6, out_specs=[hbm] * len(shapes),
        scratch_shapes=scratch,
        compiler_params=pltpu.CompilerParams(
            collective_id=0, has_side_effects=True, vmem_limit_bytes=63 << 20),
        cost_estimate=pl.CostEstimate(flops=12 * 10**9, bytes_accessed=60 * 10**6, transcendentals=10**7),
        name="forward",
    )(segment_ids, norm_gains, norm_shifts, biases, b_in.reshape(1, -1), tokens[0].T, cotangent[0].T,
      w_qkv, w_o, w_in, w_out.T)
    return kept


def nt(left, right):
    return lax.dot_general(left, right, (((1,), (1,)), ((), ())), preferred_element_type=F32)


def backward_kernel(
    par, lse, wa_h, wo_h, wi_h, wu_h, n1t_h, n2t_h, cot_h, qn_h, kn_h, vn_h, qt_h,
    kt_h, ot_h, mid_h, slope_h, act_h, go_h, mb_h, x_h,
    mixed_o, tokens_o, out_o, in_o, qkv_o, proj_o, sums_o,
    WI, WU, ACT, IG, COT, COTT, N2T, inner, F1, F2, F3, F4, mix, yr, xr, x1, y2, zr, gi, held, early,
    acck, accv, vyr, xra, zra, ysa, yra, go, xro, zro, yso, yro, sg, sgx, sgz, sgy, bsum,
    load, innersem, heldsem, ysend, yrecv, xsend, xrecv, isend, irecv, zsend, zrecv,
    axs, axr, azs, azr, ays, ayr, oxs, oxr, ozs, ozr, oys, oyr, gsend, grecv, dsend, drecv,
    outsem, finsend, finrecv, finloc,
):
    h = Place()
    c, s, t, z, x = h.c, h.s, h.t, h.z, h.x
    rows = 512
    count = 1088.0
    own0 = pl.multiple_of(c * rows, rows)
    sib0 = pl.multiple_of((1 - c) * rows, rows)
    n_tiles = 9 - c

    def fetch(n, src, dst):
        copy = pltpu.make_async_copy(src, dst, load.at[n])
        copy.start()
        return copy

    def tile_of(i):
        return jnp.where(i < 4, 4 * h.tb + i, jnp.where(i < 8, 4 * t + i - 4, 8))

    def inner_copy(i):
        slot = lax.rem(i, 2)
        return pltpu.make_async_copy(
            slope_h.at[:, pl.ds(pl.multiple_of(256 * tile_of(i), 256), 256)],
            inner.at[pl.ds(pl.multiple_of(1024 * slot, 1024), 1024)], innersem.at[slot])

    inner_copy(0).start()
    first = [fetch(0, cot_h, COT), fetch(1, wu_h, WU)]
    h.greet()

    @pl.when(c == 1)
    def _():
        IG[:, 2048:2304] = jnp.zeros((1024, 256), BF)
    sg[...] = jnp.zeros_like(sg)

    def cols_of(k):
        return slice(256 * k, 256 * k + 256) if k < 4 else slice(1024, 1152)

    def theirs(k):
        return pl.ds(pl.multiple_of(1024 * h.tb + 256 * k if k < 4 else 2048 + 128 * h.tb, 128),
                     256 if k < 4 else 128)

    def ours(k):
        return pl.ds(pl.multiple_of(1024 * t + 256 * k if k < 4 else 2048 + 128 * t, 128),
                     256 if k < 4 else 128)

    def slot_at(zp):
        return lax.rem(z - zp + 3, 4)

    def only(k, step):
        if k < 4:
            step()
        else:
            pl.when(c == 0)(step)

    def oy(k):
        return remote(go_h.at[:, :, :, theirs(k)], yr.at[:, :, :, cols_of(k)],
                      ysend.at[0, k], yrecv.at[0, k], h.ydev)

    def ox(k):
        cols = cols_of(k)
        return remote(yr.at[:, h.xb, :, cols], xr.at[:, :, cols], xsend.at[k], xrecv.at[k], h.xdev)

    near = h.peers[0]
    far = jnp.where(z < 2, z + 2, z - 2)

    def z_one(m, k, i):
        cols = cols_of(k)
        return remote((xr, y2)[m].at[lax.rem(near, 2) + 2 * i, :, cols], zr.at[m, i, :, cols],
                      zsend.at[m, k, i], zrecv.at[m, k, i], h.zdev(near))

    def z_two(m, k):
        cols = cols_of(k)
        return remote((xr, y2)[m].at[far, :, cols], zr.at[m, 2, :, cols],
                      zsend.at[m, k, 2], zrecv.at[m, k, 2], h.zdev(far))

    def MZ(m, k):
        def step():
            cols = cols_of(k)
            src = (xr, y2)[m]
            for i in range(2):
                z_one(m, k, i).wait_recv()
                at = lax.rem(z, 2) + 2 * i
                src[at, :, cols] = (
                    src[at, :, cols].astype(F32) + zr[m, i, :, cols].astype(F32)).astype(BF)
            z_two(m, k).start()
        only(k, step)

    def held_copy(k):
        return pltpu.make_async_copy(
            go_h.at[:, :, :, ours(k)], held.at[:, :, :, 0:256 if k < 4 else 128], heldsem.at[0])

    def OY(k):
        def step():
            cols = cols_of(k)
            width = cols.stop - cols.start
            oy(k).wait_recv()
            held_copy(k).wait()

            @pl.loop(0, 4)
            def _(zp):
                for xp in range(2):
                    yr[zp, xp, :, cols] = (
                        yr[zp, xp, :, cols].astype(F32) + held[zp, xp, :, 0:width].astype(F32)
                    ).astype(BF)
            ox(k).start()
        only(k, step)
        if k < 4:
            only(k + 1, lambda: held_copy(k + 1).start())

    def OX(k):
        def step():
            cols = cols_of(k)
            ox(k).wait_recv()

            @pl.loop(0, 4)
            def _(zp):
                xr[zp, :, cols] = (
                    xr[zp, :, cols].astype(F32) + yr[zp, x, :, cols].astype(F32)).astype(BF)
            for i in range(2):
                z_one(0, k, i).start()
        only(k, step)

    def LZ(m, k):
        def step():
            cols = cols_of(k)
            z_two(m, k).wait_recv()
            F4[144 * m:144 * m + 144, cols] = (
                (xr, y2)[m][z, :, cols].astype(F32) + zr[m, 2, :, cols].astype(F32))
        only(k, step)

    def tile_cols(i):
        return pl.ds(pl.multiple_of(256 * tile_of(i), 256), 256)

    def ix(i):
        cols = tile_cols(i)
        return remote(gi.at[:, h.xb, :, cols], x1.at[:, :, cols],
                      isend.at[i], irecv.at[i], h.xdev)

    def iy(k):
        return remote(x1.at[:, :, theirs(k)], y2.at[:, :, cols_of(k)],
                      ysend.at[1, k], yrecv.at[1, k], h.ydev)

    def IX(i):
        def step():
            cols = tile_cols(i)
            ix(i).wait_recv()

            @pl.loop(0, 4)
            def _(zp):
                x1[zp, :, cols] = (
                    x1[zp, :, cols].astype(F32) + gi[zp, x, :, cols].astype(F32)).astype(BF)
            if i < 4:
                iy(i).start()
            if i == 8:
                iy(4).start()
        only(4 if i == 8 else 0, step)

    def IY(k):
        def step():
            cols = cols_of(k)
            iy(k).wait_recv()

            @pl.loop(0, 4)
            def _(zp):
                y2[zp, :, cols] = (
                    y2[zp, :, cols].astype(F32) + x1[zp, :, ours(k)].astype(F32)).astype(BF)
            for i in range(2):
                z_one(1, k, i).start()
        only(k, step)

    for k in range(5):
        only(k, lambda: oy(k).start())
    held_copy(0).start()

    for copy in first:
        copy.wait()
    second = [fetch(3, n2t_h, N2T), fetch(4, wi_h, WI), fetch(5, mid_h, F4), fetch(2, act_h, ACT)]

    def hidden(i):
        base = pl.multiple_of(1024 * lax.rem(i, 2), 1024)
        inner_copy(i).wait()

        @pl.when(i + 1 < n_tiles)
        def _():
            inner_copy(i + 1).start()
        cols = pl.ds(pl.multiple_of(256 * tile_of(i), 256), 256)
        bsum[...] = jnp.zeros_like(bsum)

        @pl.loop(0, 4)
        def _(q):
            at = pl.ds(pl.multiple_of(256 * q, 256), 256)
            v = inner[pl.ds(pl.multiple_of(base + 256 * q, 256), 256), :]
            low = (mm(COT[at, :], WU[:, cols]) * v).astype(BF)
            IG[at, cols] = low
            bsum[0:1, :] = bsum[0:1, :] + jnp.sum(low.astype(F32), axis=0, keepdims=True)

        @pl.when(i == 0)
        def _():
            second[0].wait()

        @pl.loop(0, 2)
        def _(half):
            got = mm(N2T[pl.ds(pl.multiple_of(576 * half, 576), 576), :], IG[:, cols])
            line = lax.broadcasted_iota(jnp.int32, (16, 256), 0) == 8
            for q in range(4):
                block = got[144 * q:144 * q + 144, :]
                zp, xp = 2 * half + q // 2, q % 2
                gi[zp, xp, 0:128, cols] = block[0:128].astype(BF)
                gi[zp, xp, 128:144, cols] = jnp.where(line, bsum[0:1, :], block[128:144]).astype(BF)

        ix(i).start()

    def units(low, high):
        @pl.loop(low, high)
        def _(i):
            hidden(i)

    units(0, 5)
    OY(0)
    IX(0)
    units(5, 9 - c)
    IX(1)
    IX(2)

    for copy in second[1:]:
        copy.wait()
    @pl.when(c == 1)
    def _():
        ACT[:, 2048:2304] = jnp.zeros((1024, 256), BF)


    def n2_copy(i):
        at = pl.ds(pl.multiple_of(384 * i, 128), 384)
        return remote(F3.at[:, at], F2.at[:, at], dsend.at[i], drecv.at[i], h.core)

    @pl.loop(0, 3)
    def _(i):
        at = pl.ds(pl.multiple_of(384 * i, 128), 384)
        F3[:, at] = nt(IG[pl.ds(sib0, rows), :], WI[at, :]).astype(BF)
        n2_copy(i).start()

    @pl.loop(0, 3)
    def _(i):
        at = pl.ds(pl.multiple_of(384 * i, 128), 384)
        F1[:, at] = nt(IG[pl.ds(own0, rows), :], WI[at, :])
    n2_sends = [n2_copy(i) for i in range(3)]
    OY(1)
    IX(3)

    wo_load = fetch(6, wo_h, WI.at[0:640, 0:1152])
    q_loads = [fetch(7, qn_h, IG.at[:, 0:640]), fetch(8, kn_h, IG.at[:, 640:1280]),
               fetch(9, vn_h, IG.at[:, 1280:1920]),
               fetch(10, mb_h, inner), fetch(11, n1t_h, N2T)]


    def mix_copy(i):
        at = pl.ds(pl.multiple_of(384 * i, 128), 384)
        return remote(WI.at[640:1152, at], mix.at[:, at], dsend.at[3 + i], drecv.at[3 + i], h.core)

    @pl.loop(0, 3)
    def _(i):
        at = pl.ds(pl.multiple_of(384 * i, 128), 384)
        WI[640:1152, at] = nt(ACT[pl.ds(sib0, rows), :], WU[at, :]).astype(BF)
        mix_copy(i).start()
    mix_sends = [mix_copy(i) for i in range(3)]

    mask = real_features()
    for copy in n2_sends:
        copy.wait_recv()

    @pl.loop(0, 16)
    def _(q):
        at = pl.ds(pl.multiple_of(32 * q, 32), 32)
        to = pl.ds(pl.multiple_of(own0 + 32 * q, 32), 32)
        grad = F1[at, :] + F2[at, :].astype(F32)
        v = F4[at, :]
        mean = jnp.sum(v, axis=1, keepdims=True) * (1.0 / count)
        spread = (v - mean) * mask
        rstd = lax.rsqrt(jnp.sum(spread * spread, axis=1, keepdims=True) * (1.0 / count) + EPS)
        hat = spread * rstd
        scaled = grad * par[1:2, :]
        grad_out = COT[to, :].astype(F32)
        got = grad_out + rstd * (
            scaled - jnp.sum(scaled, axis=1, keepdims=True) * (1.0 / count)
            - hat * (jnp.sum(scaled * hat, axis=1, keepdims=True) * (1.0 / count))) * mask
        low = got.astype(BF)
        F1[at, :] = got
        COT[to, :] = low
        sg[3:4, 0:1152] = sg[3:4, 0:1152] + jnp.sum(grad * hat, axis=0, keepdims=True)
        sg[4:5, 0:1152] = sg[4:5, 0:1152] + jnp.sum(grad, axis=0, keepdims=True)
        sg[5:6, 0:1152] = sg[5:6, 0:1152] + jnp.sum(grad_out, axis=0, keepdims=True)
        sg[6:7, 0:1152] = sg[6:7, 0:1152] + jnp.sum(low.astype(F32), axis=0, keepdims=True)

    bg_copy = remote(COT.at[pl.ds(own0, rows)], COT.at[pl.ds(own0, rows)], dsend.at[6], drecv.at[6], h.core)
    bg_copy.start()
    IX(4)

    for copy in n2_sends:
        copy.wait_send()
    for copy in mix_sends:
        copy.wait_recv()

    @pl.loop(0, 3)
    def _(i):
        at = pl.ds(pl.multiple_of(384 * i, 128), 384)
        got = nt(ACT[pl.ds(own0, rows), :], WU[at, :]) + mix[:, at].astype(F32)
        F3[:, at] = (F4[:, at] + got + par[7:8, at]).astype(BF)
    mix_out = pltpu.make_async_copy(F3, mixed_o, outsem.at[0])
    mix_out.start()
    t_loads = [fetch(12, qt_h, WU.at[0:640, 0:1024]), fetch(13, kt_h, WU.at[0:640, 1024:2048])]
    OY(2)
    OX(0)
    o_loads = [fetch(14, ot_h.at[0], ACT.at[0:640, 0:1024]), fetch(15, ot_h.at[1], ACT.at[0:640, 1024:2048])]

    wo_load.wait()
    bg_copy.wait_recv()
    bg_copy.wait_send()
    for copy in mix_sends:
        copy.wait_send()

    @pl.loop(0, 5)
    def _(pair):
        at = pl.ds(pl.multiple_of(128 * pair, 128), 128)
        got = nt(COT[...], WI[at, 0:1152]).astype(BF)
        WI[0:1024, pl.ds(pl.multiple_of(1280 + 128 * pair, 128), 128)] = got
        COTT[at, :] = got.T

    IX(5)

    for copy in o_loads:
        copy.wait()

    def proj(col, to):
        part = COT[:, col]
        acck[0:576, :] = mm(ACT[0:576, 0:1024], part)
        acck[576:1088, :] = mm(ACT[0:512, 1024:2048], part)
        for sp in range(8):
            block = jnp.concatenate([acck[136 * sp:136 * sp + 136, :], jnp.zeros((8, 128), F32)], axis=0)
            go[sp // 2, sp % 2, :, to:to + 128] = block.astype(BF)

    ocols = (slice(0, 512), slice(512, 640))

    def oz_copy(k, i, zp):
        return remote(go.at[zp, :, :, ocols[k]], zro.at[slot_at(zp), :, :, ocols[k]],
                      ozs.at[k, i], ozr.at[k, slot_at(zp)], h.zdev(zp))

    def ox_copy(k):
        return remote(go.at[z, h.xb, :, ocols[k]], xro.at[:, ocols[k]], oxs.at[k], oxr.at[k], h.xdev)

    def o_send(k):
        for i, zp in enumerate(h.peers):
            oz_copy(k, i, zp).start()

    def oy_copy(k):
        return remote(yso.at[:, ocols[k]], yro.at[:, ocols[k]], oys.at[k], oyr.at[k], h.ydev)

    for q in range(4):
        proj(pl.ds(pl.multiple_of(512 * c + 128 * q, 128), 128), 128 * q)
    o_send(0)

    @pl.when(c == 0)
    def _():
        proj(slice(1024, 1152), 512)
        o_send(1)

    def o_after_z(k):
        cols = ocols[k]
        for i in range(3):
            ref = zro.at[i, :, :, cols]
            remote(ref, ref, ozs.at[k, 0], ozr.at[k, i], h.core).wait_recv()
        for xp in range(2):
            go[z, xp, :, cols] = (
                (go[z, xp, :, cols].astype(F32) + zro[0, xp, :, cols].astype(F32))
                + (zro[1, xp, :, cols].astype(F32) + zro[2, xp, :, cols].astype(F32))).astype(BF)
        ox_copy(k).start()

    def o_after_x(k):
        cols = ocols[k]
        ox_copy(k).wait_recv()
        yso[:, cols] = (go[z, x, :, cols].astype(F32) + xro[:, cols].astype(F32)).astype(BF)
        oy_copy(k).start()

    def o_after_y(k):
        oy_copy(k).wait_recv()
        F4[288:432, ocols[k]] = yso[:, ocols[k]].astype(F32) + yro[:, ocols[k]].astype(F32)

    def both(step, main, more):
        for k in main:
            step(k)

        @pl.when(c == 0)
        def _():
            for k in more:
                step(k)

    for copy in q_loads + t_loads:
        copy.wait()
    ACT[:, 1536:1920] = jnp.zeros((1024, 384), BF)
    WI[512:640, 0:1024] = jnp.zeros((128, 1024), BF)

    def attend(head):
        pair = head // 2
        parity = lax.rem(head, 2)
        both_heads = pl.ds(pl.multiple_of(pair * 128, 128), 128)
        feat = pl.ds(pl.multiple_of(head * 64, 64), 64)
        on_rows = lax.broadcasted_iota(jnp.int32, (128, 256), 0) // 64 == parity
        on_lanes = lax.broadcasted_iota(jnp.int32, (256, 128), 1) // 64 == parity
        zero = jnp.zeros((), BF)
        qcol = both_heads
        kcol = pl.ds(pl.multiple_of(640 + pair * 128, 128), 128)
        vcol = pl.ds(pl.multiple_of(1280 + pair * 128, 128), 128)

        @pl.when(parity == 0)
        def _():
            acck[0:1024, :] = jnp.zeros((1024, 128), F32)
            accv[...] = jnp.zeros_like(accv)
        top = 0
        for b in range(4):
            start = max(0, b - 2)
            width = (b + 1 - start) * 256
            keys = slice(start * 256, start * 256 + width)
            cols = slice(b * 256, b * 256 + 256)
            scores = mm(IG[keys, kcol], jnp.where(on_rows, WU[both_heads, cols], zero))
            probs = jnp.exp(scores + inner[top:top + width, :] - lse[pl.ds(head, 1), cols])
            top += width
            grads = mm(IG[keys, vcol], jnp.where(on_rows, COTT[both_heads, cols], zero))
            terms = jnp.sum(probs * grads, axis=0, keepdims=True)
            sgrad = (probs * (grads - terms)).astype(BF)
            accv[keys, :] = accv[keys, :] + mm(
                probs.astype(BF), jnp.where(on_lanes, WI[cols, vcol], zero))
            acck[keys, :] = acck[keys, :] + mm(
                sgrad, jnp.where(on_lanes, IG[cols, qcol], zero))
            WI[feat, cols] = (
                mm(WU[feat, 1024 + start * 256:1024 + start * 256 + width], sgrad) * 0.125
            ).astype(BF)

        @pl.when((parity == 1) | (head == 8 - c))
        def _():
            kto = pl.ds(pl.multiple_of(jnp.where(pair < 4, 512 + 128 * pair, 1664), 128), 128)
            vto = pl.ds(pl.multiple_of(jnp.where(pair < 4, 1024 + 128 * pair, 1792), 128), 128)
            ACT[:, kto] = acck[0:1024, :].astype(BF)
            ACT[:, vto] = accv[...].astype(BF)

    def heads(low, high):
        @pl.loop(low, high)
        def _(head):
            attend(head)

    acols = (slice(0, 256), slice(256, 512), slice(512, 640))

    def qcols(k):
        return slice(256 * k, 256 * k + 256) if k < 2 else slice(1536, 1664)

    def vcols(k, tp):
        start = 512 + 512 * tp + 256 * k if k < 2 else 1664 + 128 * tp
        return pl.ds(pl.multiple_of(start, 128), 256 if k < 2 else 128)

    def grads(k, tp=None):
        if k:
            return gi, (qcols(k) if tp is None else vcols(k, tp))
        return early, (slice(0, 256) if tp is None
                       else pl.ds(pl.multiple_of(256 + 256 * tp, 128), 256))

    def weights(k, tp=None):
        cols = qcols(k) if tp is None else vcols(k, tp)
        dst, to = grads(k, tp)

        @pl.loop(0, 2)
        def _(half):
            got = mm(N2T[pl.ds(pl.multiple_of(576 * half, 576), 576), :], ACT[:, cols])
            for q in range(4):
                dst[2 * half + q // 2, q % 2, :, to] = got[144 * q:144 * q + 144, :].astype(BF)

    def vy(k):
        src, cols = grads(k, h.tb)
        return remote(src.at[:, :, :, cols], vyr.at[:, :, :, acols[k]], ays.at[k], ayr.at[k],
                      h.ydev)

    def ax(m, k):
        buf, cols = grads(k) if m == 0 else (vyr, acols[k])
        src = buf.at[:, h.xb, :, cols]
        return remote(src, xra.at[m, :, :, acols[k]], axs.at[m, k], axr.at[m, k], h.xdev)

    def a_one(m, k, i):
        return remote(xra.at[m, lax.rem(near, 2) + 2 * i, :, acols[k]], zra.at[m, i, :, acols[k]],
                      azs.at[m, k, i], azr.at[m, k, i], h.zdev(near))

    def a_two(m, k):
        return remote(xra.at[m, far, :, acols[k]], zra.at[m, 2, :, acols[k]],
                      azs.at[m, k, 2], azr.at[m, k, 2], h.zdev(far))

    def AM(m, k):
        cols = acols[k]
        for i in range(2):
            a_one(m, k, i).wait_recv()
            at = lax.rem(z, 2) + 2 * i
            xra[m, at, :, cols] = (
                xra[m, at, :, cols].astype(F32) + zra[m, i, :, cols].astype(F32)).astype(BF)
        a_two(m, k).start()

    def ay(m, k):
        return remote(ysa.at[m, :, acols[k]], yra.at[m, :, acols[k]],
                      ays.at[3 + 3 * m + k], ayr.at[3 + 3 * m + k], h.ydev)

    def VY(k):
        vy(k).wait_recv()
        cols = acols[k]
        src, part = grads(k, t)

        @pl.loop(0, 4)
        def _(zp):
            for xp in range(2):
                vyr[zp, xp, :, cols] = (
                    vyr[zp, xp, :, cols].astype(F32) + src[zp, xp, :, part].astype(F32)
                ).astype(BF)
        ax(1, k).start()

    def AX(m, k):
        cols = acols[k]
        src, part = grads(k)
        ax(m, k).wait_recv()

        @pl.loop(0, 4)
        def _(zp):
            mine = src[zp, x, :, part] if m == 0 else vyr[zp, x, :, cols]
            xra[m, zp, :, cols] = (
                xra[m, zp, :, cols].astype(F32) + mine.astype(F32)).astype(BF)
        for i in range(2):
            a_one(m, k, i).start()

    def AZ(m, k):
        cols = acols[k]
        a_two(m, k).wait_recv()
        ysa[m, :, cols] = (
            xra[m, z, :, cols].astype(F32) + zra[m, 2, :, cols].astype(F32)).astype(BF)
        ay(m, k).start()

    def AY(m, k):
        ay(m, k).wait_recv()
        cols = acols[k]
        mine, other = ysa[m, :, cols].astype(F32), yra[m, :, cols].astype(F32)
        if k < 2:
            blocks = [(k, mine + other)] if m == 0 else [(2 + 2 * t + k, mine), (2 + 2 * h.tb + k, other)]
            for block, value in blocks:
                inner[pl.ds(pl.multiple_of(144 * block, 16), 144), :] = value
        elif m == 0:
            inner[864:1008, 0:128] = mine + other
        else:
            inner[864:1008, 128:256] = jnp.where(t == 0, mine, other)
            inner[1008:1152, 0:128] = jnp.where(t == 0, other, mine)

    def group(k):
        weights(k, h.tb)
        vy(k).start()
        weights(k)
        ax(0, k).start()
        weights(k, t)

    def turn(pair):
        at = slice(128 * pair, 128 * pair + 128)
        ACT[:, at if pair < 4 else slice(1536, 1664)] = WI[at, 0:1024].T

    def more(step, *args):
        @pl.when(c == 0)
        def _():
            step(*args, 2)

    IX(6)
    heads(0, 2)
    MZ(0, 0)
    OY(3)
    IX(7)
    heads(2, 4)
    turn(0)
    turn(1)
    group(0)
    IX(8)
    OY(4)
    IY(0)
    heads(4, 6)
    IY(1)
    LZ(0, 0)
    OX(1)
    MZ(1, 0)
    both(o_after_z, (0,), (1,))
    heads(6, 8)
    turn(2)
    turn(3)
    for n in range(9):
        only(4 if n == 8 else 0, lambda: ix(n).wait_send())
    group(1)
    MZ(0, 1)
    MZ(1, 1)
    IY(2)
    heads(8, 9 - c)

    @pl.when(c == 0)
    def _():
        turn(4)
        group(2)
    wa_load = fetch(16, wa_h, WI.at[:, 0:1920])
    x_load = fetch(17, x_h, COT.at[0:512])
    IY(3)
    IY(4)
    OX(2)
    MZ(1, 2)

    mix_out.wait()
    wa_load.wait()

    def n1_copy(i):
        at = pl.ds(pl.multiple_of(384 * i, 128), 384)
        return remote(F3.at[:, at], F2.at[:, at], dsend.at[7 + i], drecv.at[7 + i], h.core)

    @pl.loop(0, 3)
    def _(i):
        at = pl.ds(pl.multiple_of(384 * i, 128), 384)
        F3[:, at] = nt(ACT[pl.ds(sib0, rows), 0:1920], WI[at, 0:1920]).astype(BF)
        n1_copy(i).start()

    @pl.loop(0, 4)
    def _(i):
        at = pl.ds(pl.multiple_of(256 * i, 256), 256)
        inner[pl.ds(pl.multiple_of(512 * i, 512), 512), :] = nt(
            ACT[pl.ds(own0, rows), 0:1920], WI[at, 0:1920])
    part = nt(ACT[pl.ds(own0, rows), 0:1920], WI[1024:1152, 0:1920])
    inner[2048:2304, 0:128] = part[0:256]
    inner[2048:2304, 128:256] = part[256:512]
    n1_sends = [n1_copy(i) for i in range(3)]

    @pl.loop(0, 15)
    def _(i):
        at = pl.ds(pl.multiple_of(128 * i, 128), 128)
        sg[0:1, at] = jnp.sum(ACT[:, at].astype(F32), axis=0, keepdims=True)
    OX(3)
    OX(4)
    VY(0)
    MZ(0, 2)
    MZ(1, 3)
    MZ(1, 4)
    VY(1)
    MZ(0, 3)
    MZ(0, 4)
    LZ(0, 1)
    for n in range(3):
        LZ(1, n)
    both(o_after_x, (0,), (1,))
    more(VY)
    AX(0, 0)
    AX(0, 1)
    x_load.wait()
    for copy in n1_sends:
        copy.wait_recv()

    @pl.loop(0, 16)
    def _(i):
        at = pl.ds(pl.multiple_of(32 * i, 32), 32)
        half = i // 8
        tail = inner[pl.ds(pl.multiple_of(2048 + 32 * (i - 8 * half), 32), 32),
                     pl.ds(pl.multiple_of(128 * half, 128), 128)]
        part = jnp.concatenate(
            [inner[pl.ds(pl.multiple_of(512 * j + 32 * i, 32), 32), :] for j in range(4)] + [tail],
            axis=1)
        grad = part + F2[at, :].astype(F32)
        v = COT[at, :].astype(F32)
        mean = jnp.sum(v, axis=1, keepdims=True) * (1.0 / count)
        spread = (v - mean) * mask
        rstd = lax.rsqrt(jnp.sum(spread * spread, axis=1, keepdims=True) * (1.0 / count) + EPS)
        hat = spread * rstd
        scaled = grad * par[0:1, :]
        F1[at, :] = F1[at, :] + rstd * (
            scaled - jnp.sum(scaled, axis=1, keepdims=True) * (1.0 / count)
            - hat * (jnp.sum(scaled * hat, axis=1, keepdims=True) * (1.0 / count))) * mask
        sg[1:2, 0:1152] = sg[1:2, 0:1152] + jnp.sum(grad * hat, axis=0, keepdims=True)
        sg[2:3, 0:1152] = sg[2:3, 0:1152] + jnp.sum(grad, axis=0, keepdims=True)

    tok_outs = [pltpu.make_async_copy(F1, tokens_o, outsem.at[1])]
    tok_outs[0].start()

    sgx_copy = remote(sg, sgx, gsend.at[0], grecv.at[0], h.xdev)
    sgx_copy.start()
    more(AX, 0)
    AM(0, 0)
    AM(0, 1)
    more(AM, 0)
    sgx_copy.wait()
    sgx[...] = sgx[...] + sg[...]

    def sgz_copy(i, zp):
        return remote(sgx, sgz.at[slot_at(zp)], gsend.at[1 + i], grecv.at[1 + slot_at(zp)], h.zdev(zp))

    for i, zp in enumerate(h.peers):
        sgz_copy(i, zp).start()
    both(o_after_y, (0,), (1,))
    for n in range(2, 5):
        LZ(0, n)
    for n in range(3, 5):
        LZ(1, n)

    finals = []

    def deliver(n, src, out):
        local = pltpu.make_async_copy(src, out.at[c], finloc.at[n])
        local.start()
        over = remote(src, out.at[c], finsend.at[n], finrecv.at[n], h.core)
        over.start()
        finals.append((local, over))

    deliver(0, F4.at[288:432, 0:640], proj_o)
    deliver(1, F4.at[0:144], out_o)
    deliver(2, F4.at[144:288], in_o)
    AX(1, 0)
    AX(1, 1)
    more(AX, 1)
    AM(1, 0)
    AM(1, 1)
    more(AM, 1)
    AZ(0, 0)
    AZ(0, 1)
    more(AZ, 0)
    for i in range(3):
        remote(sgz.at[i], sgz.at[i], gsend.at[1], grecv.at[1 + i], h.core).wait_recv()
    for i, zp in enumerate(h.peers):
        sgz_copy(i, zp).wait_send()
    sg[...] = (sgx[...] + sgz[0]) + (sgz[1] + sgz[2])
    sgy_copy = remote(sg, sgy, gsend.at[4], grecv.at[4], h.ydev)
    sgy_copy.start()
    AZ(1, 0)
    AZ(1, 1)
    more(AZ, 1)
    sgy_copy.wait()
    sgx[...] = sg[...] + sgy[...]
    deliver(3, sgx, sums_o)
    for m in range(2):
        AY(m, 0)
        AY(m, 1)
        more(AY, m)
    deliver(4, inner.at[0:1152], qkv_o)

    for copy in tok_outs:
        copy.wait()
    for copy in n1_sends:
        copy.wait_send()

    def drain(k):
        oy(k).wait_send()
        ox(k).wait_send()
        iy(k).wait_send()
        for m in range(2):
            for i in range(2):
                z_one(m, k, i).wait_send()
            z_two(m, k).wait_send()

    for n in range(5):
        only(n, lambda: drain(n))

    def o_drain(k):
        ox_copy(k).wait_send()
        oy_copy(k).wait_send()
        for i, zp in enumerate(h.peers):
            oz_copy(k, i, zp).wait_send()

    both(o_drain, (0,), (1,))

    def a_drain(k):
        vy(k).wait_send()
        for m in range(2):
            ay(m, k).wait_send()
            ax(m, k).wait_send()
            for i in range(2):
                a_one(m, k, i).wait_send()
            a_two(m, k).wait_send()

    a_drain(0)
    a_drain(1)
    more(a_drain)
    for local, over in finals:
        local.wait()
        over.wait()


def run_backward(saved):
    (wa, wo, wi, wu, n1t, n2t, cot, qn, kn, vn, qt, kt, ot, lse, mid, slope, act, go, par, mb, x) = saved
    hbm = pl.BlockSpec(memory_space=pltpu.HBM)
    vmem = pl.BlockSpec(memory_space=pltpu.VMEM)
    sds = jax.ShapeDtypeStruct
    V = pltpu.VMEM
    dma = pltpu.SemaphoreType.DMA
    shapes = [
        sds((512, 1152), BF), sds((512, 1152), F32), sds((2, 144, 1152), F32),
        sds((2, 144, 1152), F32), sds((2, 1152, 256), F32), sds((2, 144, 640), F32),
        sds((2, 8, 1920), F32),
    ]
    scratch = [
        V((1152, 2304), BF), V((1152, 2304), BF), V((1024, 2304), BF), V((1024, 2304), BF),
        V((1024, 1152), BF), V((640, 1024), BF), V((1152, 1024), BF), V((2304, 256), F32),
        V((512, 1152), F32), V((512, 1152), BF), V((512, 1152), BF), V((512, 1152), F32),
        V((512, 1152), BF), V((4, 2, 144, 1152), BF), V((4, 144, 1152), BF), V((4, 144, 2304), BF), V((4, 144, 1152), BF),
        V((2, 3, 144, 1152), BF), V((4, 2, 144, 2304), BF), V((4, 2, 144, 256), BF), V((4, 2, 144, 768), BF),
        V((1088, 128), F32), V((1024, 128), F32),
        V((4, 2, 144, 640), BF), V((2, 4, 144, 640), BF), V((2, 3, 144, 640), BF), V((2, 144, 640), BF), V((2, 144, 640), BF),
        V((4, 2, 144, 640), BF), V((144, 640), BF), V((3, 2, 144, 640), BF), V((144, 640), BF),
        V((144, 640), BF),
        V((8, 1920), F32), V((8, 1920), F32), V((3, 8, 1920), F32), V((8, 1920), F32), V((8, 256), F32),
        dma((18,)), dma((2,)), dma((1,)),
        dma((2, 5)), dma((2, 5)), dma((5,)), dma((5,)), dma((9,)), dma((9,)), dma((2, 5, 3)), dma((2, 5, 3)),
        dma((2, 3)), dma((2, 3)), dma((2, 3, 3)), dma((2, 3, 3)), dma((9,)), dma((9,)),
        dma((2,)), dma((2,)), dma((2, 3)), dma((2, 3)), dma((2,)), dma((2,)),
        dma((5,)), dma((5,)), dma((10,)), dma((10,)), dma((6,)), dma((5,)), dma((5,)), dma((5,)),
    ]
    return pl.pallas_call(
        backward_kernel, out_shape=shapes, in_specs=[vmem] * 2 + [hbm] * 19,
        out_specs=[hbm] * len(shapes), scratch_shapes=scratch,
        compiler_params=pltpu.CompilerParams(
            collective_id=1, has_side_effects=True, vmem_limit_bytes=65300 << 10),
        cost_estimate=pl.CostEstimate(flops=40 * 10**9, bytes_accessed=80 * 10**6, transcendentals=2 * 10**7),
        name="backward",
    )(par, lse, wa, wo, wi, wu, n1t, n2t, cot, qn, kn, vn, qt, kt, ot, mid, slope, act, go, mb, x)


def finish_kernel(mixed_h, tokens_h, out_h, in_h, qkv_h, proj_h, sums_h,
                  mixed, tokens, gains, shifts, biases, w_qkv, w_o, w_in, b_in, w_out,
                  mixed_in, tokens_in, out_in, in_in, qkv_in, proj_in, sums_in, line, isem):
    c = lax.axis_index("ctx")
    s = lax.axis_index("shard")
    loads = [pltpu.make_async_copy(src, dst, isem.at[n]) for n, (src, dst) in enumerate((
        (tokens_h, tokens_in), (mixed_h, mixed_in), (qkv_h, qkv_in), (out_h, out_in), (in_h, in_in),
        (proj_h, proj_in), (sums_h, sums_in)))]
    for copy in loads:
        copy.start()

    def turned(v):
        v = v.T
        return jnp.concatenate([v[144 * q:144 * q + 136] for q in range(8)], axis=0)

    loads[0].wait()
    loads[1].wait()
    for i in range(4):
        at = slice(128 * i, 128 * i + 128)
        tokens[:, at] = turned(tokens_in[at, :])
        mixed[:, at] = turned(mixed_in[at, :].astype(F32)).astype(BF)

    def join(v):
        block = lax.broadcasted_iota(jnp.int32, v.shape, 1) // 136
        got = v
        for q in range(1, 8):
            got = jnp.where(block == q, pltpu.roll(v, 1152 - 8 * q, 1), got)
        return got[:, 0:1088]

    def heads(core, n):
        yield 2 * n, 0, 256, 0
        yield 2 * n + 1, 0, 256, 256
        if core == 0:
            yield 6 + n // 2, 128 * (n % 2), 64, 512

    for copy in loads[2:]:
        copy.wait()

    def for_core(core):
        at = slice(68 * core, 68 * core + 68)
        for n in range(3):
            for owner in range(2):
                for block, start, width, to in heads(owner, n):
                    to = 1088 * n + 576 * owner + to
                    w_qkv[:, to:to + width] = qkv_in[
                        owner, 144 * block + at.start:144 * block + at.stop, start:start + width]
        wide = jnp.concatenate(
            [proj_in[0, at, 0:512], proj_in[1, at, 0:512], proj_in[0, at, 512:640]], axis=1)
        w_o[...] = join(wide)
        w_in[:, 0:1152] = in_in[0, at, :]
        w_in[:, 1152:2176] = in_in[1, at, 0:1024]
        w_out[:, 0:1152] = out_in[0, at, :]
        w_out[:, 1152:2176] = out_in[1, at, 0:1024]

    pl.when(c == 0)(lambda: for_core(0))
    pl.when(c == 1)(lambda: for_core(1))

    rows = sums_in[0] + sums_in[1]
    mine = pltpu.roll(rows, 1920 - (s * BR + c * 68), 1)[:, 0:68]
    gains[0:1, :] = mine[1:2]
    gains[1:2, :] = mine[3:4]
    shifts[0:1, :] = mine[2:3]
    shifts[1:2, :] = mine[4:5]
    biases[2:3, :] = mine[6:7]
    biases[3:4, :] = mine[5:6]
    for n, row in ((0, 0), (2, 1)):
        start, more = 512 * n, 1536 + 128 * n
        line[:, 0:512] = sums_in[0, :, start:start + 512]
        line[:, 512:576] = sums_in[0, :, more:more + 64]
        line[:, 576:1088] = sums_in[1, :, start:start + 512]
        got = pltpu.roll(line[:, 0:1152], 1152 - (2 * s + c) * 68, 1)[:, 0:68]
        biases[row:row + 1, :] = got[0:1]
    line[:, 0:1152] = in_in[0, 136:144, :]
    line[:, 1152:2176] = in_in[1, 136:144, 0:1024]
    b_in[...] = pltpu.roll(line[...], 2176 - (2 * s + c) * 136, 1)[0:1, 0:136]


def finish(mixed, tokens_grad, out_g, in_g, qkv_g, proj_g, sums):
    sds = jax.ShapeDtypeStruct
    shapes = [
        sds((1088, 512), BF), sds((1088, 512), F32), sds((2, 68), F32), sds((2, 68), F32),
        sds((4, 68), F32), sds((68, 3264), F32), sds((68, 1088), F32), sds((68, 2176), F32),
        sds((1, 136), F32), sds((68, 2176), F32),
    ]
    vmem = pl.BlockSpec(memory_space=pltpu.VMEM)
    hbm = pl.BlockSpec(memory_space=pltpu.HBM)
    given = (mixed, tokens_grad, out_g, in_g, qkv_g, proj_g, sums)
    got = pl.pallas_call(
        finish_kernel, out_shape=shapes, in_specs=[hbm] * 7, out_specs=[vmem] * len(shapes),
        scratch_shapes=[pltpu.VMEM(v.shape, v.dtype) for v in given] + [
            pltpu.VMEM((8, 2176), F32), pltpu.SemaphoreType.DMA((7,))],
        compiler_params=pltpu.CompilerParams(vmem_limit_bytes=63 << 20), name="finish",
    )(*given)
    return (got[0].T[None], got[1].T[None]) + tuple(got[2:9]) + (got[9].T,)


def fused(tokens, segment_ids, norm_gains, norm_shifts, biases, w_qkv, w_o, w_in, b_in, w_out,
          cotangent):
    saved = run_forward(tokens, segment_ids, norm_gains, norm_shifts, biases, w_qkv, w_o, w_in,
                        b_in, w_out, cotangent)
    sums = run_backward(saved)
    return finish(*sums)


def per_device(
    tokens, segment_ids, norm_gains, norm_shifts, biases, w_qkv, w_o, w_in, b_in, w_out, cotangent
):
    rows_here = tokens.shape[1]
    score_scale = HEAD_DIM ** (-0.5)
    gains_full, shifts_full, bias_full, qkv_full, proj_full, up_full, down_full = (
        lax.all_gather(norm_gains, "shard", axis=1, tiled=True),
        lax.all_gather(norm_shifts, "shard", axis=1, tiled=True),
        lax.all_gather(biases, "shard", axis=1, tiled=True),
        lax.all_gather(w_qkv, "shard", axis=0, tiled=True),
        lax.all_gather(w_o, "shard", axis=0, tiled=True),
        lax.all_gather(w_in, "shard", axis=0, tiled=True),
        lax.all_gather(w_out, "shard", axis=1, tiled=True),
    )
    gains_full = gains_full.astype(jnp.float32)
    shifts_full = shifts_full.astype(jnp.float32)
    bias_full = bias_full.astype(jnp.float32)
    hidden = tokens[0].astype(jnp.float32)
    normed, norm_back_one = jax.vjp(layer_norm, hidden, gains_full[0], shifts_full[0])
    normed_low = normed.astype(jnp.bfloat16)
    projected = jnp.dot(normed_low, qkv_full, preferred_element_type=jnp.float32)
    queries = (projected[:, :D] + bias_full[0]).astype(jnp.bfloat16)
    key_rows = projected[:, D : 2 * D].astype(jnp.bfloat16)
    value_rows = (projected[:, 2 * D :] + bias_full[1]).astype(jnp.bfloat16)
    all_keys, all_values = (
        lax.all_gather(key_rows, "ctx", axis=0, tiled=True),
        lax.all_gather(value_rows, "ctx", axis=0, tiled=True),
    )
    seq_length = all_keys.shape[0]
    offset = lax.axis_index("ctx") * rows_here
    key_segments = segment_ids[0]
    query_segments = lax.dynamic_slice_in_dim(key_segments, offset, rows_here)
    query_position = offset + lax.iota(jnp.int32, rows_here)
    key_position = lax.iota(jnp.int32, seq_length)
    allowed = (key_position[None, :] <= query_position[:, None]) & (
        key_segments[None, :] == query_segments[:, None]
    )
    query_heads = split_heads(queries)
    key_heads = split_heads(all_keys)
    value_heads = split_heads(all_values)

    def head_scores(query_head, key_head):
        scores = (
            jnp.einsum("qd,kd->qk", query_head, key_head, preferred_element_type=jnp.float32)
            * score_scale
        )
        return jnp.where(allowed, scores, -1e30)

    def head_forward(operands):
        query_head, key_head, value_head = operands
        masked = head_scores(query_head, key_head)
        highest = jnp.max(masked, axis=1, keepdims=True)
        weights = jnp.exp(masked - highest)
        summed = jnp.sum(weights, axis=1, keepdims=True)
        probabilities = (weights / summed).astype(jnp.bfloat16)
        result = jnp.dot(probabilities, value_head, preferred_element_type=jnp.float32)
        return (result, (highest + jnp.log(summed))[:, 0])

    head_out, log_total = lax.map(head_forward, (query_heads, key_heads, value_heads))
    attended = merge_heads(head_out).astype(jnp.bfloat16)
    middle = (
        hidden + jnp.dot(attended, proj_full, preferred_element_type=jnp.float32) + bias_full[2]
    )
    normed_two, norm_back_two = jax.vjp(layer_norm, middle, gains_full[1], shifts_full[1])
    normed_two_low = normed_two.astype(jnp.bfloat16)
    mlp_inputs = lax.all_gather(normed_two_low, "tp", axis=0, tiled=True)
    inner_values = jnp.dot(mlp_inputs, up_full, preferred_element_type=jnp.float32) + b_in.astype(
        jnp.float32
    )
    active, gelu_back = jax.vjp(gelu_tanh, inner_values)
    active_low = active.astype(jnp.bfloat16)
    mixed_rows = (
        middle
        + lax.psum_scatter(
            jnp.dot(active_low, down_full, preferred_element_type=jnp.float32).astype(jnp.bfloat16),
            "tp",
            scatter_dimension=0,
            tiled=True,
        ).astype(jnp.float32)
        + bias_full[3]
    )
    mixed_out = mixed_rows.astype(jnp.bfloat16)[None]
    grad_low = cotangent[0]
    grad_out = grad_low.astype(jnp.float32)
    grad_rows = lax.all_gather(grad_low, "tp", axis=0, tiled=True)
    down_grad = contract_rows(active_low, grad_rows)
    out_bias_grad = jnp.sum(grad_out, axis=0)
    active_grad = contract_cols(grad_rows, down_full)
    inner_grad = gelu_back(active_grad)[0].astype(jnp.bfloat16)
    up_grad = contract_rows(mlp_inputs, inner_grad)
    in_bias_grad = jnp.sum(inner_grad.astype(jnp.float32), axis=0)
    normed_two_grad = lax.psum_scatter(
        contract_cols(inner_grad, up_full), "tp", scatter_dimension=0, tiled=True
    )
    middle_part, gain_two_grad, shift_two_grad = norm_back_two(normed_two_grad)
    middle_grad = grad_out + middle_part
    branch_grad = middle_grad.astype(jnp.bfloat16)
    proj_grad = contract_rows(attended, branch_grad)
    attn_bias_grad = jnp.sum(branch_grad.astype(jnp.float32), axis=0)
    attended_grad = split_heads(contract_cols(branch_grad, proj_full).astype(jnp.bfloat16))

    def head_backward(operands):
        query_head, key_head, value_head, grad_head, log_head = operands
        masked = head_scores(query_head, key_head)
        probabilities = jnp.exp(masked - log_head[:, None])
        probs_grad = jnp.einsum(
            "qd,kd->qk", grad_head, value_head, preferred_element_type=jnp.float32
        )
        row_terms = jnp.sum(probabilities * probs_grad, axis=1, keepdims=True)
        scores_grad = (probabilities * (probs_grad - row_terms)).astype(jnp.bfloat16)
        query_grad = (
            jnp.dot(scores_grad, key_head, preferred_element_type=jnp.float32) * score_scale
        )
        key_grad = (
            jnp.einsum("qk,qd->kd", scores_grad, query_head, preferred_element_type=jnp.float32)
            * score_scale
        )
        value_grad = jnp.einsum(
            "qk,qd->kd",
            probabilities.astype(jnp.bfloat16),
            grad_head,
            preferred_element_type=jnp.float32,
        )
        return (query_grad, key_grad, value_grad)

    query_grads, key_grads, value_grads = lax.map(
        head_backward, (query_heads, key_heads, value_heads, attended_grad, log_total)
    )
    key_summed, value_summed = (
        lax.psum_scatter(
            merge_heads(key_grads).astype(jnp.bfloat16), "ctx", scatter_dimension=0, tiled=True
        ).astype(jnp.float32),
        lax.psum_scatter(
            merge_heads(value_grads).astype(jnp.bfloat16), "ctx", scatter_dimension=0, tiled=True
        ).astype(jnp.float32),
    )
    query_low = merge_heads(query_grads).astype(jnp.bfloat16)
    value_low = value_summed.astype(jnp.bfloat16)
    qkv_grad = jnp.concatenate([query_low, key_summed.astype(jnp.bfloat16), value_low], axis=1)
    qkv_weight_grad = contract_rows(normed_low, qkv_grad)
    query_bias_grad = jnp.sum(query_low.astype(jnp.float32), axis=0)
    value_bias_grad = jnp.sum(value_low.astype(jnp.float32), axis=0)
    normed_grad = contract_cols(qkv_grad, qkv_full)
    hidden_part, gain_one_grad, shift_one_grad = norm_back_one(normed_grad)
    tokens_grad = (middle_grad + hidden_part)[None]
    gains_grad = jnp.stack([gain_one_grad, gain_two_grad])
    shifts_grad = jnp.stack([shift_one_grad, shift_two_grad])
    biases_grad = jnp.stack([query_bias_grad, value_bias_grad, attn_bias_grad, out_bias_grad])
    gains_grad, shifts_grad, biases_grad, qkv_weight_grad, proj_grad = lax.psum(
        (gains_grad, shifts_grad, biases_grad, qkv_weight_grad, proj_grad), "tp"
    )
    (
        gains_grad,
        shifts_grad,
        biases_grad,
        qkv_weight_grad,
        proj_grad,
        up_grad,
        in_bias_grad,
        down_grad,
    ) = (
        lax.psum_scatter(gains_grad, ("shard", "ctx"), scatter_dimension=1, tiled=True),
        lax.psum_scatter(shifts_grad, ("shard", "ctx"), scatter_dimension=1, tiled=True),
        lax.psum_scatter(biases_grad, ("shard", "ctx"), scatter_dimension=1, tiled=True),
        lax.psum_scatter(qkv_weight_grad, ("shard", "ctx"), scatter_dimension=0, tiled=True),
        lax.psum_scatter(proj_grad, ("shard", "ctx"), scatter_dimension=0, tiled=True),
        lax.psum_scatter(up_grad, ("shard", "ctx"), scatter_dimension=0, tiled=True),
        lax.psum_scatter(in_bias_grad, ("shard", "ctx"), scatter_dimension=0, tiled=True),
        lax.psum_scatter(down_grad, ("shard", "ctx"), scatter_dimension=1, tiled=True),
    )
    return (
        mixed_out,
        tokens_grad,
        gains_grad,
        shifts_grad,
        biases_grad,
        qkv_weight_grad,
        proj_grad,
        up_grad,
        in_bias_grad[None],
        down_grad,
    )


def solution(mesh):
    in_specs = (
        P(("shard", "tp"), "ctx", None),
        P(("shard", "tp"), None),
        P(None, "shard"),
        P(None, "shard"),
        P(None, "shard"),
        P("shard", None),
        P("shard", None),
        P("shard", "tp"),
        P("tp"),
        P("tp", "shard"),
        P(("shard", "tp"), "ctx", None),
    )
    out_specs = (
        P(("shard", "tp"), "ctx", None),
        P(("shard", "tp"), "ctx", None),
        P(None, ("shard", "ctx")),
        P(None, ("shard", "ctx")),
        P(None, ("shard", "ctx")),
        P(("shard", "ctx"), None),
        P(("shard", "ctx"), None),
        P(("shard", "ctx"), "tp"),
        P("tp", ("shard", "ctx")),
        P("tp", ("shard", "ctx")),
    )
    fits = dict(mesh.shape) == {"shard": 8, "ctx": 2, "tp": 2}
    return jax.shard_map(
        fused if fits else per_device, mesh=mesh, in_specs=in_specs, out_specs=out_specs, check_vma=False
    )
```

```python
import math

import jax
import jax.numpy as jnp
from jax import lax
from jax.experimental import pallas as pl
from jax.experimental.pallas import tpu as pltpu
from jax.sharding import PartitionSpec as P

D = 1088
HEADS = 17
HEAD_DIM = 64


def layer_norm(values, gain_row, shift_row):
    center = jnp.mean(values, axis=-1, keepdims=True)
    spread = values - center
    variance = jnp.mean(spread * spread, axis=-1, keepdims=True)
    return spread * lax.rsqrt(variance + 1e-05) * gain_row + shift_row


def gelu_tanh(values):
    return (
        0.5
        * values
        * (
            1.0
            + jnp.tanh(math.sqrt(2.0 / math.pi) * (values + 0.044715 * values * values * values))
        )
    )


def contract_rows(left_side, right_side):
    return lax.dot_general(
        left_side, right_side, (((0,), (0,)), ((), ())), preferred_element_type=jnp.float32
    )


def contract_cols(left_side, right_side):
    return lax.dot_general(
        left_side, right_side, (((1,), (1,)), ((), ())), preferred_element_type=jnp.float32
    )


def split_heads(matrix):
    return matrix.reshape(matrix.shape[0], HEADS, HEAD_DIM).transpose(1, 0, 2)


def merge_heads(stacked):
    return stacked.transpose(1, 0, 2).reshape(stacked.shape[1], D)


BF = jnp.bfloat16
F32 = jnp.float32
MESH = pl.DeviceIdType.MESH
EPS = 1e-05
BR = 144
UNIT = 128


def mm(left, right):
    return jnp.dot(left, right, preferred_element_type=F32)


def remote(src, dst, send, recv, device):
    return pltpu.make_async_remote_copy(
        src_ref=src, dst_ref=dst, send_sem=send, recv_sem=recv,
        device_id=device, device_id_type=MESH,
    )


class Place:
    def __init__(self):
        self.s = lax.axis_index("shard")
        self.c = lax.axis_index("ctx")
        self.t = lax.axis_index("tp")
        self.z = self.s // 2
        self.x = self.s - 2 * self.z
        self.xb = 1 - self.x
        self.tb = 1 - self.t
        z = self.z
        self.peers = [
            z + 1 - 2 * lax.rem(z, 2),
            jnp.where(z < 2, 2, 1),
            jnp.where(z < 2, 3, 0),
        ]
        self.core = (self.s, 1 - self.c, self.t)
        self.xdev = (2 * z + self.xb, self.c, self.t)
        self.ydev = (self.s, self.c, self.tb)

    def zdev(self, zp):
        return (2 * zp + self.x, self.c, self.t)

    def greet(self):
        barrier = pltpu.get_barrier_semaphore()
        devices = [self.core, self.xdev, self.ydev] + [self.zdev(p) for p in self.peers]
        for device in devices:
            pl.semaphore_signal(barrier, inc=1, device_id=device, device_id_type=MESH)
        pl.semaphore_wait(barrier, len(devices))


def rows_of(s):
    return pl.ds(pl.multiple_of(s * BR, 16), BR)


class Gather:
    def __init__(self, here, number, own, loc, route, send, recv):
        self.h, self.p, self.own, self.loc, self.route = here, number, own, loc, route
        self.send, self.recv = send, recv
        self.two, self.three = (
            (here.ydev, here.xdev) if route == "zyx" else (here.xdev, here.ydev))
        if route == "zx":
            self.three = None

    def copy(self, src, s, t, device, i):
        return remote(src, self.loc(s, t), self.send.at[self.p, i],
                      self.recv.at[self.p, s * 2 + t], device)

    def take(self, s, t):
        ref = self.loc(s, t)
        self.copy(ref, s, t, self.h.core, 0).wait_recv()

    def along(self, k):
        h = self.h
        to = h.z + jnp.where(h.peers[k] < h.z, 1, -1)
        return (to >= 0) & (to <= 3), h.zdev(jnp.clip(to, 0, 3))

    def own_z(self):
        h = self.h
        pl.when(h.z < 3)(self.copy(self.own, h.s, h.t, h.zdev(jnp.minimum(h.z + 1, 3)), 0).start)
        pl.when(h.z > 0)(self.copy(self.own, h.s, h.t, h.zdev(jnp.maximum(h.z - 1, 0)), 1).start)

    def own_two(self):
        self.copy(self.own, self.h.s, self.h.t, self.two, 5).start()

    def own_three(self):
        if self.route in ("zxy", "zyx"):
            self.copy(self.own, self.h.s, self.h.t, self.three, 10).start()

    def z(self, k):
        h = self.h
        s = 2 * h.peers[k] + h.x
        self.take(s, h.t)
        block = self.loc(s, h.t)
        on, device = self.along(k)
        pl.when(on)(self.copy(block, s, h.t, device, 2 + k).start)
        self.copy(block, s, h.t, self.two, 6 + k).start()
        if self.three:
            self.copy(block, s, h.t, self.three, 11 + k).start()

    def second(self, k):
        h = self.h
        zp = ([h.z] + h.peers)[k]
        s, t = (2 * zp + h.x, h.tb) if self.route == "zyx" else (2 * zp + h.xb, h.t)
        self.take(s, t)
        if self.three:
            self.copy(self.loc(s, t), s, t, self.three, 14 + k).start()

    def third(self, k):
        h = self.h
        zp = ([h.z] + h.peers)[k]
        if self.route == "zyx":
            self.take(2 * zp + h.xb, h.t)
            self.take(2 * zp + h.xb, h.tb)
        elif self.three:
            if not (self.route == "kv" and k == 0):
                self.take(2 * zp + h.x, h.tb)
            self.take(2 * zp + h.xb, h.tb)

    def drain(self):
        h = self.h

        def sent(i):
            return self.copy(self.own, h.s, h.t, h.core, i).wait_send

        pl.when(h.z < 3)(sent(0))
        pl.when(h.z > 0)(sent(1))
        for k in range(3):
            pl.when(self.along(k)[0])(sent(2 + k))
        for i in range(5, 9):
            sent(i)()
        if self.three:
            for i in range(10 if self.route != "kv" else 11, 18):
                sent(i)()


def real_features():
    lane = lax.broadcasted_iota(jnp.int32, (1, 1152), 1)
    return (lax.rem(lane, BR) < 136).astype(F32)


def normalise(x, mask, gain, shift, count):
    mean = jnp.sum(x, axis=1, keepdims=True) * (1.0 / count)
    spread = (x - mean) * mask
    var = jnp.sum(spread * spread, axis=1, keepdims=True) * (1.0 / count)
    return spread * lax.rsqrt(var + EPS) * gain + shift


def forward_kernel(
    seg, gains, shifts, biases, b_in, tok_h, cot_h, w_qkv_h, w_o_h, w_in_h, w_out_h,
    wa_o, wo_o, wi_o, wu_o, n1t_o, n2t_o, cot_o, qn_o, kn_o, vn_o, qt_o, kt_o, ot_o,
    lse_o, mid_o, slope_o, act_o, go_o, par_o, mb_o, x_o,
    wa, wog, wo, wi, wu, n1, cot, cott, n2, sm, par, bins, qn, kn, vn, qt, kt, vt, mb, ot, att, mid,
    slope, act, tile, stage, lse, x_ref, segr, segc,
    tok, cot_in, w_qkv, w_o, w_in, w_out, spread,
    send, recv, dsend, drecv, ssend, srecv, lsem, osem, isem,
):
    h = Place()
    c, s, t = h.c, h.s, h.t
    rows = 512
    length = 2 * rows
    count = 1088
    own = pl.ds(pl.multiple_of(c * rows, rows), rows)
    sib = pl.ds(pl.multiple_of((1 - c) * rows, rows), rows)

    def piece(number, buf, route, col, width):
        def loc(sp, tp):
            where = col(tp)
            if not isinstance(where, int):
                where = pl.multiple_of(where, UNIT)
            return buf.at[rows_of(sp), pl.ds(where, width)]

        return Gather(h, number, loc(s, t), loc, route, send, recv)

    A = ([piece(0, wa, "zx", lambda tp: 0, 512),
          piece(1, wa, "kv", lambda tp: 512 + 512 * tp, 512)],
         [piece(7, wa, "zx", lambda tp: 1536, 128),
          piece(8, wa, "kv", lambda tp: 1664 + 128 * tp, 128)])
    O = ([piece(2, wog.at[c], "zx", lambda tp: 0, 512)],
         [piece(9, wog.at[c], "zx", lambda tp: 512, 128)])
    I = ([piece(3, wi, "zxy", lambda tp: 1024 * tp, 640),
          piece(4, wi, "zyx", lambda tp: 1024 * tp + 640, 384)],
         [piece(10, wi, "zyx", lambda tp: 2048 + 128 * tp, 128)])
    U = ([piece(5, wu, "zxy", lambda tp: 1024 * tp, 640),
          piece(6, wu, "zyx", lambda tp: 1024 * tp + 640, 384)],
         [piece(11, wu, "zyx", lambda tp: 2048 + 128 * tp, 128)])

    def each(group, stage, *args):
        for p in group[0]:
            getattr(p, stage)(*args)

        @pl.when(c == 0)
        def _():
            for p in group[1]:
                getattr(p, stage)(*args)

    def small_copy(sp, device, i):
        return remote(sm.at[sp], sm.at[sp], ssend.at[i], srecv.at[sp], device)

    loads = [pltpu.make_async_copy(src, dst, lsem.at[n]) for n, (src, dst) in enumerate((
        (w_qkv_h, w_qkv), (w_o_h, w_o), (tok_h, tok), (w_in_h, w_in), (w_out_h, w_out),
        (cot_h, cot_in)))]
    for copy in loads:
        copy.start()
    wide = lambda v: v.astype(F32)

    def deep(v):
        return jnp.concatenate([v, jnp.zeros((8, v.shape[1]), F32)], axis=0).astype(BF)

    def either(make):
        pl.when(c == 0)(lambda: make(0))
        pl.when(c == 1)(lambda: make(1))

    @pl.when(c == 1)
    def _():
        wi[:, 2048:2304] = jnp.zeros((1152, 256), BF)
        wu[:, 2048:2304] = jnp.zeros((1152, 256), BF)
        wa[:, 1536:1920] = jnp.zeros((1152, 384), BF)

    sm[s] = jnp.zeros((8, 256), F32)
    sm[s, 0:2, 0:136] = wide(gains[...])
    sm[s, 2:4, 0:136] = wide(shifts[...])
    sm[s, 4:8, 0:136] = wide(biases[...])
    loads[0].wait()

    def columns(core):
        for i in range(3):
            base = 1088 * i + 576 * core
            wa[rows_of(s), 512 * i:512 * i + 512] = deep(wide(w_qkv[:, base:base + 512]))
            if core == 0:
                wa[rows_of(s), 1536 + 128 * i:1664 + 128 * i] = deep(jnp.concatenate(
                    [wide(w_qkv[:, base + 512:base + 576]), jnp.zeros((136, 64), F32)], axis=1))

    either(columns)
    h.greet()
    for i, zp in enumerate(h.peers):
        small_copy(s, h.zdev(zp), i).start()
    small_copy(s, h.xdev, 3).start()
    each(A, "own_z")
    each(A, "own_two")
    feature = lax.broadcasted_iota(jnp.int32, (1088, 1), 0)
    place = feature + 8 * (feature // 136)
    spread[...] = (lax.broadcasted_iota(jnp.int32, (1088, 1152), 1) == place).astype(BF)
    loads[1].wait()

    def o_columns(core):
        at = slice(512 * core, 512 * core + 512)
        wog[core, rows_of(s), 0:512] = deep(mm(w_o[...], spread[:, at]))
        if core == 0:
            wog[core, rows_of(s), 512:640] = deep(mm(w_o[...], spread[:, 1024:1152]))

    either(o_columns)
    each(O, "own_z")
    for copy in loads[3:5]:
        copy.wait()

    def own_units(core):
        low = 1152 * core
        for src, dst in ((w_in, wi), (w_out, wu)):
            dst[rows_of(s), pl.ds(pl.multiple_of(t * 1024, UNIT), 1024)] = deep(
                wide(src[:, low:low + 1024]))
            if core == 0:
                dst[rows_of(s), pl.ds(pl.multiple_of(2048 + t * 128, UNIT), 128)] = deep(
                    wide(src[:, 1024:1152]))
        size = 1152 - 128 * core
        bins[t, :, 0:size] = jnp.broadcast_to(wide(b_in[0:1, low:low + size]), (8, size))
        if core == 1:
            bins[t, :, 1024:1152] = jnp.zeros((8, 128), F32)

    either(own_units)
    bin_copy = remote(bins.at[t], bins.at[t], ssend.at[7], srecv.at[8], h.ydev)
    bin_copy.start()
    each(I, "own_three")

    def spread_out(src, dst, to):
        @pl.loop(0, 3)
        def _(i):
            at = pl.ds(pl.multiple_of(384 * i, UNIT), 384)
            dst[to, at] = lax.dot_general(
                src[...], spread[:, at], (((0,), (0,)), ((), ())), preferred_element_type=F32
            ).astype(BF)

    loads[2].wait()
    spread_out(tok, x_ref, pl.ds(0, rows))
    ids = jnp.broadcast_to(seg[...], (8, 1024))
    segr[...] = ids
    segc[...] = ids.T

    top = 0
    for b in range(4):
        first = max(0, b - 2)
        width = (b + 1 - first) * 256
        kpos = lax.broadcasted_iota(jnp.int32, (width, 256), 0) + first * 256
        qpos = lax.broadcasted_iota(jnp.int32, (width, 256), 1) + b * 256
        seen = (kpos <= qpos) & (
            segc[first * 256:first * 256 + width, 0:1] == segr[0:1, b * 256:b * 256 + 256]
        )
        mb[top:top + width, :] = jnp.where(seen, 0.0, -1e30)
        top += width

    for k, zp in enumerate(h.peers):
        sp = 2 * zp + h.x
        small_copy(sp, h.xdev, 4 + k).wait_recv()
        small_copy(sp, h.xdev, 4 + k).start()
    each(A, "z", 0)
    for zp in [h.z] + h.peers:
        small_copy(2 * zp + h.xb, h.xdev, 0).wait_recv()

    padded = jnp.zeros((8, 1152), F32)
    natural = jnp.zeros((8, 1152), F32)
    for sp in range(8):
        wide = jnp.concatenate([sm[sp], jnp.zeros((8, 896), F32)], axis=1)
        padded = padded + (pltpu.roll(wide, 144 * sp, 1) if sp else wide)
        natural = natural + (pltpu.roll(wide, 136 * sp, 1) if sp else wide)
    par[0:8] = padded
    shifted = pltpu.roll(natural, 576, 1)
    par[8:16] = jnp.where(c == 0, natural, shifted)
    mask = real_features()
    each(A, "second", 0)
    loads[5].wait()
    spread_out(cot_in, cot, own)
    cot_copy = remote(cot.at[own], cot.at[own], dsend.at[0], drecv.at[0], h.core)
    cot_copy.start()

    @pl.loop(0, rows // 128)
    def _(i):
        at = pl.ds(pl.multiple_of(i * 128, 128), 128)
        to = pl.ds(pl.multiple_of(c * rows + i * 128, 128), 128)
        n1[to, :] = normalise(
            x_ref[at, :].astype(F32), mask, par[0:1, :], par[2:3, :], count
        ).astype(BF)

    n1_copy = remote(n1.at[own], n1.at[own], dsend.at[1], drecv.at[1], h.core)
    n1_copy.start()

    outs = []

    def flush(src, dst):
        copy = pltpu.make_async_copy(src, dst, osem.at[len(outs)])
        copy.start()
        outs.append(copy)

    flush(par, par_o)
    flush(mb, mb_o)
    flush(x_ref, x_o)

    def turn(src, dst, i, later):
        slot = i % 2
        if later:
            pltpu.make_async_copy(stage.at[slot], dst.at[:, 0:256], isem.at[slot]).wait()
        stage[slot] = src[256 * i:256 * i + 256, :].T
        pltpu.make_async_copy(
            stage.at[slot], dst.at[:, pl.ds(256 * i, 256)], isem.at[slot]).start()

    each(A, "z", 1)
    each(I, "own_z")
    each(A, "second", 1)
    cot_copy.wait_recv()
    flush(cot, cot_o)
    for i in range(2):
        cott[:, 256 * i:256 * i + 256] = cot[256 * i:256 * i + 256, :].T
    each(A, "z", 2)
    each(O, "own_two")
    each(O, "z", 0)
    each(A, "second", 2)
    n1_copy.wait_recv()
    for i in range(2):
        turn(n1, n1t_o, i, False)
    each(O, "z", 1)
    each(A, "second", 3)
    each(O, "z", 2)
    each(I, "own_two")
    each(I, "z", 0)

    def project(i, col, width, name, first_head):
        at = pl.ds(pl.multiple_of(i * 512, 512), 512)
        got = mm(n1[at, :], wa[:, col:col + width])
        where = 64 * first_head
        if name != "k":
            row = 12 if name == "q" else 13
            got = got + par[row:row + 1, where:where + width]
        low = got.astype(BF)
        if name == "q":
            low = low * jnp.asarray(0.125, BF)
        natural_ref, turned = {"q": (qn, qt), "k": (kn, kt), "v": (vn, vt)}[name]
        turned[where:where + width, at] = low.T
        natural_ref[at, where:where + width] = low

    for j in range(2):
        @pl.loop(0, 2)
        def _(i):
            project(i, 256 * j, 256, "q", 4 * j)
    for k in range(4):
        each(A, "third", k)
    for name, col in (("k", 512), ("v", 1024)):
        for j in range(2):
            @pl.loop(0, 2)
            def _(i):
                project(i, col + 256 * j, 256, name, 4 * j)
    each(I, "z", 1)
    each(U, "own_z")
    each(I, "second", 0)

    @pl.when(c == 0)
    def _():
        for name, col in (("q", 1536), ("k", 1664), ("v", 1792)):
            @pl.loop(0, 2)
            def _(i):
                project(i, col, 128, name, 8)

    @pl.when(c == 1)
    def _():
        for turned in (qt, kt, vt):
            turned[512:640, :] = jnp.zeros((128, length), BF)
        for natural_ref in (qn, kn, vn):
            natural_ref[:, 512:640] = jnp.zeros((length, 128), BF)

    flush(wa, wa_o)
    for src, dst in ((qn, qn_o), (kn, kn_o), (vn, vn_o), (qt, qt_o), (kt, kt_o)):
        flush(src, dst)
    lse[...] = jnp.zeros_like(lse)
    ot[c, 512:640, :] = jnp.zeros((128, length), BF)

    def attend(head):
        feat = pl.ds(pl.multiple_of(head * 64, 64), 64)
        pair = pl.ds(pl.multiple_of(head // 2 * 128, 128), 128)
        mine = lax.broadcasted_iota(jnp.int32, (128, 256), 0) // 64 == lax.rem(head, 2)
        top = 0
        for b in range(4):
            first = max(0, b - 2)
            width = (b + 1 - first) * 256
            keys = slice(first * 256, first * 256 + width)
            cols = slice(b * 256, b * 256 + 256)
            scores = mm(kn[keys, pair], jnp.where(mine, qt[pair, cols], jnp.zeros((), BF)))
            scores = scores + mb[top:top + width, :]
            top += width
            highest = jnp.max(scores, axis=0, keepdims=True)
            weights = jnp.exp(scores - highest)
            total = jnp.sum(weights, axis=0, keepdims=True)
            probs = (weights * (1.0 / total)).astype(BF)
            ot[c, feat, cols] = mm(vt[feat, keys], probs).astype(BF)
            lse[pl.ds(head, 1), cols] = highest + jnp.log(total)

    def heads(low, high):
        @pl.loop(low, high)
        def _(head):
            attend(head)

    each(I, "z", 2)
    each(O, "second", 0)
    heads(0, 2)
    each(O, "second", 1)
    each(O, "second", 2)
    each(I, "second", 1)
    each(U, "own_two")
    each(U, "own_three")
    heads(2, 4)
    each(O, "second", 3)
    wo_copy = remote(wog.at[c], wog.at[c], dsend.at[2], drecv.at[2], h.core)
    wo_copy.start()
    each(I, "second", 2)
    each(U, "z", 0)
    heads(4, 6)
    each(I, "second", 3)
    each(I, "third", 0)
    each(U, "z", 1)
    heads(6, 9 - c)
    each(U, "second", 0)
    each(I, "third", 1)
    each(U, "z", 2)

    flush(lse, lse_o)
    for i in range(2):
        at = pl.ds(pl.multiple_of(c * rows + 256 * i, 256), 256)
        att[c, 256 * i:256 * i + 256, :] = ot[c, :, at].T
    for i in range(2):
        at = pl.ds(pl.multiple_of((1 - c) * rows + 256 * i, 256), 256)
        vt[256 * i:256 * i + 256, 0:640] = ot[c, :, at].T
    att_copy = remote(vt.at[0:rows, 0:640], att.at[c], dsend.at[3], drecv.at[3], h.core)
    att_copy.start()
    ot_copy = remote(ot.at[c], ot.at[c], dsend.at[4], drecv.at[4], h.core)
    ot_copy.start()
    each(U, "second", 1)

    wo_copy.wait_recv()

    def order_rows(half, src, to, width):
        for sp in range(8):
            slope[136 * sp:136 * sp + 136, 0:width] = (
                wog[half, 144 * sp:144 * sp + 144, src:src + width].astype(F32)[0:136])
        wo[0:576, to:to + width] = slope[0:576, 0:width].astype(BF)
        wo[640:1152, to:to + width] = slope[576:1088, 0:width].astype(BF)

    for half in range(2):
        for q in range(2):
            order_rows(half, 256 * q, 512 * half + 256 * q, 256)
    order_rows(0, 512, 1024, 128)
    wo[576:640, :] = jnp.zeros((64, 1152), BF)
    wo[1152:1280, :] = jnp.zeros((128, 1152), BF)
    flush(wo.at[pl.ds(pl.multiple_of(c * 640, 128), 640)], wo_o)
    att_copy.wait_recv()
    att_copy.wait_send()
    each(I, "third", 2)

    @pl.loop(0, 4)
    def _(i):
        at = pl.ds(pl.multiple_of(i * 128, 128), 128)
        to = pl.ds(pl.multiple_of(c * rows + i * 128, 128), 128)
        x = (
            x_ref[at, :].astype(F32)
            + (mm(att[0, at, :], wo[0:640, :]) + mm(att[1, at, :], wo[640:1280, :]))
            + par[6:7, :]
        )
        mid[at, :] = x
        n2[to, :] = normalise(x, mask, par[1:2, :], par[3:4, :], count).astype(BF)

    flush(mid, mid_o)
    n2_copy = remote(n2.at[own], n2.at[own], dsend.at[5], drecv.at[5], h.core)
    n2_copy.start()
    ot_copy.wait_recv()
    flush(ot, ot_o)
    for i in range(2, 4):
        cott[:, 256 * i:256 * i + 256] = cot[256 * i:256 * i + 256, :].T
        turn(n1, n1t_o, i, True)
    n2_copy.wait_recv()
    for i in range(4):
        turn(n2, n2t_o, i, True)
    each(I, "third", 3)
    flush(wi, wi_o)
    bin_copy.wait_recv()
    root = math.sqrt(2.0 / math.pi)

    def slot_copies(slot, cols):
        base = pl.multiple_of(1024 * slot, 1024)
        return (
            pltpu.make_async_copy(slope.at[pl.ds(base, 1024)], slope_o.at[:, cols], isem.at[2 + slot]),
            pltpu.make_async_copy(act.at[slot], act_o.at[:, cols], isem.at[4 + slot]),
            pltpu.make_async_copy(tile.at[slot], go_o.at[:, :, :, cols], isem.at[6 + slot]),
        )

    def hidden(i):
        j = jnp.where(i < 4, 4 * h.tb + i, jnp.where(i < 8, 4 * t + i - 4, 8))
        slot = lax.rem(i, 2)
        base = pl.multiple_of(1024 * slot, 1024)
        cols = pl.ds(pl.multiple_of(j * 256, 256), 256)

        @pl.when(i >= 2)
        def _():
            for copy in slot_copies(slot, cols):
                copy.wait()
        half = j // 4
        off = pl.multiple_of(256 * (j - 4 * half), 256)
        bias = jnp.where(
            j < 8,
            bins[pl.ds(jnp.minimum(half, 1), 1), 0:1, pl.ds(jnp.where(j < 8, off, 0), 256)][0],
            jnp.concatenate([bins[0, 0:1, 1024:1152], bins[1, 0:1, 1024:1152]], axis=1),
        )

        @pl.loop(0, 4)
        def _(q):
            at = pl.ds(pl.multiple_of(q * 256, 256), 256)
            v = mm(n2[at, :], wi[:, cols]) + bias
            square = v * v
            bent = jnp.tanh(root * (v + 0.044715 * square * v))
            act[slot, at, :] = (0.5 * v * (1.0 + bent)).astype(BF)
            slope[pl.ds(pl.multiple_of(base + 256 * q, 256), 256), :] = (
                0.5 * (1.0 + bent) + (0.5 * root) * v * (1.0 - bent * bent) * (
                    1.0 + (3.0 * 0.044715) * square))

        @pl.loop(0, 2)
        def _(half):
            got = mm(cott[pl.ds(pl.multiple_of(576 * half, 576), 576), :], act[slot])
            for q in range(4):
                tile[slot, 2 * half + q // 2, q % 2] = got[144 * q:144 * q + 144, :].astype(BF)
        for copy in slot_copies(slot, cols):
            copy.start()

    def units(low, high):
        @pl.loop(low, high)
        def _(i):
            hidden(i)

    def last_rows(k):
        each(U, "third", k)
        at = pl.ds(pl.multiple_of(2 * BR * ([h.z] + h.peers)[k], 16), 2 * BR)
        flush(wu.at[at], wu_o.at[at])

    units(0, 1)
    each(U, "second", 2)
    units(1, 2)
    each(U, "second", 3)
    units(2, 4)
    last_rows(0)
    units(4, 6)
    last_rows(1)
    units(6, 9 - c)
    last_rows(2)
    last_rows(3)
    for slot in range(2):
        for copy in slot_copies(slot, pl.ds(0, 256)):
            copy.wait()
    for slot in range(2):
        pltpu.make_async_copy(stage.at[slot], n2t_o.at[:, 0:256], isem.at[slot]).wait()
    for copy in outs:
        copy.wait()
    for i in range(7):
        small_copy(s, h.xdev, i).wait_send()
    for copy in (bin_copy, cot_copy, n1_copy, wo_copy, ot_copy, n2_copy):
        copy.wait_send()
    for group in (A, O, I, U):
        each(group, "drain")


def run_forward(tokens, segment_ids, norm_gains, norm_shifts, biases, w_qkv, w_o, w_in, b_in,
                w_out, cotangent):
    hbm = pl.BlockSpec(memory_space=pltpu.HBM)
    vmem = pl.BlockSpec(memory_space=pltpu.VMEM)
    sds = jax.ShapeDtypeStruct
    shapes = [
        sds((1152, 1920), BF), sds((640, 1152), BF), sds((1152, 2304), BF), sds((1152, 2304), BF),
        sds((1152, 1024), BF), sds((1152, 1024), BF), sds((1024, 1152), BF),
        sds((1024, 640), BF), sds((1024, 640), BF), sds((1024, 640), BF),
        sds((640, 1024), BF), sds((640, 1024), BF), sds((2, 640, 1024), BF),
        sds((16, 1024), F32), sds((512, 1152), F32), sds((1024, 2304), F32), sds((1024, 2304), BF),
        sds((4, 2, 144, 2304), BF), sds((16, 1152), F32), sds((2304, 256), F32), sds((512, 1152), BF),
    ]
    V = pltpu.VMEM
    dma = pltpu.SemaphoreType.DMA
    scratch = [
        V((1152, 1920), BF), V((2, 1152, 640), BF), V((1280, 1152), BF), V((1152, 2304), BF),
        V((1152, 2304), BF), V((1024, 1152), BF), V((1024, 1152), BF), V((1152, 1024), BF),
        V((1024, 1152), BF),
        V((8, 8, 256), F32), V((16, 1152), F32), V((2, 8, 1152), F32),
        V((1024, 640), BF), V((1024, 640), BF), V((1024, 640), BF),
        V((640, 1024), BF), V((640, 1024), BF), V((640, 1024), BF),
        V((2304, 256), F32), V((2, 640, 1024), BF), V((2, 512, 640), BF), V((512, 1152), F32),
        V((2048, 256), F32), V((2, 1024, 256), BF), V((2, 4, 2, 144, 256), BF),
        V((2, 1152, 256), BF), V((16, 1024), F32), V((512, 1152), BF), V((8, 1024), jnp.int32), V((1024, 8), jnp.int32),
        V((1088, 512), BF), V((1088, 512), BF), V((136, 3264), BF), V((136, 1088), BF),
        V((136, 2176), BF), V((136, 2176), BF), V((1088, 1152), BF),
        dma((12, 18)), dma((12, 16)), dma((6,)), dma((6,)), dma((8,)), dma((9,)), dma((12,)),
        dma((20,)), dma((8,)),
    ]
    kept = pl.pallas_call(
        forward_kernel, out_shape=shapes, in_specs=[vmem] * 5 + [hbm] * 6, out_specs=[hbm] * len(shapes),
        scratch_shapes=scratch,
        compiler_params=pltpu.CompilerParams(
            collective_id=0, has_side_effects=True, vmem_limit_bytes=63 << 20),
        cost_estimate=pl.CostEstimate(flops=12 * 10**9, bytes_accessed=60 * 10**6, transcendentals=10**7),
        name="forward",
    )(segment_ids, norm_gains, norm_shifts, biases, b_in.reshape(1, -1), tokens[0].T, cotangent[0].T,
      w_qkv, w_o, w_in, w_out.T)
    return kept


def nt(left, right):
    return lax.dot_general(left, right, (((1,), (1,)), ((), ())), preferred_element_type=F32)


def backward_kernel(
    par, lse, wa_h, wo_h, wi_h, wu_h, n1t_h, n2t_h, cot_h, qn_h, kn_h, vn_h, qt_h,
    kt_h, ot_h, mid_h, slope_h, act_h, go_h, mb_h, x_h,
    mixed_o, tokens_o, out_o, in_o, qkv_o, proj_o, sums_o,
    WI, WU, ACT, IG, COT, COTT, N2T, inner, F1, F2, F3, F4, mix, yr, xr, x1, y2, zr, gi, held, early,
    acck, accv, vyr, xra, zra, ysa, yra, go, xro, zro, yso, yro, sg, sgx, sgz, sgy, bsum,
    load, innersem, heldsem, ysend, yrecv, xsend, xrecv, isend, irecv, zsend, zrecv,
    axs, axr, azs, azr, ays, ayr, oxs, oxr, ozs, ozr, oys, oyr, gsend, grecv, dsend, drecv,
    outsem, finsend, finrecv, finloc,
):
    h = Place()
    c, s, t, z, x = h.c, h.s, h.t, h.z, h.x
    rows = 512
    count = 1088.0
    own0 = pl.multiple_of(c * rows, rows)
    sib0 = pl.multiple_of((1 - c) * rows, rows)
    n_tiles = 9 - c

    def fetch(n, src, dst):
        copy = pltpu.make_async_copy(src, dst, load.at[n])
        copy.start()
        return copy

    def tile_of(i):
        return jnp.where(i < 4, 4 * h.tb + i, jnp.where(i < 8, 4 * t + i - 4, 8))

    def inner_copy(i):
        slot = lax.rem(i, 2)
        return pltpu.make_async_copy(
            slope_h.at[:, pl.ds(pl.multiple_of(256 * tile_of(i), 256), 256)],
            inner.at[pl.ds(pl.multiple_of(1024 * slot, 1024), 1024)], innersem.at[slot])

    inner_copy(0).start()
    first = [fetch(0, cot_h, COT), fetch(1, wu_h, WU)]
    h.greet()

    @pl.when(c == 1)
    def _():
        IG[:, 2048:2304] = jnp.zeros((1024, 256), BF)
    sg[...] = jnp.zeros_like(sg)

    def cols_of(k):
        return slice(256 * k, 256 * k + 256) if k < 4 else slice(1024, 1152)

    def theirs(k):
        return pl.ds(pl.multiple_of(1024 * h.tb + 256 * k if k < 4 else 2048 + 128 * h.tb, 128),
                     256 if k < 4 else 128)

    def ours(k):
        return pl.ds(pl.multiple_of(1024 * t + 256 * k if k < 4 else 2048 + 128 * t, 128),
                     256 if k < 4 else 128)

    def slot_at(zp):
        return lax.rem(z - zp + 3, 4)

    def only(k, step):
        if k < 4:
            step()
        else:
            pl.when(c == 0)(step)

    def oy(k):
        return remote(go_h.at[:, :, :, theirs(k)], yr.at[:, :, :, cols_of(k)],
                      ysend.at[0, k], yrecv.at[0, k], h.ydev)

    def ox(k):
        cols = cols_of(k)
        return remote(yr.at[:, h.xb, :, cols], xr.at[:, :, cols], xsend.at[k], xrecv.at[k], h.xdev)

    near = h.peers[0]
    far = jnp.where(z < 2, z + 2, z - 2)

    def z_one(m, k, i):
        cols = cols_of(k)
        return remote((xr, y2)[m].at[lax.rem(near, 2) + 2 * i, :, cols], zr.at[m, i, :, cols],
                      zsend.at[m, k, i], zrecv.at[m, k, i], h.zdev(near))

    def z_two(m, k):
        cols = cols_of(k)
        return remote((xr, y2)[m].at[far, :, cols], zr.at[m, 2, :, cols],
                      zsend.at[m, k, 2], zrecv.at[m, k, 2], h.zdev(far))

    def MZ(m, k):
        def step():
            cols = cols_of(k)
            src = (xr, y2)[m]
            for i in range(2):
                z_one(m, k, i).wait_recv()
                at = lax.rem(z, 2) + 2 * i
                src[at, :, cols] = (
                    src[at, :, cols].astype(F32) + zr[m, i, :, cols].astype(F32)).astype(BF)
            z_two(m, k).start()
        only(k, step)

    def held_copy(k):
        return pltpu.make_async_copy(
            go_h.at[:, :, :, ours(k)], held.at[:, :, :, 0:256 if k < 4 else 128], heldsem.at[0])

    def OY(k):
        def step():
            cols = cols_of(k)
            width = cols.stop - cols.start
            oy(k).wait_recv()
            held_copy(k).wait()

            @pl.loop(0, 4)
            def _(zp):
                for xp in range(2):
                    yr[zp, xp, :, cols] = (
                        yr[zp, xp, :, cols].astype(F32) + held[zp, xp, :, 0:width].astype(F32)
                    ).astype(BF)
            ox(k).start()
        only(k, step)
        if k < 4:
            only(k + 1, lambda: held_copy(k + 1).start())

    def OX(k):
        def step():
            cols = cols_of(k)
            ox(k).wait_recv()

            @pl.loop(0, 4)
            def _(zp):
                xr[zp, :, cols] = (
                    xr[zp, :, cols].astype(F32) + yr[zp, x, :, cols].astype(F32)).astype(BF)
            for i in range(2):
                z_one(0, k, i).start()
        only(k, step)

    def LZ(m, k):
        def step():
            cols = cols_of(k)
            z_two(m, k).wait_recv()
            F4[144 * m:144 * m + 144, cols] = (
                (xr, y2)[m][z, :, cols].astype(F32) + zr[m, 2, :, cols].astype(F32))
        only(k, step)

    def tile_cols(i):
        return pl.ds(pl.multiple_of(256 * tile_of(i), 256), 256)

    def ix(i):
        cols = tile_cols(i)
        return remote(gi.at[:, h.xb, :, cols], x1.at[:, :, cols],
                      isend.at[i], irecv.at[i], h.xdev)

    def iy(k):
        return remote(x1.at[:, :, theirs(k)], y2.at[:, :, cols_of(k)],
                      ysend.at[1, k], yrecv.at[1, k], h.ydev)

    def IX(i):
        def step():
            cols = tile_cols(i)
            ix(i).wait_recv()

            @pl.loop(0, 4)
            def _(zp):
                x1[zp, :, cols] = (
                    x1[zp, :, cols].astype(F32) + gi[zp, x, :, cols].astype(F32)).astype(BF)
            if i < 4:
                iy(i).start()
            if i == 8:
                iy(4).start()
        only(4 if i == 8 else 0, step)

    def IY(k):
        def step():
            cols = cols_of(k)
            iy(k).wait_recv()

            @pl.loop(0, 4)
            def _(zp):
                y2[zp, :, cols] = (
                    y2[zp, :, cols].astype(F32) + x1[zp, :, ours(k)].astype(F32)).astype(BF)
            for i in range(2):
                z_one(1, k, i).start()
        only(k, step)

    for k in range(5):
        only(k, lambda: oy(k).start())
    held_copy(0).start()

    for copy in first:
        copy.wait()
    second = [fetch(3, n2t_h, N2T), fetch(4, wi_h, WI), fetch(5, mid_h, F4), fetch(2, act_h, ACT)]

    def hidden(i):
        base = pl.multiple_of(1024 * lax.rem(i, 2), 1024)
        inner_copy(i).wait()

        @pl.when(i + 1 < n_tiles)
        def _():
            inner_copy(i + 1).start()
        cols = pl.ds(pl.multiple_of(256 * tile_of(i), 256), 256)
        bsum[...] = jnp.zeros_like(bsum)

        @pl.loop(0, 4)
        def _(q):
            at = pl.ds(pl.multiple_of(256 * q, 256), 256)
            v = inner[pl.ds(pl.multiple_of(base + 256 * q, 256), 256), :]
            low = (mm(COT[at, :], WU[:, cols]) * v).astype(BF)
            IG[at, cols] = low
            bsum[0:1, :] = bsum[0:1, :] + jnp.sum(low.astype(F32), axis=0, keepdims=True)

        @pl.when(i == 0)
        def _():
            second[0].wait()

        @pl.loop(0, 2)
        def _(half):
            got = mm(N2T[pl.ds(pl.multiple_of(576 * half, 576), 576), :], IG[:, cols])
            line = lax.broadcasted_iota(jnp.int32, (16, 256), 0) == 8
            for q in range(4):
                block = got[144 * q:144 * q + 144, :]
                zp, xp = 2 * half + q // 2, q % 2
                gi[zp, xp, 0:128, cols] = block[0:128].astype(BF)
                gi[zp, xp, 128:144, cols] = jnp.where(line, bsum[0:1, :], block[128:144]).astype(BF)

        ix(i).start()

    def units(low, high):
        @pl.loop(low, high)
        def _(i):
            hidden(i)

    units(0, 5)
    OY(0)
    IX(0)
    units(5, 9 - c)
    IX(1)
    IX(2)

    for copy in second[1:]:
        copy.wait()
    @pl.when(c == 1)
    def _():
        ACT[:, 2048:2304] = jnp.zeros((1024, 256), BF)


    def n2_copy(i):
        at = pl.ds(pl.multiple_of(384 * i, 128), 384)
        return remote(F3.at[:, at], F2.at[:, at], dsend.at[i], drecv.at[i], h.core)

    @pl.loop(0, 3)
    def _(i):
        at = pl.ds(pl.multiple_of(384 * i, 128), 384)
        F3[:, at] = nt(IG[pl.ds(sib0, rows), :], WI[at, :]).astype(BF)
        n2_copy(i).start()

    @pl.loop(0, 3)
    def _(i):
        at = pl.ds(pl.multiple_of(384 * i, 128), 384)
        F1[:, at] = nt(IG[pl.ds(own0, rows), :], WI[at, :])
    n2_sends = [n2_copy(i) for i in range(3)]
    OY(1)
    IX(3)

    wo_load = fetch(6, wo_h, WI.at[0:640, 0:1152])
    q_loads = [fetch(7, qn_h, IG.at[:, 0:640]), fetch(8, kn_h, IG.at[:, 640:1280]),
               fetch(9, vn_h, IG.at[:, 1280:1920]),
               fetch(10, mb_h, inner), fetch(11, n1t_h, N2T)]


    def mix_copy(i):
        at = pl.ds(pl.multiple_of(384 * i, 128), 384)
        return remote(WI.at[640:1152, at], mix.at[:, at], dsend.at[3 + i], drecv.at[3 + i], h.core)

    @pl.loop(0, 3)
    def _(i):
        at = pl.ds(pl.multiple_of(384 * i, 128), 384)
        WI[640:1152, at] = nt(ACT[pl.ds(sib0, rows), :], WU[at, :]).astype(BF)
        mix_copy(i).start()
    mix_sends = [mix_copy(i) for i in range(3)]

    mask = real_features()
    for copy in n2_sends:
        copy.wait_recv()

    @pl.loop(0, 16)
    def _(q):
        at = pl.ds(pl.multiple_of(32 * q, 32), 32)
        to = pl.ds(pl.multiple_of(own0 + 32 * q, 32), 32)
        grad = F1[at, :] + F2[at, :].astype(F32)
        v = F4[at, :]
        mean = jnp.sum(v, axis=1, keepdims=True) * (1.0 / count)
        spread = (v - mean) * mask
        rstd = lax.rsqrt(jnp.sum(spread * spread, axis=1, keepdims=True) * (1.0 / count) + EPS)
        hat = spread * rstd
        scaled = grad * par[1:2, :]
        grad_out = COT[to, :].astype(F32)
        got = grad_out + rstd * (
            scaled - jnp.sum(scaled, axis=1, keepdims=True) * (1.0 / count)
            - hat * (jnp.sum(scaled * hat, axis=1, keepdims=True) * (1.0 / count))) * mask
        low = got.astype(BF)
        F1[at, :] = got
        COT[to, :] = low
        sg[3:4, 0:1152] = sg[3:4, 0:1152] + jnp.sum(grad * hat, axis=0, keepdims=True)
        sg[4:5, 0:1152] = sg[4:5, 0:1152] + jnp.sum(grad, axis=0, keepdims=True)
        sg[5:6, 0:1152] = sg[5:6, 0:1152] + jnp.sum(grad_out, axis=0, keepdims=True)
        sg[6:7, 0:1152] = sg[6:7, 0:1152] + jnp.sum(low.astype(F32), axis=0, keepdims=True)

    bg_copy = remote(COT.at[pl.ds(own0, rows)], COT.at[pl.ds(own0, rows)], dsend.at[6], drecv.at[6], h.core)
    bg_copy.start()
    IX(4)

    for copy in n2_sends:
        copy.wait_send()
    for copy in mix_sends:
        copy.wait_recv()

    @pl.loop(0, 3)
    def _(i):
        at = pl.ds(pl.multiple_of(384 * i, 128), 384)
        got = nt(ACT[pl.ds(own0, rows), :], WU[at, :]) + mix[:, at].astype(F32)
        F3[:, at] = (F4[:, at] + got + par[7:8, at]).astype(BF)
    mix_out = pltpu.make_async_copy(F3, mixed_o, outsem.at[0])
    mix_out.start()
    t_loads = [fetch(12, qt_h, WU.at[0:640, 0:1024]), fetch(13, kt_h, WU.at[0:640, 1024:2048])]
    OY(2)
    OX(0)
    o_loads = [fetch(14, ot_h.at[0], ACT.at[0:640, 0:1024]), fetch(15, ot_h.at[1], ACT.at[0:640, 1024:2048])]

    wo_load.wait()
    bg_copy.wait_recv()
    bg_copy.wait_send()
    for copy in mix_sends:
        copy.wait_send()

    @pl.loop(0, 5)
    def _(pair):
        at = pl.ds(pl.multiple_of(128 * pair, 128), 128)
        got = nt(COT[...], WI[at, 0:1152]).astype(BF)
        WI[0:1024, pl.ds(pl.multiple_of(1280 + 128 * pair, 128), 128)] = got
        COTT[at, :] = got.T

    IX(5)

    for copy in o_loads:
        copy.wait()

    def proj(col, to):
        part = COT[:, col]
        acck[0:576, :] = mm(ACT[0:576, 0:1024], part)
        acck[576:1088, :] = mm(ACT[0:512, 1024:2048], part)
        for sp in range(8):
            block = jnp.concatenate([acck[136 * sp:136 * sp + 136, :], jnp.zeros((8, 128), F32)], axis=0)
            go[sp // 2, sp % 2, :, to:to + 128] = block.astype(BF)

    ocols = (slice(0, 512), slice(512, 640))

    def oz_copy(k, i, zp):
        return remote(go.at[zp, :, :, ocols[k]], zro.at[slot_at(zp), :, :, ocols[k]],
                      ozs.at[k, i], ozr.at[k, slot_at(zp)], h.zdev(zp))

    def ox_copy(k):
        return remote(go.at[z, h.xb, :, ocols[k]], xro.at[:, ocols[k]], oxs.at[k], oxr.at[k], h.xdev)

    def o_send(k):
        for i, zp in enumerate(h.peers):
            oz_copy(k, i, zp).start()

    def oy_copy(k):
        return remote(yso.at[:, ocols[k]], yro.at[:, ocols[k]], oys.at[k], oyr.at[k], h.ydev)

    for q in range(4):
        proj(pl.ds(pl.multiple_of(512 * c + 128 * q, 128), 128), 128 * q)
    o_send(0)

    @pl.when(c == 0)
    def _():
        proj(slice(1024, 1152), 512)
        o_send(1)

    def o_after_z(k):
        cols = ocols[k]
        for i in range(3):
            ref = zro.at[i, :, :, cols]
            remote(ref, ref, ozs.at[k, 0], ozr.at[k, i], h.core).wait_recv()
        for xp in range(2):
            go[z, xp, :, cols] = (
                (go[z, xp, :, cols].astype(F32) + zro[0, xp, :, cols].astype(F32))
                + (zro[1, xp, :, cols].astype(F32) + zro[2, xp, :, cols].astype(F32))).astype(BF)
        ox_copy(k).start()

    def o_after_x(k):
        cols = ocols[k]
        ox_copy(k).wait_recv()
        yso[:, cols] = (go[z, x, :, cols].astype(F32) + xro[:, cols].astype(F32)).astype(BF)
        oy_copy(k).start()

    def o_after_y(k):
        oy_copy(k).wait_recv()
        F4[288:432, ocols[k]] = yso[:, ocols[k]].astype(F32) + yro[:, ocols[k]].astype(F32)

    def both(step, main, more):
        for k in main:
            step(k)

        @pl.when(c == 0)
        def _():
            for k in more:
                step(k)

    for copy in q_loads + t_loads:
        copy.wait()
    ACT[:, 1536:1920] = jnp.zeros((1024, 384), BF)
    WI[512:640, 0:1024] = jnp.zeros((128, 1024), BF)

    def attend(head):
        pair = head // 2
        parity = lax.rem(head, 2)
        both_heads = pl.ds(pl.multiple_of(pair * 128, 128), 128)
        feat = pl.ds(pl.multiple_of(head * 64, 64), 64)
        on_rows = lax.broadcasted_iota(jnp.int32, (128, 256), 0) // 64 == parity
        on_lanes = lax.broadcasted_iota(jnp.int32, (256, 128), 1) // 64 == parity
        zero = jnp.zeros((), BF)
        qcol = both_heads
        kcol = pl.ds(pl.multiple_of(640 + pair * 128, 128), 128)
        vcol = pl.ds(pl.multiple_of(1280 + pair * 128, 128), 128)

        @pl.when(parity == 0)
        def _():
            acck[0:1024, :] = jnp.zeros((1024, 128), F32)
            accv[...] = jnp.zeros_like(accv)
        top = 0
        for b in range(4):
            start = max(0, b - 2)
            width = (b + 1 - start) * 256
            keys = slice(start * 256, start * 256 + width)
            cols = slice(b * 256, b * 256 + 256)
            scores = mm(IG[keys, kcol], jnp.where(on_rows, WU[both_heads, cols], zero))
            probs = jnp.exp(scores + inner[top:top + width, :] - lse[pl.ds(head, 1), cols])
            top += width
            grads = mm(IG[keys, vcol], jnp.where(on_rows, COTT[both_heads, cols], zero))
            terms = jnp.sum(probs * grads, axis=0, keepdims=True)
            sgrad = (probs * (grads - terms)).astype(BF)
            accv[keys, :] = accv[keys, :] + mm(
                probs.astype(BF), jnp.where(on_lanes, WI[cols, vcol], zero))
            acck[keys, :] = acck[keys, :] + mm(
                sgrad, jnp.where(on_lanes, IG[cols, qcol], zero))
            WI[feat, cols] = (
                mm(WU[feat, 1024 + start * 256:1024 + start * 256 + width], sgrad) * 0.125
            ).astype(BF)

        @pl.when((parity == 1) | (head == 8 - c))
        def _():
            kto = pl.ds(pl.multiple_of(jnp.where(pair < 4, 512 + 128 * pair, 1664), 128), 128)
            vto = pl.ds(pl.multiple_of(jnp.where(pair < 4, 1024 + 128 * pair, 1792), 128), 128)
            ACT[:, kto] = acck[0:1024, :].astype(BF)
            ACT[:, vto] = accv[...].astype(BF)

    def heads(low, high):
        @pl.loop(low, high)
        def _(head):
            attend(head)

    acols = (slice(0, 256), slice(256, 512), slice(512, 640))

    def qcols(k):
        return slice(256 * k, 256 * k + 256) if k < 2 else slice(1536, 1664)

    def vcols(k, tp):
        start = 512 + 512 * tp + 256 * k if k < 2 else 1664 + 128 * tp
        return pl.ds(pl.multiple_of(start, 128), 256 if k < 2 else 128)

    def grads(k, tp=None):
        if k:
            return gi, (qcols(k) if tp is None else vcols(k, tp))
        return early, (slice(0, 256) if tp is None
                       else pl.ds(pl.multiple_of(256 + 256 * tp, 128), 256))

    def weights(k, tp=None):
        cols = qcols(k) if tp is None else vcols(k, tp)
        dst, to = grads(k, tp)

        @pl.loop(0, 2)
        def _(half):
            got = mm(N2T[pl.ds(pl.multiple_of(576 * half, 576), 576), :], ACT[:, cols])
            for q in range(4):
                dst[2 * half + q // 2, q % 2, :, to] = got[144 * q:144 * q + 144, :].astype(BF)

    def vy(k):
        src, cols = grads(k, h.tb)
        return remote(src.at[:, :, :, cols], vyr.at[:, :, :, acols[k]], ays.at[k], ayr.at[k],
                      h.ydev)

    def ax(m, k):
        buf, cols = grads(k) if m == 0 else (vyr, acols[k])
        src = buf.at[:, h.xb, :, cols]
        return remote(src, xra.at[m, :, :, acols[k]], axs.at[m, k], axr.at[m, k], h.xdev)

    def a_one(m, k, i):
        return remote(xra.at[m, lax.rem(near, 2) + 2 * i, :, acols[k]], zra.at[m, i, :, acols[k]],
                      azs.at[m, k, i], azr.at[m, k, i], h.zdev(near))

    def a_two(m, k):
        return remote(xra.at[m, far, :, acols[k]], zra.at[m, 2, :, acols[k]],
                      azs.at[m, k, 2], azr.at[m, k, 2], h.zdev(far))

    def AM(m, k):
        cols = acols[k]
        for i in range(2):
            a_one(m, k, i).wait_recv()
            at = lax.rem(z, 2) + 2 * i
            xra[m, at, :, cols] = (
                xra[m, at, :, cols].astype(F32) + zra[m, i, :, cols].astype(F32)).astype(BF)
        a_two(m, k).start()

    def ay(m, k):
        return remote(ysa.at[m, :, acols[k]], yra.at[m, :, acols[k]],
                      ays.at[3 + 3 * m + k], ayr.at[3 + 3 * m + k], h.ydev)

    def VY(k):
        vy(k).wait_recv()
        cols = acols[k]
        src, part = grads(k, t)

        @pl.loop(0, 4)
        def _(zp):
            for xp in range(2):
                vyr[zp, xp, :, cols] = (
                    vyr[zp, xp, :, cols].astype(F32) + src[zp, xp, :, part].astype(F32)
                ).astype(BF)
        ax(1, k).start()

    def AX(m, k):
        cols = acols[k]
        src, part = grads(k)
        ax(m, k).wait_recv()

        @pl.loop(0, 4)
        def _(zp):
            mine = src[zp, x, :, part] if m == 0 else vyr[zp, x, :, cols]
            xra[m, zp, :, cols] = (
                xra[m, zp, :, cols].astype(F32) + mine.astype(F32)).astype(BF)
        for i in range(2):
            a_one(m, k, i).start()

    def AZ(m, k):
        cols = acols[k]
        a_two(m, k).wait_recv()
        ysa[m, :, cols] = (
            xra[m, z, :, cols].astype(F32) + zra[m, 2, :, cols].astype(F32)).astype(BF)
        ay(m, k).start()

    def AY(m, k):
        ay(m, k).wait_recv()
        cols = acols[k]
        mine, other = ysa[m, :, cols].astype(F32), yra[m, :, cols].astype(F32)
        if k < 2:
            blocks = [(k, mine + other)] if m == 0 else [(2 + 2 * t + k, mine), (2 + 2 * h.tb + k, other)]
            for block, value in blocks:
                inner[pl.ds(pl.multiple_of(144 * block, 16), 144), :] = value
        elif m == 0:
            inner[864:1008, 0:128] = mine + other
        else:
            inner[864:1008, 128:256] = jnp.where(t == 0, mine, other)
            inner[1008:1152, 0:128] = jnp.where(t == 0, other, mine)

    def group(k):
        weights(k, h.tb)
        vy(k).start()
        weights(k)
        ax(0, k).start()
        weights(k, t)

    def turn(pair):
        at = slice(128 * pair, 128 * pair + 128)
        ACT[:, at if pair < 4 else slice(1536, 1664)] = WI[at, 0:1024].T

    def more(step, *args):
        @pl.when(c == 0)
        def _():
            step(*args, 2)

    IX(6)
    heads(0, 2)
    MZ(0, 0)
    OY(3)
    IX(7)
    heads(2, 4)
    turn(0)
    turn(1)
    group(0)
    IX(8)
    OY(4)
    IY(0)
    heads(4, 6)
    IY(1)
    LZ(0, 0)
    OX(1)
    MZ(1, 0)
    both(o_after_z, (0,), (1,))
    heads(6, 8)
    turn(2)
    turn(3)
    for n in range(9):
        only(4 if n == 8 else 0, lambda: ix(n).wait_send())
    group(1)
    MZ(0, 1)
    MZ(1, 1)
    IY(2)
    heads(8, 9 - c)

    @pl.when(c == 0)
    def _():
        turn(4)
        group(2)
    wa_load = fetch(16, wa_h, WI.at[:, 0:1920])
    x_load = fetch(17, x_h, COT.at[0:512])
    IY(3)
    IY(4)
    OX(2)
    MZ(1, 2)

    mix_out.wait()
    wa_load.wait()

    def n1_copy(i):
        at = pl.ds(pl.multiple_of(384 * i, 128), 384)
        return remote(F3.at[:, at], F2.at[:, at], dsend.at[7 + i], drecv.at[7 + i], h.core)

    @pl.loop(0, 3)
    def _(i):
        at = pl.ds(pl.multiple_of(384 * i, 128), 384)
        F3[:, at] = nt(ACT[pl.ds(sib0, rows), 0:1920], WI[at, 0:1920]).astype(BF)
        n1_copy(i).start()

    @pl.loop(0, 4)
    def _(i):
        at = pl.ds(pl.multiple_of(256 * i, 256), 256)
        inner[pl.ds(pl.multiple_of(512 * i, 512), 512), :] = nt(
            ACT[pl.ds(own0, rows), 0:1920], WI[at, 0:1920])
    part = nt(ACT[pl.ds(own0, rows), 0:1920], WI[1024:1152, 0:1920])
    inner[2048:2304, 0:128] = part[0:256]
    inner[2048:2304, 128:256] = part[256:512]
    n1_sends = [n1_copy(i) for i in range(3)]

    @pl.loop(0, 15)
    def _(i):
        at = pl.ds(pl.multiple_of(128 * i, 128), 128)
        sg[0:1, at] = jnp.sum(ACT[:, at].astype(F32), axis=0, keepdims=True)
    OX(3)
    OX(4)
    VY(0)
    MZ(0, 2)
    MZ(1, 3)
    MZ(1, 4)
    VY(1)
    MZ(0, 3)
    MZ(0, 4)
    LZ(0, 1)
    for n in range(3):
        LZ(1, n)
    both(o_after_x, (0,), (1,))
    more(VY)
    AX(0, 0)
    AX(0, 1)
    x_load.wait()
    for copy in n1_sends:
        copy.wait_recv()

    @pl.loop(0, 16)
    def _(i):
        at = pl.ds(pl.multiple_of(32 * i, 32), 32)
        half = i // 8
        tail = inner[pl.ds(pl.multiple_of(2048 + 32 * (i - 8 * half), 32), 32),
                     pl.ds(pl.multiple_of(128 * half, 128), 128)]
        part = jnp.concatenate(
            [inner[pl.ds(pl.multiple_of(512 * j + 32 * i, 32), 32), :] for j in range(4)] + [tail],
            axis=1)
        grad = part + F2[at, :].astype(F32)
        v = COT[at, :].astype(F32)
        mean = jnp.sum(v, axis=1, keepdims=True) * (1.0 / count)
        spread = (v - mean) * mask
        rstd = lax.rsqrt(jnp.sum(spread * spread, axis=1, keepdims=True) * (1.0 / count) + EPS)
        hat = spread * rstd
        scaled = grad * par[0:1, :]
        F1[at, :] = F1[at, :] + rstd * (
            scaled - jnp.sum(scaled, axis=1, keepdims=True) * (1.0 / count)
            - hat * (jnp.sum(scaled * hat, axis=1, keepdims=True) * (1.0 / count))) * mask
        sg[1:2, 0:1152] = sg[1:2, 0:1152] + jnp.sum(grad * hat, axis=0, keepdims=True)
        sg[2:3, 0:1152] = sg[2:3, 0:1152] + jnp.sum(grad, axis=0, keepdims=True)

    tok_outs = [pltpu.make_async_copy(F1, tokens_o, outsem.at[1])]
    tok_outs[0].start()

    sgx_copy = remote(sg, sgx, gsend.at[0], grecv.at[0], h.xdev)
    sgx_copy.start()
    more(AX, 0)
    AM(0, 0)
    AM(0, 1)
    more(AM, 0)
    sgx_copy.wait()
    sgx[...] = sgx[...] + sg[...]

    def sgz_copy(i, zp):
        return remote(sgx, sgz.at[slot_at(zp)], gsend.at[1 + i], grecv.at[1 + slot_at(zp)], h.zdev(zp))

    for i, zp in enumerate(h.peers):
        sgz_copy(i, zp).start()
    both(o_after_y, (0,), (1,))
    for n in range(2, 5):
        LZ(0, n)
    for n in range(3, 5):
        LZ(1, n)

    finals = []

    def deliver(n, src, out):
        local = pltpu.make_async_copy(src, out.at[c], finloc.at[n])
        local.start()
        over = remote(src, out.at[c], finsend.at[n], finrecv.at[n], h.core)
        over.start()
        finals.append((local, over))

    deliver(0, F4.at[288:432, 0:640], proj_o)
    deliver(1, F4.at[0:144], out_o)
    deliver(2, F4.at[144:288], in_o)
    AX(1, 0)
    AX(1, 1)
    more(AX, 1)
    AM(1, 0)
    AM(1, 1)
    more(AM, 1)
    AZ(0, 0)
    AZ(0, 1)
    more(AZ, 0)
    for i in range(3):
        remote(sgz.at[i], sgz.at[i], gsend.at[1], grecv.at[1 + i], h.core).wait_recv()
    for i, zp in enumerate(h.peers):
        sgz_copy(i, zp).wait_send()
    sg[...] = (sgx[...] + sgz[0]) + (sgz[1] + sgz[2])
    sgy_copy = remote(sg, sgy, gsend.at[4], grecv.at[4], h.ydev)
    sgy_copy.start()
    AZ(1, 0)
    AZ(1, 1)
    more(AZ, 1)
    sgy_copy.wait()
    sgx[...] = sg[...] + sgy[...]
    deliver(3, sgx, sums_o)
    for m in range(2):
        AY(m, 0)
        AY(m, 1)
        more(AY, m)
    deliver(4, inner.at[0:1152], qkv_o)

    for copy in tok_outs:
        copy.wait()
    for copy in n1_sends:
        copy.wait_send()

    def drain(k):
        oy(k).wait_send()
        ox(k).wait_send()
        iy(k).wait_send()
        for m in range(2):
            for i in range(2):
                z_one(m, k, i).wait_send()
            z_two(m, k).wait_send()

    for n in range(5):
        only(n, lambda: drain(n))

    def o_drain(k):
        ox_copy(k).wait_send()
        oy_copy(k).wait_send()
        for i, zp in enumerate(h.peers):
            oz_copy(k, i, zp).wait_send()

    both(o_drain, (0,), (1,))

    def a_drain(k):
        vy(k).wait_send()
        for m in range(2):
            ay(m, k).wait_send()
            ax(m, k).wait_send()
            for i in range(2):
                a_one(m, k, i).wait_send()
            a_two(m, k).wait_send()

    a_drain(0)
    a_drain(1)
    more(a_drain)
    for local, over in finals:
        local.wait()
        over.wait()


def run_backward(saved):
    (wa, wo, wi, wu, n1t, n2t, cot, qn, kn, vn, qt, kt, ot, lse, mid, slope, act, go, par, mb, x) = saved
    hbm = pl.BlockSpec(memory_space=pltpu.HBM)
    vmem = pl.BlockSpec(memory_space=pltpu.VMEM)
    sds = jax.ShapeDtypeStruct
    V = pltpu.VMEM
    dma = pltpu.SemaphoreType.DMA
    shapes = [
        sds((512, 1152), BF), sds((512, 1152), F32), sds((2, 144, 1152), F32),
        sds((2, 144, 1152), F32), sds((2, 1152, 256), F32), sds((2, 144, 640), F32),
        sds((2, 8, 1920), F32),
    ]
    scratch = [
        V((1152, 2304), BF), V((1152, 2304), BF), V((1024, 2304), BF), V((1024, 2304), BF),
        V((1024, 1152), BF), V((640, 1024), BF), V((1152, 1024), BF), V((2304, 256), F32),
        V((512, 1152), F32), V((512, 1152), BF), V((512, 1152), BF), V((512, 1152), F32),
        V((512, 1152), BF), V((4, 2, 144, 1152), BF), V((4, 144, 1152), BF), V((4, 144, 2304), BF), V((4, 144, 1152), BF),
        V((2, 3, 144, 1152), BF), V((4, 2, 144, 2304), BF), V((4, 2, 144, 256), BF), V((4, 2, 144, 768), BF),
        V((1088, 128), F32), V((1024, 128), F32),
        V((4, 2, 144, 640), BF), V((2, 4, 144, 640), BF), V((2, 3, 144, 640), BF), V((2, 144, 640), BF), V((2, 144, 640), BF),
        V((4, 2, 144, 640), BF), V((144, 640), BF), V((3, 2, 144, 640), BF), V((144, 640), BF),
        V((144, 640), BF),
        V((8, 1920), F32), V((8, 1920), F32), V((3, 8, 1920), F32), V((8, 1920), F32), V((8, 256), F32),
        dma((18,)), dma((2,)), dma((1,)),
        dma((2, 5)), dma((2, 5)), dma((5,)), dma((5,)), dma((9,)), dma((9,)), dma((2, 5, 3)), dma((2, 5, 3)),
        dma((2, 3)), dma((2, 3)), dma((2, 3, 3)), dma((2, 3, 3)), dma((9,)), dma((9,)),
        dma((2,)), dma((2,)), dma((2, 3)), dma((2, 3)), dma((2,)), dma((2,)),
        dma((5,)), dma((5,)), dma((10,)), dma((10,)), dma((6,)), dma((5,)), dma((5,)), dma((5,)),
    ]
    return pl.pallas_call(
        backward_kernel, out_shape=shapes, in_specs=[vmem] * 2 + [hbm] * 19,
        out_specs=[hbm] * len(shapes), scratch_shapes=scratch,
        compiler_params=pltpu.CompilerParams(
            collective_id=1, has_side_effects=True, vmem_limit_bytes=65300 << 10),
        cost_estimate=pl.CostEstimate(flops=40 * 10**9, bytes_accessed=80 * 10**6, transcendentals=2 * 10**7),
        name="backward",
    )(par, lse, wa, wo, wi, wu, n1t, n2t, cot, qn, kn, vn, qt, kt, ot, mid, slope, act, go, mb, x)


def finish_kernel(mixed_h, tokens_h, out_h, in_h, qkv_h, proj_h, sums_h,
                  mixed, tokens, gains, shifts, biases, w_qkv, w_o, w_in, b_in, w_out,
                  mixed_in, tokens_in, out_in, in_in, qkv_in, proj_in, sums_in, line, isem):
    c = lax.axis_index("ctx")
    s = lax.axis_index("shard")
    loads = [pltpu.make_async_copy(src, dst, isem.at[n]) for n, (src, dst) in enumerate((
        (tokens_h, tokens_in), (mixed_h, mixed_in), (qkv_h, qkv_in), (out_h, out_in), (in_h, in_in),
        (proj_h, proj_in), (sums_h, sums_in)))]
    for copy in loads:
        copy.start()

    def turned(v):
        v = v.T
        return jnp.concatenate([v[144 * q:144 * q + 136] for q in range(8)], axis=0)

    loads[0].wait()
    loads[1].wait()
    for i in range(4):
        at = slice(128 * i, 128 * i + 128)
        tokens[:, at] = turned(tokens_in[at, :])
        mixed[:, at] = turned(mixed_in[at, :].astype(F32)).astype(BF)

    def join(v):
        block = lax.broadcasted_iota(jnp.int32, v.shape, 1) // 136
        got = v
        for q in range(1, 8):
            got = jnp.where(block == q, pltpu.roll(v, 1152 - 8 * q, 1), got)
        return got[:, 0:1088]

    def heads(core, n):
        yield 2 * n, 0, 256, 0
        yield 2 * n + 1, 0, 256, 256
        if core == 0:
            yield 6 + n // 2, 128 * (n % 2), 64, 512

    for copy in loads[2:]:
        copy.wait()

    def for_core(core):
        at = slice(68 * core, 68 * core + 68)
        for n in range(3):
            for owner in range(2):
                for block, start, width, to in heads(owner, n):
                    to = 1088 * n + 576 * owner + to
                    w_qkv[:, to:to + width] = qkv_in[
                        owner, 144 * block + at.start:144 * block + at.stop, start:start + width]
        wide = jnp.concatenate(
            [proj_in[0, at, 0:512], proj_in[1, at, 0:512], proj_in[0, at, 512:640]], axis=1)
        w_o[...] = join(wide)
        w_in[:, 0:1152] = in_in[0, at, :]
        w_in[:, 1152:2176] = in_in[1, at, 0:1024]
        w_out[:, 0:1152] = out_in[0, at, :]
        w_out[:, 1152:2176] = out_in[1, at, 0:1024]

    pl.when(c == 0)(lambda: for_core(0))
    pl.when(c == 1)(lambda: for_core(1))

    rows = sums_in[0] + sums_in[1]
    mine = pltpu.roll(rows, 1920 - (s * BR + c * 68), 1)[:, 0:68]
    gains[0:1, :] = mine[1:2]
    gains[1:2, :] = mine[3:4]
    shifts[0:1, :] = mine[2:3]
    shifts[1:2, :] = mine[4:5]
    biases[2:3, :] = mine[6:7]
    biases[3:4, :] = mine[5:6]
    for n, row in ((0, 0), (2, 1)):
        start, more = 512 * n, 1536 + 128 * n
        line[:, 0:512] = sums_in[0, :, start:start + 512]
        line[:, 512:576] = sums_in[0, :, more:more + 64]
        line[:, 576:1088] = sums_in[1, :, start:start + 512]
        got = pltpu.roll(line[:, 0:1152], 1152 - (2 * s + c) * 68, 1)[:, 0:68]
        biases[row:row + 1, :] = got[0:1]
    line[:, 0:1152] = in_in[0, 136:144, :]
    line[:, 1152:2176] = in_in[1, 136:144, 0:1024]
    b_in[...] = pltpu.roll(line[...], 2176 - (2 * s + c) * 136, 1)[0:1, 0:136]


def finish(mixed, tokens_grad, out_g, in_g, qkv_g, proj_g, sums):
    sds = jax.ShapeDtypeStruct
    shapes = [
        sds((1088, 512), BF), sds((1088, 512), F32), sds((2, 68), F32), sds((2, 68), F32),
        sds((4, 68), F32), sds((68, 3264), F32), sds((68, 1088), F32), sds((68, 2176), F32),
        sds((1, 136), F32), sds((68, 2176), F32),
    ]
    vmem = pl.BlockSpec(memory_space=pltpu.VMEM)
    hbm = pl.BlockSpec(memory_space=pltpu.HBM)
    given = (mixed, tokens_grad, out_g, in_g, qkv_g, proj_g, sums)
    got = pl.pallas_call(
        finish_kernel, out_shape=shapes, in_specs=[hbm] * 7, out_specs=[vmem] * len(shapes),
        scratch_shapes=[pltpu.VMEM(v.shape, v.dtype) for v in given] + [
            pltpu.VMEM((8, 2176), F32), pltpu.SemaphoreType.DMA((7,))],
        compiler_params=pltpu.CompilerParams(vmem_limit_bytes=63 << 20), name="finish",
    )(*given)
    return (got[0].T[None], got[1].T[None]) + tuple(got[2:9]) + (got[9].T,)


def fused(tokens, segment_ids, norm_gains, norm_shifts, biases, w_qkv, w_o, w_in, b_in, w_out,
          cotangent):
    saved = run_forward(tokens, segment_ids, norm_gains, norm_shifts, biases, w_qkv, w_o, w_in,
                        b_in, w_out, cotangent)
    sums = run_backward(saved)
    return finish(*sums)


def per_device(
    tokens, segment_ids, norm_gains, norm_shifts, biases, w_qkv, w_o, w_in, b_in, w_out, cotangent
):
    rows_here = tokens.shape[1]
    score_scale = HEAD_DIM ** (-0.5)
    gains_full, shifts_full, bias_full, qkv_full, proj_full, up_full, down_full = (
        lax.all_gather(norm_gains, "shard", axis=1, tiled=True),
        lax.all_gather(norm_shifts, "shard", axis=1, tiled=True),
        lax.all_gather(biases, "shard", axis=1, tiled=True),
        lax.all_gather(w_qkv, "shard", axis=0, tiled=True),
        lax.all_gather(w_o, "shard", axis=0, tiled=True),
        lax.all_gather(w_in, "shard", axis=0, tiled=True),
        lax.all_gather(w_out, "shard", axis=1, tiled=True),
    )
    gains_full = gains_full.astype(jnp.float32)
    shifts_full = shifts_full.astype(jnp.float32)
    bias_full = bias_full.astype(jnp.float32)
    hidden = tokens[0].astype(jnp.float32)
    normed, norm_back_one = jax.vjp(layer_norm, hidden, gains_full[0], shifts_full[0])
    normed_low = normed.astype(jnp.bfloat16)
    projected = jnp.dot(normed_low, qkv_full, preferred_element_type=jnp.float32)
    queries = (projected[:, :D] + bias_full[0]).astype(jnp.bfloat16)
    key_rows = projected[:, D : 2 * D].astype(jnp.bfloat16)
    value_rows = (projected[:, 2 * D :] + bias_full[1]).astype(jnp.bfloat16)
    all_keys, all_values = (
        lax.all_gather(key_rows, "ctx", axis=0, tiled=True),
        lax.all_gather(value_rows, "ctx", axis=0, tiled=True),
    )
    seq_length = all_keys.shape[0]
    offset = lax.axis_index("ctx") * rows_here
    key_segments = segment_ids[0]
    query_segments = lax.dynamic_slice_in_dim(key_segments, offset, rows_here)
    query_position = offset + lax.iota(jnp.int32, rows_here)
    key_position = lax.iota(jnp.int32, seq_length)
    allowed = (key_position[None, :] <= query_position[:, None]) & (
        key_segments[None, :] == query_segments[:, None]
    )
    query_heads = split_heads(queries)
    key_heads = split_heads(all_keys)
    value_heads = split_heads(all_values)

    def head_scores(query_head, key_head):
        scores = (
            jnp.einsum("qd,kd->qk", query_head, key_head, preferred_element_type=jnp.float32)
            * score_scale
        )
        return jnp.where(allowed, scores, -1e30)

    def head_forward(operands):
        query_head, key_head, value_head = operands
        masked = head_scores(query_head, key_head)
        highest = jnp.max(masked, axis=1, keepdims=True)
        weights = jnp.exp(masked - highest)
        summed = jnp.sum(weights, axis=1, keepdims=True)
        probabilities = (weights / summed).astype(jnp.bfloat16)
        result = jnp.dot(probabilities, value_head, preferred_element_type=jnp.float32)
        return (result, (highest + jnp.log(summed))[:, 0])

    head_out, log_total = lax.map(head_forward, (query_heads, key_heads, value_heads))
    attended = merge_heads(head_out).astype(jnp.bfloat16)
    middle = (
        hidden + jnp.dot(attended, proj_full, preferred_element_type=jnp.float32) + bias_full[2]
    )
    normed_two, norm_back_two = jax.vjp(layer_norm, middle, gains_full[1], shifts_full[1])
    normed_two_low = normed_two.astype(jnp.bfloat16)
    mlp_inputs = lax.all_gather(normed_two_low, "tp", axis=0, tiled=True)
    inner_values = jnp.dot(mlp_inputs, up_full, preferred_element_type=jnp.float32) + b_in.astype(
        jnp.float32
    )
    active, gelu_back = jax.vjp(gelu_tanh, inner_values)
    active_low = active.astype(jnp.bfloat16)
    mixed_rows = (
        middle
        + lax.psum_scatter(
            jnp.dot(active_low, down_full, preferred_element_type=jnp.float32).astype(jnp.bfloat16),
            "tp",
            scatter_dimension=0,
            tiled=True,
        ).astype(jnp.float32)
        + bias_full[3]
    )
    mixed_out = mixed_rows.astype(jnp.bfloat16)[None]
    grad_low = cotangent[0]
    grad_out = grad_low.astype(jnp.float32)
    grad_rows = lax.all_gather(grad_low, "tp", axis=0, tiled=True)
    down_grad = contract_rows(active_low, grad_rows)
    out_bias_grad = jnp.sum(grad_out, axis=0)
    active_grad = contract_cols(grad_rows, down_full)
    inner_grad = gelu_back(active_grad)[0].astype(jnp.bfloat16)
    up_grad = contract_rows(mlp_inputs, inner_grad)
    in_bias_grad = jnp.sum(inner_grad.astype(jnp.float32), axis=0)
    normed_two_grad = lax.psum_scatter(
        contract_cols(inner_grad, up_full), "tp", scatter_dimension=0, tiled=True
    )
    middle_part, gain_two_grad, shift_two_grad = norm_back_two(normed_two_grad)
    middle_grad = grad_out + middle_part
    branch_grad = middle_grad.astype(jnp.bfloat16)
    proj_grad = contract_rows(attended, branch_grad)
    attn_bias_grad = jnp.sum(branch_grad.astype(jnp.float32), axis=0)
    attended_grad = split_heads(contract_cols(branch_grad, proj_full).astype(jnp.bfloat16))

    def head_backward(operands):
        query_head, key_head, value_head, grad_head, log_head = operands
        masked = head_scores(query_head, key_head)
        probabilities = jnp.exp(masked - log_head[:, None])
        probs_grad = jnp.einsum(
            "qd,kd->qk", grad_head, value_head, preferred_element_type=jnp.float32
        )
        row_terms = jnp.sum(probabilities * probs_grad, axis=1, keepdims=True)
        scores_grad = (probabilities * (probs_grad - row_terms)).astype(jnp.bfloat16)
        query_grad = (
            jnp.dot(scores_grad, key_head, preferred_element_type=jnp.float32) * score_scale
        )
        key_grad = (
            jnp.einsum("qk,qd->kd", scores_grad, query_head, preferred_element_type=jnp.float32)
            * score_scale
        )
        value_grad = jnp.einsum(
            "qk,qd->kd",
            probabilities.astype(jnp.bfloat16),
            grad_head,
            preferred_element_type=jnp.float32,
        )
        return (query_grad, key_grad, value_grad)

    query_grads, key_grads, value_grads = lax.map(
        head_backward, (query_heads, key_heads, value_heads, attended_grad, log_total)
    )
    key_summed, value_summed = (
        lax.psum_scatter(
            merge_heads(key_grads).astype(jnp.bfloat16), "ctx", scatter_dimension=0, tiled=True
        ).astype(jnp.float32),
        lax.psum_scatter(
            merge_heads(value_grads).astype(jnp.bfloat16), "ctx", scatter_dimension=0, tiled=True
        ).astype(jnp.float32),
    )
    query_low = merge_heads(query_grads).astype(jnp.bfloat16)
    value_low = value_summed.astype(jnp.bfloat16)
    qkv_grad = jnp.concatenate([query_low, key_summed.astype(jnp.bfloat16), value_low], axis=1)
    qkv_weight_grad = contract_rows(normed_low, qkv_grad)
    query_bias_grad = jnp.sum(query_low.astype(jnp.float32), axis=0)
    value_bias_grad = jnp.sum(value_low.astype(jnp.float32), axis=0)
    normed_grad = contract_cols(qkv_grad, qkv_full)
    hidden_part, gain_one_grad, shift_one_grad = norm_back_one(normed_grad)
    tokens_grad = (middle_grad + hidden_part)[None]
    gains_grad = jnp.stack([gain_one_grad, gain_two_grad])
    shifts_grad = jnp.stack([shift_one_grad, shift_two_grad])
    biases_grad = jnp.stack([query_bias_grad, value_bias_grad, attn_bias_grad, out_bias_grad])
    gains_grad, shifts_grad, biases_grad, qkv_weight_grad, proj_grad = lax.psum(
        (gains_grad, shifts_grad, biases_grad, qkv_weight_grad, proj_grad), "tp"
    )
    (
        gains_grad,
        shifts_grad,
        biases_grad,
        qkv_weight_grad,
        proj_grad,
        up_grad,
        in_bias_grad,
        down_grad,
    ) = (
        lax.psum_scatter(gains_grad, ("shard", "ctx"), scatter_dimension=1, tiled=True),
        lax.psum_scatter(shifts_grad, ("shard", "ctx"), scatter_dimension=1, tiled=True),
        lax.psum_scatter(biases_grad, ("shard", "ctx"), scatter_dimension=1, tiled=True),
        lax.psum_scatter(qkv_weight_grad, ("shard", "ctx"), scatter_dimension=0, tiled=True),
        lax.psum_scatter(proj_grad, ("shard", "ctx"), scatter_dimension=0, tiled=True),
        lax.psum_scatter(up_grad, ("shard", "ctx"), scatter_dimension=0, tiled=True),
        lax.psum_scatter(in_bias_grad, ("shard", "ctx"), scatter_dimension=0, tiled=True),
        lax.psum_scatter(down_grad, ("shard", "ctx"), scatter_dimension=1, tiled=True),
    )
    return (
        mixed_out,
        tokens_grad,
        gains_grad,
        shifts_grad,
        biases_grad,
        qkv_weight_grad,
        proj_grad,
        up_grad,
        in_bias_grad[None],
        down_grad,
    )


def solution(mesh):
    in_specs = (
        P(("shard", "tp"), "ctx", None),
        P(("shard", "tp"), None),
        P(None, "shard"),
        P(None, "shard"),
        P(None, "shard"),
        P("shard", None),
        P("shard", None),
        P("shard", "tp"),
        P("tp"),
        P("tp", "shard"),
        P(("shard", "tp"), "ctx", None),
    )
    out_specs = (
        P(("shard", "tp"), "ctx", None),
        P(("shard", "tp"), "ctx", None),
        P(None, ("shard", "ctx")),
        P(None, ("shard", "ctx")),
        P(None, ("shard", "ctx")),
        P(("shard", "ctx"), None),
        P(("shard", "ctx"), None),
        P(("shard", "ctx"), "tp"),
        P("tp", ("shard", "ctx")),
        P("tp", ("shard", "ctx")),
    )
    fits = dict(mesh.shape) == {"shard": 8, "ctx": 2, "tp": 2}
    return jax.shard_map(
        fused if fits else per_device, mesh=mesh, in_specs=in_specs, out_specs=out_specs, check_vma=False
    )
```
